32 devices in a mesh: dp: 16 (over z, y, x), mp: 2 (over core).
Axes of the slice: x: 2, y: 2, z: 4, core: 2. Of those that a mesh axis runs over, the one named last changes fastest.
Arguments:
- tokens: bfloat16 [4096, 768], P(('dp', 'mp')), may hold values from -6 to 6
- cotangent: bfloat16 [4096, 768], P(('dp', 'mp')), may hold values from -6 to 6
- char_ids: int32 [4096, 20], P(('dp', 'mp')), may hold values from 0 to 511
- char_lens: int32 [4096], P(('dp', 'mp')), may hold values from 1 to 20, as said below
- w_qkv: bfloat16 [1, 768, 3, 768], P(None, None, None, 'mp'), may hold values from -0.21875 to 0.21875
- b_qkv: bfloat16 [1, 2, 768], P(None, None, 'mp'), may hold values from -3 to 3
- w_out: bfloat16 [1, 768, 768], P(None, 'mp'), may hold values from -0.875 to 0.875
- w_up: bfloat16 [1, 768, 3072], P(None, None, 'mp'), may hold values from -0.21875 to 0.21875
- up_bias: bfloat16 [1, 3072], P(None, 'mp'), may hold values from -3 to 3
- w_down: bfloat16 [1, 3072, 768], P(None, 'mp'), may hold values from -0.109375 to 0.109375
- res_bias: bfloat16 [1, 3, 768], replicated, may hold values from -3 to 3
- norm_gain: bfloat16 [1, 3, 768], replicated, may hold values from 0.5 to 1.5
- norm_bias: bfloat16 [1, 3, 768], replicated, may hold values from -1.75 to 1.75
- char_table: bfloat16 [512, 256], replicated, may hold values from -6 to 6
- gru_in: bfloat16 [1, 2, 256, 1152], replicated, may hold values from -0.375 to 0.375
- gru_hid: bfloat16 [1, 2, 384, 1152], replicated, may hold values from -0.3125 to 0.3125
- gru_bias: bfloat16 [1, 2, 2, 1152], replicated, may hold values from -3 to 3
- conv_w: bfloat16 [1, 3, 1536, 768], replicated, may hold values from -0.09375 to 0.09375
Outputs:
- out: bfloat16 [4096, 768], P(('dp', 'mp'))
- tokens_grad: float32 [4096, 768], P(('dp', 'mp'))
- w_qkv_grad: float32 [1, 768, 3, 768], P(None, 'dp', None, 'mp')
- b_qkv_grad: float32 [1, 2, 768], P(None, None, 'mp')
- w_out_grad: float32 [1, 768, 768], P(None, 'mp', 'dp')
- w_up_grad: float32 [1, 768, 3072], P(None, 'dp', 'mp')
- up_bias_grad: float32 [1, 3072], P(None, 'mp')
- w_down_grad: float32 [1, 3072, 768], P(None, 'mp', 'dp')
- res_bias_grad: float32 [1, 3, 768], replicated
- norm_gain_grad: float32 [1, 3, 768], replicated
- norm_bias_grad: float32 [1, 3, 768], replicated
- char_table_grad: float32 [512, 256], replicated
- gru_in_grad: float32 [1, 2, 256, 1152], replicated
- gru_hid_grad: float32 [1, 2, 384, 1152], replicated
- gru_bias_grad: float32 [1, 2, 2, 1152], replicated
- conv_w_grad: float32 [1, 3, 1536, 768], P(None, None, 'dp')
The draws below stay inside these ranges and needn't reach their ends.
Inputs may be any that keep to these rules, and one draw needn't show every extreme that they name: `char_lens`: every block of 128 consecutive tokens holds a token of 20 characters.
All inputs are finite; a program needn't handle non-finite values.
Results may differ from the reference program's by a relative error of at most 0.018.
Values may be sent and summed in bfloat16 or wider, within the bound.
No kernel may reach another device: no remote copies, remote signals or barrier semaphores. Data moves between devices by JAX's collectives and lax.ppermute only.
A program may use at most 256 MiB of HBM per device.

```python
import math
import jax
import jax.numpy as jnp
import numpy as np
from jax import lax

D = 768
HEADS = 12
FF = 3072
GH = 384
CE = 256
CV = 512
CHARS = 20
LAYERS = 1
TOK_DEV = 128
HD = 64
SEQ = 256
TOKENS = 4096
N_DP = 16


def draw_char_lens(key, part):
    key = jax.random.fold_in(key, 11)
    first_key, second_key, third_key, fourth_key = jax.random.split(key, 4)
    long_lengths = jnp.maximum(CHARS - jax.random.randint(first_key, (TOKENS,), 0, 4), 1)
    any_lengths = jax.random.randint(second_key, (TOKENS,), 1, CHARS + 1)
    picker = jax.random.randint(third_key, (TOKENS,), 0, 5)
    lengths = jnp.where(picker == 0, any_lengths, long_lengths)
    chosen = jax.random.randint(fourth_key, (), 0, TOK_DEV)
    positions = jnp.arange(TOKENS)
    return jnp.where(positions % TOK_DEV == chosen, CHARS, lengths).astype(jnp.int32)


def draw_gru_bias(key, part):
    key = jax.random.fold_in(key, 23)
    base_key, level_key, pick_key = jax.random.split(key, 3)
    shape = (LAYERS, 2, 2, 3 * GH)
    base = jnp.clip(0.5 * jax.random.normal(base_key, shape, jnp.float32), -1.5, 1.5)
    level = jax.random.uniform(level_key, (LAYERS, 2, 1, 3 * GH), jnp.float32, 1.25, 1.55)
    picks = jax.random.randint(pick_key, (LAYERS, 2, 1, 3 * GH), 0, 4)
    slow_part = jnp.where(picks == 0, 0.0, level)
    units = jnp.arange(3 * GH)
    gate_cols = (units >= GH) & (units < 2 * GH)
    values = jnp.where(gate_cols, slow_part + 0.15 * base, base)
    return values.astype(jnp.bfloat16)


def plant(entries, own_key, smallest, largest):
    index_at = [jax.random.randint(jax.random.fold_in(own_key, axis), (), 0, length) for axis, length in enumerate(entries.shape)]
    main_axis = entries.shape.index(max(entries.shape))
    neighbour = index_at[:main_axis] + [(index_at[main_axis] + 1) % entries.shape[main_axis]] + index_at[main_axis + 1:]
    return entries.at[tuple(index_at)].set(smallest).at[tuple(neighbour)].set(largest)


def block_levels(key, shape, cuts, least, largest):
    level = 1.0
    for dim, parts in cuts:
        draws = jax.random.uniform(jax.random.fold_in(jax.random.fold_in(key, 6), dim), (parts,), jnp.float32, least / len(cuts), largest / len(cuts))
        level = level * jnp.repeat(jnp.exp(draws), shape[dim] // parts).reshape((-1,) + (1,) * (len(shape) - 1 - dim))
    return level


def cumulative_ranks(number_of, lean):
    loads = [(1 << 20) // math.isqrt(rank ** lean) + 1 for rank in range(1, number_of + 1)]
    scale = 1 + sum(loads) // (1 << 30)
    return np.cumsum(np.array([max(1, weight // scale) for weight in loads]))


def ranked_ids(stream_key, shape, amount, slope):
    table = cumulative_ranks(amount, slope)
    pick = jax.random.randint(jax.random.fold_in(stream_key, 1), shape, 0, int(table[amount - 1]))
    rank = jnp.searchsorted(jnp.asarray(table, jnp.int32), pick, side="right")
    return jax.random.permutation(jax.random.fold_in(stream_key, 2), amount)[rank].astype(jnp.int32)


def normal_values(own_key, extent, scale, reach, shards=(), kind=jnp.bfloat16):
    level = block_levels(own_key, extent, shards, -0.22, 0.18) if shards else 1.0
    values = jax.random.normal(own_key, extent, jnp.float32) * scale * level
    return jnp.minimum(jnp.maximum(values, -reach), reach).astype(kind)


def setup_inputs(seed: int = 0) -> dict:
    keys = jax.random.split(jax.random.key(seed), 19)
    return {
        "tokens": normal_values(keys[0], (TOKENS, D), 1.0, 6.0, ((0, 32),)),
        "cotangent": normal_values(keys[1], (TOKENS, D), 1.0, 6.0, ((0, 32),)),
        "char_ids": plant(ranked_ids(keys[2], (TOKENS, CHARS), CV, 2), jax.random.fold_in(keys[2], 3), 0, CV - 1).astype(jnp.int32),
        "char_lens": draw_char_lens(jax.random.fold_in(keys[18], 71), 0),
        "w_qkv": normal_values(keys[4], (LAYERS, D, 3, D), D ** -0.5, 0.21875, ((3, 2),)),
        "b_qkv": normal_values(keys[5], (LAYERS, 2, D), 0.5, 3.0, ((2, 2),)),
        "w_out": normal_values(keys[6], (LAYERS, D, D), (D // 16) ** -0.5, 0.875, ((1, 2),)),
        "w_up": normal_values(keys[7], (LAYERS, D, FF), D ** -0.5, 0.21875, ((2, 2),)),
        "up_bias": normal_values(keys[8], (LAYERS, FF), 0.5, 3.0, ((1, 2),)),
        "w_down": normal_values(keys[9], (LAYERS, FF, D), FF ** -0.5, 0.109375, ((1, 2),)),
        "res_bias": normal_values(keys[10], (LAYERS, 3, D), 0.5, 3.0),
        "norm_gain": jnp.clip(1.0 + 0.1 * jax.random.normal(keys[11], (LAYERS, 3, D), jnp.float32), 0.5, 1.5).astype(jnp.bfloat16),
        "norm_bias": normal_values(keys[12], (LAYERS, 3, D), 0.3, 1.75),
        "char_table": normal_values(keys[13], (CV, CE), 1.0, 6.0),
        "gru_in": normal_values(keys[14], (LAYERS, 2, CE, 3 * GH), CE ** -0.5, 0.375),
        "gru_hid": normal_values(keys[15], (LAYERS, 2, GH, 3 * GH), GH ** -0.5, 0.3125),
        "gru_bias": draw_gru_bias(jax.random.fold_in(keys[18], 71), 0),
        "conv_w": normal_values(keys[17], (LAYERS, 3, D + 2 * GH, D), (3 * (D + 2 * GH)) ** -0.5, 0.09375),
    }


@jax.custom_vjp
def low(v):
    return lax.optimization_barrier(v.astype(jnp.bfloat16)).astype(jnp.float32)

@jax.custom_vjp
def low_back(v):
    return v

def low_keep(v):
    return (low(v), None)

def low_pass(kept, grad):
    return (grad,)

def back_keep(v):
    return (v, None)

def back_low(kept, grad):
    return (low(grad),)
low.defvjp(low_keep, low_pass)
low_back.defvjp(back_keep, back_low)
PRECISE = lax.Precision.HIGHEST
EPSILON = 1e-05

def product(left, right):
    return jnp.matmul(left, right, precision=PRECISE)

def norm_apply(totals, scales, offsets):
    centre = lax.optimization_barrier(jnp.mean(totals, -1, keepdims=True))
    centred = totals - centre
    spread = lax.optimization_barrier(jnp.mean(centred * centred, -1, keepdims=True))
    return centred * lax.rsqrt(spread + EPSILON) * scales + offsets

def gelu_apply(inputs):
    return jax.nn.gelu(inputs, approximate=True)

def gate_apply(drive_step, recur_step, carried, mask_step):
    width = carried.shape[-1]
    reset = jax.nn.sigmoid(drive_step[:, :width] + recur_step[:, :width])
    update = jax.nn.sigmoid(drive_step[:, width:2 * width] + recur_step[:, width:2 * width])
    fresh = jnp.tanh(drive_step[:, 2 * width:] + reset * recur_step[:, 2 * width:])
    moved = (1.0 - update) * fresh + update * carried
    return mask_step * moved + (1.0 - mask_step) * carried

def char_channel(embedded, in_weight, hid_weight, gru_shift, char_mask):
    finals = []
    for direction in range(2):
        drive_all = low_back(jnp.einsum('cse,eg->csg', embedded, in_weight[direction], precision=PRECISE) + gru_shift[direction, 0])
        hid_matrix = hid_weight[direction]
        hid_offset = gru_shift[direction, 1]

        def advance(carried, inputs, hid_matrix=hid_matrix, hid_offset=hid_offset):
            drive_step, mask_step = inputs
            recur_step = low_back(product(low(carried), hid_matrix) + hid_offset)
            return (gate_apply(drive_step, recur_step, carried, mask_step), None)
        initial = jnp.zeros((embedded.shape[1], GH), jnp.float32)
        last_state, _ = lax.scan(jax.checkpoint(advance), initial, (drive_all, char_mask), reverse=direction == 1)
        finals.append(last_state)
    return jnp.concatenate(finals, 1)

def one_layer(layer_in, weights, embedded, char_mask):
    qkv_weight, qkv_shift, out_weight, up_weight, up_shift, down_weight, res_shift, gains, offsets, in_weight, hid_weight, gru_shift, conv_kernel = weights
    seq_len = layer_in.shape[0]
    head_shape = (seq_len, HEADS, HD)
    projected = jnp.einsum('sd,dkn->skn', low(layer_in), qkv_weight, precision=PRECISE)
    queries = low(low_back(projected[:, 0] + qkv_shift[0])).reshape(head_shape)
    keys_all = low(low_back(projected[:, 1])).reshape(head_shape)
    values_all = low(low_back(projected[:, 2] + qkv_shift[1])).reshape(head_shape)
    scores = low_back(jnp.einsum('qhd,khd->hqk', queries, keys_all, precision=PRECISE) * HD ** (-0.5))
    probs = low(jax.nn.softmax(scores, axis=-1))
    mixed = jnp.einsum('hqk,khd->qhd', probs, values_all, precision=PRECISE).reshape(seq_len, D)
    mixed = low(low_back(mixed))
    attn_out = low_back(product(mixed, out_weight))
    first_norm = norm_apply(layer_in + attn_out + res_shift[0], gains[0], offsets[0])
    pre_act = low_back(product(low(first_norm), up_weight) + up_shift)
    ffn_out = low_back(product(low(gelu_apply(pre_act)), down_weight))
    second_norm = norm_apply(first_norm + ffn_out + res_shift[1], gains[1], offsets[1])
    char_out = char_channel(embedded, in_weight, hid_weight, gru_shift, char_mask)
    joined = low(jnp.concatenate([second_norm, char_out], 1))
    padded = jnp.pad(joined, ((1, 1), (0, 0)))
    conv_raw = product(padded[0:seq_len], conv_kernel[0]) + product(padded[1:seq_len + 1], conv_kernel[1])
    conv_raw = conv_raw + product(padded[2:seq_len + 2], conv_kernel[2]) + res_shift[2]
    conv_act = gelu_apply(low_back(conv_raw))
    return norm_apply(second_norm + conv_act, gains[2], offsets[2])

def forward(seq_rows, layer_weights, table, seq_ids, seq_lens):
    embedded = jnp.take(table, seq_ids.T, axis=0)
    char_mask = (jnp.arange(CHARS)[:, None] < seq_lens[None, :]).astype(jnp.float32)[:, :, None]
    current = seq_rows
    for layer in range(LAYERS):
        current = one_layer(current, tuple((weight[layer] for weight in layer_weights)), embedded, char_mask)
    return current

def reference(tokens, cotangent, char_ids, char_lens, w_qkv, b_qkv, w_out, w_up, up_bias, w_down, res_bias, norm_gain, norm_bias, char_table, gru_in, gru_hid, gru_bias, conv_w):
    layer_weights = tuple((weight.astype(jnp.float32) for weight in (w_qkv, b_qkv, w_out, w_up, up_bias, w_down, res_bias, norm_gain, norm_bias, gru_in, gru_hid, gru_bias, conv_w)))
    table = char_table.astype(jnp.float32)
    all_rows = tokens.astype(jnp.float32).reshape(N_DP, SEQ, D)
    all_cot = cotangent.astype(jnp.float32).reshape(N_DP, SEQ, D)
    all_ids = char_ids.reshape(N_DP, SEQ, CHARS)
    all_lens = char_lens.reshape(N_DP, SEQ)

    def one_sequence(totals, inputs):
        seq_rows, seq_cot, seq_ids, seq_lens = inputs

        def wrapped(rows_in, weights_in, table_in):
            return forward(rows_in, weights_in, table_in, seq_ids, seq_lens)
        result, pullback = jax.vjp(wrapped, seq_rows, layer_weights, table)
        row_grad, weight_grads, table_grad = pullback(seq_cot)
        totals = jax.tree.map(jnp.add, totals, (weight_grads, table_grad))
        return (totals, (result, row_grad))
    zeros_all = jax.tree.map(jnp.zeros_like, (layer_weights, table))
    (weight_grads, table_grad), (results, row_grads) = lax.scan(one_sequence, zeros_all, (all_rows, all_cot, all_ids, all_lens))
    return (results.reshape(TOKENS, D).astype(jnp.bfloat16), row_grads.reshape(TOKENS, D), weight_grads[0], weight_grads[1], weight_grads[2], weight_grads[3], weight_grads[4], weight_grads[5], weight_grads[6], weight_grads[7], weight_grads[8], table_grad, weight_grads[9], weight_grads[10], weight_grads[11], weight_grads[12])
```

```python
import jax
import jax.numpy as jnp
from jax import lax
from jax.experimental import pallas as pl
from jax.experimental.pallas import tpu as pltpu
from jax.sharding import PartitionSpec as P

HD = 64
EPSILON = 1e-05
bf16 = jnp.bfloat16
f32 = jnp.float32


def dot(left, right):
    return jnp.dot(left, right, preferred_element_type=f32)


def dot_t(left, right):
    return lax.dot_general(left, right, (((0,), (0,)), ((), ())), preferred_element_type=f32)


def dot_r(left, right):
    return lax.dot_general(left, right, (((1,), (1,)), ((), ())), preferred_element_type=f32)


def sigmoid(x):
    return 0.5 * jnp.tanh(0.5 * x) + 0.5


def gru_fwd_kernel(ef, eb, lens, win, whid, bias, c_ref, cof, chf, hpf, cob, chb, hpb, h_ref):
    s = pl.program_id(0)
    n = pl.num_programs(0)
    gh = h_ref.shape[2]

    @pl.when(s == 0)
    def _():
        h_ref[...] = jnp.zeros_like(h_ref)

    for d, (e, co, ch, hp) in enumerate(((ef, cof, chf, hpf), (eb, cob, chb, hpb))):
        slot = s if d == 0 else n - 1 - s
        mask = (slot < lens[...]).astype(f32)
        h = h_ref[d]
        low = h.astype(bf16)
        g = dot(e[0], win[d]) + bias[2 * d : 2 * d + 1]
        y = dot(low, whid[d]) + bias[2 * d + 1 : 2 * d + 2]
        r = sigmoid(g[:, :gh] + y[:, :gh])
        z = sigmoid(g[:, gh : 2 * gh] + y[:, gh : 2 * gh])
        yn = y[:, 2 * gh :]
        fresh = jnp.tanh(g[:, 2 * gh :] + r * yn)
        keep = mask * (1.0 - z)
        moved = keep * (h - fresh)
        h_ref[d] = h - moved
        an = keep * (1.0 - fresh * fresh)
        ay = an * r
        ar = ay * yn * (1.0 - r)
        co[0, :, 0:gh] = ay.astype(bf16)
        co[0, :, gh : 2 * gh] = ar.astype(bf16)
        co[0, :, 2 * gh : 3 * gh] = (moved * z).astype(bf16)
        co[0, :, 3 * gh :] = an.astype(bf16)
        ch[0] = 1.0 - keep
        hp[0] = low

    @pl.when(s == n - 1)
    def _():
        c_ref[:, :gh] = h_ref[0].astype(bf16)
        c_ref[:, gh:] = h_ref[1].astype(bf16)


def gru_fwd(emb, lens, win, whid, bias):
    slots, rows, width = emb.shape
    gh = whid.shape[1]
    fw = lambda s: (s, 0, 0)
    bw = lambda s: (slots - 1 - s, 0, 0)
    blk = lambda w, im: pl.BlockSpec((1, rows, w), im)
    full = lambda a: pl.BlockSpec(a.shape, lambda s: (0,) * a.ndim)
    sd = jax.ShapeDtypeStruct
    return pl.pallas_call(
        gru_fwd_kernel,
        grid=(slots,),
        in_specs=[blk(width, fw), blk(width, bw), full(lens), full(win), full(whid), full(bias)],
        out_specs=[pl.BlockSpec((rows, 2 * gh), lambda s: (0, 0))]
        + [blk(4 * gh, fw), blk(gh, fw), blk(gh, fw), blk(4 * gh, bw), blk(gh, bw), blk(gh, bw)],
        out_shape=[sd((rows, 2 * gh), bf16)]
        + [sd((slots, rows, 4 * gh), bf16), sd((slots, rows, gh), f32), sd((slots, rows, gh), bf16)] * 2,
        scratch_shapes=[pltpu.VMEM((2, rows, gh), f32)],
        compiler_params=pltpu.CompilerParams(vmem_limit_bytes=32 << 20),
        cost_estimate=pl.CostEstimate(flops=1 << 20, bytes_accessed=1 << 10, transcendentals=0),
        name="gru_fwd",
    )(emb, emb, lens, win, whid, bias)


def gru_bwd_kernel(dc, wht, cof, chf, cob, chb, gf, gb, bs_ref, dh_ref, acc):
    i = pl.program_id(0)
    n = pl.num_programs(0)
    gh = dh_ref.shape[2]

    @pl.when(i == 0)
    def _():
        dh_ref[0] = dc[:, :gh]
        dh_ref[1] = dc[:, gh:]
        acc[...] = jnp.zeros_like(acc)

    for d, (co, ch, g) in enumerate(((cof, chf, gf), (cob, chb, gb))):
        dh = dh_ref[d]
        parts = [dh * co[0, :, k * gh : (k + 1) * gh].astype(f32) for k in range(4)]
        low = [p.astype(bf16) for p in parts]
        for k in range(4):
            g[0, :, k * gh : (k + 1) * gh] = low[k]
            acc[d, :, k * gh : (k + 1) * gh] += parts[k].reshape(-1, 8, gh).sum(0)
        dy = jnp.concatenate(low[:3], 1)
        dh_ref[d] = dh * ch[0] + dot(dy, wht[d])

    @pl.when(i == n - 1)
    def _():
        bs_ref[...] = acc[...].sum(1)


def gru_bwd(dc, wht, cof, chf, cob, chb):
    slots, rows, gh = chf.shape
    fw = lambda s: (slots - 1 - s, 0, 0)
    bw = lambda s: (s, 0, 0)
    blk = lambda w, im: pl.BlockSpec((1, rows, w), im)
    full = lambda a: pl.BlockSpec(a.shape, lambda s: (0,) * a.ndim)
    sd = jax.ShapeDtypeStruct
    return pl.pallas_call(
        gru_bwd_kernel,
        grid=(slots,),
        in_specs=[full(dc), full(wht), blk(4 * gh, fw), blk(gh, fw), blk(4 * gh, bw), blk(gh, bw)],
        out_specs=[blk(4 * gh, fw), blk(4 * gh, bw), pl.BlockSpec((2, 4 * gh), lambda s: (0, 0))],
        out_shape=[sd((slots, rows, 4 * gh), bf16)] * 2 + [sd((2, 4 * gh), f32)],
        scratch_shapes=[pltpu.VMEM((2, rows, gh), f32), pltpu.VMEM((2, 8, 4 * gh), f32)],
        compiler_params=pltpu.CompilerParams(vmem_limit_bytes=32 << 20),
        cost_estimate=pl.CostEstimate(flops=1 << 20, bytes_accessed=1 << 10, transcendentals=0),
        name="gru_bwd",
    )(dc, wht, cof, chf, cob, chb)


GELU_A = 0.7978845608028654
GELU_B = 0.044715


def norm_stats(total):
    centre = jnp.mean(total, -1, keepdims=True)
    centred = total - centre
    scale = lax.rsqrt(jnp.mean(centred * centred, -1, keepdims=True) + EPSILON)
    return centred * scale, scale


def norm_back(grad, hat, scale, gain):
    scaled = grad * gain
    inner = jnp.mean(scaled, -1, keepdims=True)
    along = jnp.mean(scaled * hat, -1, keepdims=True)
    return (scaled - inner - hat * along) * scale


def gelu_pair(u):
    square = u * u
    t = jnp.tanh(GELU_A * (u + GELU_B * u * square))
    half = 0.5 * (1.0 + t)
    slope = half + 0.5 * u * (1.0 - t * t) * (GELU_A + 3.0 * GELU_A * GELU_B * square)
    return u * half, slope


def turned(values):
    rows = values.shape[0] // 2
    return jnp.concatenate([values[rows:], values[:rows]], 0)


def own_sum(values):
    return jnp.sum(values[: values.shape[0] // 2], 0, keepdims=True)


def pair_of(left, right):
    return jnp.concatenate([left, right], 0)


class Halves:
    def __init__(self, length, bit):
        self.count = lax.axis_size("dp")
        self.length, self.bit = length, bit
        self.chunk = length // self.count
        self.direct = self.chunk % 16 == 0

    def operands(self):
        if self.direct:
            return []
        mine = (lax.axis_index("dp") >> self.bit) & 1
        where = jnp.arange(self.length, dtype=jnp.int32)
        kept = where.reshape(self.count >> (self.bit + 1), 2, -1)
        pick = lambda side: jax.nn.one_hot(
            lax.dynamic_index_in_dim(kept, side, 1, keepdims=False).reshape(-1), self.length, dtype=bf16
        )
        return [pick(1 - mine), pick(mine)]

    def scratch(self, rows):
        return [pltpu.VMEM((self.length, rows), bf16)]

    def sides(self, values, turned_ref, place, picks):
        if not self.direct:
            return [dot_r(pick[...], values).astype(bf16) for pick in picks]
        turned_ref[...] = values.T
        mine = (place[0] >> self.bit) & 1
        out = []
        for side in (1 - mine, mine):
            parts = []
            for k in range(self.count):
                if not (k >> self.bit) & 1:
                    start = pl.multiple_of((k + (side << self.bit)) * self.chunk, 16)
                    parts.append(turned_ref[pl.ds(start, self.chunk), :])
            out.append(jnp.concatenate(parts, 0))
        return out


VMEM = pl.BlockSpec(memory_space=pltpu.VMEM)
SMEM = pl.BlockSpec(memory_space=pltpu.SMEM)


def whole_call(kernel, args, outs, scratch, limit, flops, name):
    return pl.pallas_call(
        kernel,
        in_specs=[SMEM] + [VMEM] * (len(args) - 1),
        out_specs=[VMEM] * len(outs),
        out_shape=[jax.ShapeDtypeStruct(*o) for o in outs],
        scratch_shapes=scratch,
        compiler_params=pltpu.CompilerParams(vmem_limit_bytes=limit << 20),
        cost_estimate=pl.CostEstimate(flops=1 << 20, bytes_accessed=1 << 10, transcendentals=0),
        name=name,
    )(*args)


def attend_fwd(place, mine, other, wqkv, bqkv, wout, vec, q_ref, k_ref, v_ref, p_ref, m_ref, base_ref, send_ref):
    x = pair_of(mine[...], other[...])
    bias = bqkv[...].astype(f32)
    q = (dot(x, wqkv[0]) + bias[0:1]).astype(bf16)
    k = dot(x, wqkv[1]).astype(bf16)
    v = (dot(x, wqkv[2]) + bias[1:2]).astype(bf16)
    q_ref[...], k_ref[...], v_ref[...] = q, k, v
    mixed = []
    for h in range(p_ref.shape[0]):
        at = slice(h * HD, (h + 1) * HD)
        s = dot_r(q[:, at], k[:, at]) * HD**-0.5
        e = jnp.exp(s - jnp.max(s, -1, keepdims=True))
        p = (e / jnp.sum(e, -1, keepdims=True)).astype(bf16)
        p_ref[h] = p
        mixed.append(dot(p, v[:, at]).astype(bf16))
    mixed = jnp.concatenate(mixed, 1)
    m_ref[...] = mixed
    part = dot(mixed, wout[...])
    send_ref[...] = part.astype(bf16)
    base_ref[...] = x.astype(f32) + part + vec[0:1]


def feed_fwd(place, base, got, wup, bup, wdown, vec, hat_ref, scale_ref, act_ref, slope_ref, out_ref, send_ref):
    hat, scale = norm_stats(base[...] + turned(got[...]).astype(f32))
    hat_ref[...], scale_ref[...] = hat, scale
    h1 = hat * vec[3:4] + vec[6:7]
    act, slope = gelu_pair(dot(h1.astype(bf16), wup[...]) + bup[...].astype(f32))
    act = act.astype(bf16)
    act_ref[...] = act
    slope_ref[...] = slope.astype(bf16)
    part = dot(act, wdown[...])
    send_ref[...] = part.astype(bf16)
    out_ref[...] = h1 + part + vec[1:2]


def unite(halves, place, base, got, cm, co, conv, tm, to, vec, *rest):
    picks, rest = rest[: 0 if halves.direct else 2], rest[0 if halves.direct else 2 :]
    res_ref, dc_ref, dr_ref, sums_ref, gone_ref, kept_ref, turned_ref, cat_ref = rest
    core = place[1]
    hat2, scale2 = norm_stats(base[...] + turned(got[...]).astype(f32))
    h2 = hat2 * vec[4:5] + vec[7:8]
    joined = jnp.concatenate([h2.astype(bf16), pair_of(cm[...], co[...])], 1)
    rows = joined.shape[0]
    width = h2.shape[1]
    spot = lax.broadcasted_iota(jnp.int32, (rows, 1), 0)
    half = rows // 2
    not_first = (spot != core * half).astype(f32)
    not_last = (spot != (rows - 1 + core * half) % rows).astype(f32)
    later = lambda a: pltpu.roll(a, 1, 0) * not_first
    sooner = lambda a: pltpu.roll(a, rows - 1, 0) * not_last
    raw = later(dot(joined, conv[0])) + dot(joined, conv[1]) + sooner(dot(joined, conv[2])) + vec[2:3]
    act, slope = gelu_pair(raw)
    hat3, scale3 = norm_stats(h2 + act)
    res_ref[...] = (hat3 * vec[5:6] + vec[8:9])[:half].astype(bf16)
    cot = pair_of(tm[...], to[...]).astype(f32)
    d_r3 = norm_back(cot, hat3, scale3, vec[5:6])
    d_f = (d_r3 * slope).astype(bf16).astype(f32)
    d_fs = [sooner(d_f).astype(bf16), d_f.astype(bf16), later(d_f).astype(bf16)]
    d_h2 = d_r3 + sum(dot_r(d_fs[i], conv[i, :width]) for i in range(3))
    dc_ref[...] = sum(dot_r(d_fs[i][:half], conv[i, width:]) for i in range(3))
    d_r2 = norm_back(d_h2, hat2, scale2, vec[4:5])
    dr_ref[...] = d_r2
    sums = [own_sum(d_r2), own_sum(d_f), own_sum(d_h2 * hat2), own_sum(cot * hat3), own_sum(d_h2), own_sum(cot)]
    for i, value in enumerate(sums):
        sums_ref[i : i + 1] = value
    span = width // 2
    for i in range(3):
        cat_ref[i] = d_fs[i]
        part = cat_ref[i, :, pl.ds(pl.multiple_of(core * span, 128), span)]
        if i == 0:
            gone, kept = halves.sides(joined, turned_ref, place, picks)
        gone_ref[:, i * span : (i + 1) * span] = dot(gone, part).astype(bf16)
        kept_ref[:, i * span : (i + 1) * span] = dot(kept, part).astype(bf16)


def feed_back(halves, place, dr, act, slope, hat, wup, wdown, vec, *rest):
    picks, rest = rest[: 0 if halves.direct else 2], rest[0 if halves.direct else 2 :]
    base_ref, send_ref, sum_ref, gone_ref, kept_ref, turned_ref = rest
    low = dr[...].astype(bf16)
    d_u = (dot_r(low, wdown[...]) * slope[...].astype(f32)).astype(bf16)
    sum_ref[...] = jnp.sum(d_u.astype(f32), 0, keepdims=True)
    part = dot_r(d_u, wup[...])
    send_ref[...] = part.astype(bf16)
    base_ref[...] = dr[...] + part
    h1 = (hat[...] * vec[3:4] + vec[6:7]).astype(bf16)
    span = d_u.shape[1]
    for place_, (left, right) in enumerate(((h1, d_u), (low, act[...]))):
        gone, kept = halves.sides(left, turned_ref, place, picks)
        gone_ref[:, place_ * span : (place_ + 1) * span] = dot(gone, right).astype(bf16)
        kept_ref[:, place_ * span : (place_ + 1) * span] = dot(kept, right).astype(bf16)


def attend_back(halves, place, base, got, hat, scale, q, k, v, p, mixed, mine, other, wqkv, wout, vec, *rest):
    picks, rest = rest[: 0 if halves.direct else 2], rest[0 if halves.direct else 2 :]
    base_ref, send_ref, sums_ref, shift_ref, gone_ref, kept_ref, turned_ref = rest
    d_h1 = base[...] + turned(got[...]).astype(f32)
    d_r1 = norm_back(d_h1, hat[...], scale[...], vec[3:4])
    for i, value in enumerate((own_sum(d_r1), own_sum(d_h1 * hat[...]), own_sum(d_h1))):
        sums_ref[i : i + 1] = value
    low = d_r1.astype(bf16)
    d_mixed = dot_r(low, wout[...]).astype(bf16)
    d_q, d_k, d_v = [], [], []
    for h in range(p.shape[0]):
        at = slice(h * HD, (h + 1) * HD)
        prob = p[h].astype(f32)
        d_p = dot_r(d_mixed[:, at], v[:, at])
        d_v.append(dot_t(p[h], d_mixed[:, at]).astype(bf16))
        d_s = (prob * (d_p - jnp.sum(prob * d_p, -1, keepdims=True))).astype(bf16)
        d_q.append((dot(d_s, k[:, at]) * HD**-0.5).astype(bf16))
        d_k.append((dot_t(d_s, q[:, at]) * HD**-0.5).astype(bf16))
    d_proj = [jnp.concatenate(a, 1) for a in (d_q, d_k, d_v)]
    shift_ref[0:1] = jnp.sum(d_proj[0].astype(f32), 0, keepdims=True)
    shift_ref[1:2] = jnp.sum(d_proj[2].astype(f32), 0, keepdims=True)
    part = sum(dot_r(d_proj[i], wqkv[i]) for i in range(3))
    rows = part.shape[0] // 2
    base_ref[...] = d_r1[:rows] + part[:rows]
    send_ref[...] = part[rows:].astype(bf16)
    span = d_mixed.shape[1]
    x = pair_of(mine[...], other[...])
    gone, kept = halves.sides(x, turned_ref, place, picks)
    for i in range(3):
        gone_ref[:, i * span : (i + 1) * span] = dot(gone, d_proj[i]).astype(bf16)
        kept_ref[:, i * span : (i + 1) * span] = dot(kept, d_proj[i]).astype(bf16)
    gone, kept = halves.sides(low, turned_ref, place, picks)
    gone_ref[:, 3 * span :] = dot(gone, mixed[...]).astype(bf16)
    kept_ref[:, 3 * span :] = dot(kept, mixed[...]).astype(bf16)


class Packing:
    def __init__(self, width, embed, gh, vocab):
        self.width, self.embed, self.gh, self.vocab = width, embed, gh, vocab
        self.groups = 6 * gh // width
        self.per_row = width // embed
        self.long = -(-vocab // (16 * self.per_row)) * 16
        self.hid_at = self.groups * embed
        self.table_at = self.hid_at + self.groups * gh
        self.small_at = self.table_at + self.long
        unit = 16 * lax.axis_size("dp")
        if lax.axis_size("dp") % 8 == 0:
            unit = 8 * lax.axis_size("dp")
        self.rows = -(-(self.small_at + 32) // unit) * unit
        self.half = self.rows // 2


def put(pack, core, kept_ref, gone_ref, at, value):
    rows = value.shape[0]
    cuts = [(max(at, h * pack.half), min(at + rows, (h + 1) * pack.half), h) for h in range(2)]
    for low, high, h in cuts:
        if high > low:
            piece = value[low - at : high - at].astype(bf16)
            where = slice(low - h * pack.half, high - h * pack.half)

            @pl.when(core == h)
            def _(piece=piece, where=where):
                kept_ref[where] = piece

            @pl.when(core != h)
            def _(piece=piece, where=where):
                gone_ref[where] = piece


def gru_weights(pack, place, gf, gb, hpf, hpb, emb, ids, win, small, kept_ref, gone_ref, hid_acc, in_acc, table_acc):
    i = pl.program_id(0)
    gh = hpf.shape[-1]
    flat = lambda ref: ref[...].reshape(-1, ref.shape[-1])

    @pl.when(i == 0)
    def _():
        hid_acc[...] = jnp.zeros_like(hid_acc)
        in_acc[...] = jnp.zeros_like(in_acc)
        table_acc[...] = jnp.zeros_like(table_acc)

    e = flat(emb)
    d_e = 0.0
    for d, (g, before) in enumerate(((gf, hpf), (gb, hpb))):
        grads = flat(g)
        hid_acc[d] += dot_t(flat(before), grads[:, : 3 * gh])
        in_acc[d] += dot_t(e, grads[:, gh:])
        d_e = d_e + dot_r(grads[:, gh:], win[d])
    chosen = lax.broadcasted_iota(jnp.int32, (pack.vocab, e.shape[0]), 0) == ids[0]
    table_acc[...] += dot(chosen.astype(bf16), d_e.astype(bf16))

    @pl.when(i == pl.num_programs(0) - 1)
    def _():
        core = place[1]
        store = lambda at, value: put(pack, core, kept_ref, gone_ref, at, value)
        whole = jnp.concatenate([in_acc[0], in_acc[1]], 1)
        for g in range(pack.groups):
            store(g * pack.embed, whole[:, g * pack.width : (g + 1) * pack.width])
        whole = jnp.concatenate(
            [a for d in range(2) for a in (hid_acc[d, :, gh:], hid_acc[d, :, :gh])], 1
        )
        for g in range(pack.groups):
            store(pack.hid_at + g * gh, whole[:, g * pack.width : (g + 1) * pack.width])
        parts = []
        for g in range(pack.per_row):
            part = table_acc[g * pack.long : min((g + 1) * pack.long, pack.vocab)]
            short = pack.long - part.shape[0]
            if short:
                part = jnp.concatenate([part, jnp.zeros((short, pack.embed), f32)], 0)
            parts.append(part)
        store(pack.table_at, jnp.concatenate(parts, 1))
        store(pack.small_at, small[...])


def gru_pack(pack, place, gf, gb, hpf, hpb, emb, ids, win, small, step):
    slots, rows, gh = hpf.shape
    count = slots // step
    blk = lambda a: pl.BlockSpec((step,) + a.shape[1:], lambda i: (i, 0, 0))
    full = lambda a: pl.BlockSpec(a.shape, lambda i: (0,) * a.ndim)
    out = jax.ShapeDtypeStruct((pack.half, pack.width), bf16)
    return pl.pallas_call(
        lambda *refs: gru_weights(pack, *refs),
        grid=(count,),
        in_specs=[SMEM]
        + [blk(a) for a in (gf, gb, hpf, hpb, emb)]
        + [pl.BlockSpec((1, 1, step * rows), lambda i: (i, 0, 0)), full(win), full(small)],
        out_specs=[pl.BlockSpec((pack.half, pack.width), lambda i: (0, 0))] * 2,
        out_shape=[out, out],
        scratch_shapes=[
            pltpu.VMEM((2, gh, 3 * gh), f32),
            pltpu.VMEM((2, pack.embed, 3 * gh), f32),
            pltpu.VMEM((pack.vocab, pack.embed), f32),
        ],
        compiler_params=pltpu.CompilerParams(vmem_limit_bytes=48 << 20),
        cost_estimate=pl.CostEstimate(flops=1 << 20, bytes_accessed=1 << 10, transcendentals=0),
        name="gru_pack",
    )(place, gf, gb, hpf, hpb, emb, ids.reshape(count, 1, step * rows), win, small)


def unpack(pack, place, own, got, in_ref, hid_ref, table_ref, small_ref, all_ref):
    core = place[1]
    start = pl.multiple_of(core * pack.half, 16)
    all_ref[pl.ds(start, pack.half), :] = own[...]
    start = pl.multiple_of((1 - core) * pack.half, 16)
    all_ref[pl.ds(start, pack.half), :] = got[...]
    gh, width = pack.gh, pack.width
    for at, length, ref in ((0, pack.embed, in_ref), (pack.hid_at, gh, hid_ref)):
        for g in range(pack.groups):
            piece = all_ref[at + g * length : at + (g + 1) * length].astype(f32)
            for d in range(2):
                low, high = max(g * width, d * 3 * gh), min((g + 1) * width, (d + 1) * 3 * gh)
                if high > low:
                    ref[d, :, low - d * 3 * gh : high - d * 3 * gh] = piece[:, low - g * width : high - g * width]
    for g in range(pack.per_row):
        count = min((g + 1) * pack.long, pack.vocab) - g * pack.long
        piece = all_ref[pack.table_at : pack.table_at + count, g * pack.embed : (g + 1) * pack.embed]
        table_ref[g * pack.long : g * pack.long + count] = piece.astype(f32)
    small_ref[...] = all_ref[pack.small_at : pack.small_at + 32].astype(f32)


def swap(values):
    return lax.ppermute(values, "mp", [(0, 1), (1, 0)])


def flip(values, bit):
    count = lax.axis_size("dp")
    return lax.ppermute(values, "dp", [(i, i ^ (1 << bit)) for i in range(count)])


def bit_of(bit):
    return (lax.axis_index("dp") >> bit) & 1


def added(left, right, dtype=bf16):
    return (left.astype(f32) + right.astype(f32)).astype(dtype)


def reduce_rows(gone, kept, order, last=f32):
    count = lax.axis_size("dp")
    bits = count.bit_length() - 1
    held = [bit for bit in range(bits)[::-1] if bit != order[0]]
    shape = (2,) * (bits - 1) + (kept.shape[0] * 2 // count, kept.shape[1])
    got = flip(gone, order[0]).reshape(shape)
    kept = kept.reshape(shape)
    for bit in order[1:]:
        axis = held.index(bit)
        side = lambda a, index: lax.dynamic_index_in_dim(a, index, axis, keepdims=False)
        mine = bit_of(bit)
        gone = added(side(kept, 1 - mine), side(got, 1 - mine))
        kept = added(side(kept, mine), side(got, mine))
        got = flip(gone, bit)
        held.pop(axis)
    return added(kept, got, last)


def all_sum(block, order):
    dims = []
    for bit in order:
        dim = 0 if block.shape[0] % 16 == 0 else 1
        dims.append(dim)
        size = block.shape[dim] // 2
        side = lambda index: lax.dynamic_slice_in_dim(block, index * size, size, dim)
        mine = bit_of(bit)
        block = added(side(mine), flip(side(1 - mine), bit))
    for bit, dim in zip(order[::-1], dims[::-1]):
        got = flip(block, bit)
        block = jnp.where(
            bit_of(bit) == 0, jnp.concatenate([block, got], dim), jnp.concatenate([got, block], dim)
        )
    return block


def per_device(
    tokens,
    cotangent,
    char_ids,
    char_lens,
    w_qkv,
    b_qkv,
    w_out,
    w_up,
    up_bias,
    w_down,
    res_bias,
    norm_gain,
    norm_bias,
    char_table,
    gru_in,
    gru_hid,
    gru_bias,
    conv_w,
):
    core = lax.axis_index("mp")
    place = jnp.stack([lax.axis_index("dp"), core]).astype(jnp.int32)
    rows, width = tokens.shape
    both = 2 * rows
    slots = char_ids.shape[1]
    vocab, embed = char_table.shape
    gh = gru_hid.shape[2]
    bits = list(range(lax.axis_size("dp").bit_length() - 1))
    order_a = bits
    order_b = bits[1::-1] + bits[2:]
    order_c = bits[2:3] + bits[:2] + bits[3:]
    wqkv = w_qkv[0].swapaxes(0, 1)
    cols = wqkv.shape[2]
    wout, wup, wdown, conv = w_out[0], w_up[0], w_down[0], conv_w[0]
    units = wup.shape[1]
    vec = jnp.concatenate([res_bias[0], norm_gain[0], norm_bias[0]], 0).astype(f32)
    heads = cols // HD

    tokens_other = swap(tokens)
    cot_other = swap(cotangent)

    ids = char_ids.T.reshape(-1)
    one_hot = (ids[:, None] == jnp.arange(vocab, dtype=jnp.int32)[None, :]).astype(bf16)
    emb = dot(one_hot, char_table).astype(bf16).reshape(slots, rows, embed)
    chars, cof, chf, hpf, cob, chb, hpb = gru_fwd(
        emb, char_lens[:, None], gru_in[0], gru_hid[0], gru_bias[0].astype(f32).reshape(4, -1)
    )
    chars_other = swap(chars)

    q, k, v, p, mixed, base, send = whole_call(
        attend_fwd,
        (place, tokens, tokens_other, wqkv, b_qkv[0], wout, vec),
        [((both, cols), bf16)] * 3
        + [((heads, both, both), bf16), ((both, cols), bf16), ((both, width), f32), ((both, width), bf16)],
        [],
        24,
        2 << 30,
        "attend_fwd",
    )
    hat1, scale1, act, slope, base, send = whole_call(
        feed_fwd,
        (place, base, swap(send), wup, up_bias, wdown, vec),
        [((both, width), f32), ((both, 1), f32), ((both, units), bf16), ((both, units), bf16)]
        + [((both, width), f32), ((both, width), bf16)],
        [],
        24,
        2 << 30,
        "feed_fwd",
    )
    halves = Halves(2 * width, order_a[0])
    span = 3 * width // 2
    result, d_chars, d_r2, sums_b, gone, kept = whole_call(
        lambda *refs: unite(halves, *refs),
        (place, base, swap(send), chars, chars_other, conv, cotangent, cot_other, vec, *halves.operands()),
        [((rows, width), bf16), ((rows, width), f32), ((both, width), f32), ((6, width), f32)]
        + [((width, span), bf16)] * 2,
        halves.scratch(both) + [pltpu.VMEM((3, both, width), bf16)],
        32,
        4 << 30,
        "unite",
    )
    kernel = reduce_rows(gone, kept, order_a, bf16)

    halves = Halves(width, order_b[0])
    base, send, up_shift, gone, kept = whole_call(
        lambda *refs: feed_back(halves, *refs),
        (place, d_r2, act, slope, hat1, wup, wdown, vec, *halves.operands()),
        [((both, width), f32), ((both, width), bf16), ((1, units), f32)] + [((width // 2, 2 * units), bf16)] * 2,
        halves.scratch(both),
        24,
        4 << 30,
        "feed_back",
    )
    feed_grad = reduce_rows(gone, kept, order_b)

    halves = Halves(width, order_c[0])
    base, send, sums_a, q_shift, gone, kept = whole_call(
        lambda *refs: attend_back(halves, *refs),
        (place, base, swap(send), hat1, scale1, q, k, v, p, mixed, tokens, tokens_other, wqkv, wout, vec)
        + tuple(halves.operands()),
        [((rows, width), f32), ((rows, width), bf16), ((3, width), f32), ((2, cols), f32)]
        + [((width // 2, 4 * cols), bf16)] * 2,
        halves.scratch(both),
        24,
        4 << 30,
        "attend_back",
    )
    tokens_grad = base + swap(send).astype(f32)
    attend_grad = reduce_rows(gone, kept, order_c)

    hid = gru_hid[0]
    hid_t = jnp.concatenate([hid[:, :, 2 * gh :], hid[:, :, : 2 * gh]], 2).transpose(0, 2, 1)
    g_f, g_b, sums = gru_bwd(d_chars, hid_t, cof, chf, cob, chb)

    side = jnp.concatenate([q_shift.reshape(1, -1), up_shift], 1).reshape(-1, width)
    zero = jnp.zeros_like(side)
    shifts = [jnp.concatenate([sums[d, gh:], sums[d, gh : 3 * gh], sums[d, :gh]]) for d in range(2)]
    small = jnp.concatenate(
        [
            sums_a[0:1],
            sums_b[0:2],
            sums_a[1:2],
            sums_b[2:4],
            sums_a[2:3],
            sums_b[4:6],
            jnp.concatenate(shifts).reshape(-1, width),
            jnp.where(core == 0, side, zero),
            jnp.where(core == 1, side, zero),
        ],
        0,
    )
    small = jnp.pad(small, ((0, 32 - small.shape[0]), (0, 0)))
    pack = Packing(width, embed, gh, vocab)
    kept, gone = gru_pack(pack, place, g_f, g_b, hpf, hpb, emb, ids, gru_in[0], small, 4)
    own = all_sum(added(kept, swap(gone)), order_a)
    in_out, hid_out, table_out, small = whole_call(
        lambda *refs: unpack(pack, *refs),
        (place, own, swap(own)),
        [((2, embed, 3 * gh), f32), ((2, gh, 3 * gh), f32), ((vocab, embed), f32), ((32, width), f32)],
        [pltpu.VMEM((pack.rows, width), bf16)],
        32,
        1 << 20,
        "unpack",
    )
    res_out, gain_out, offset_out = small[:9].reshape(3, 1, 3, width)
    shift_out = small[9:15].reshape(1, 2, 2, 3 * gh)
    sides = lax.dynamic_slice_in_dim(small, 15 + core * side.shape[0], side.shape[0], 0).reshape(-1)
    kernel_other = swap(kernel)
    low = jnp.where(core == 0, kernel, kernel_other)
    high = jnp.where(core == 0, kernel_other, kernel)
    cut = width // 2
    kernel = jnp.stack(
        [jnp.concatenate([a[:, i * cut : (i + 1) * cut] for a in (low, high)], 1) for i in range(3)]
    ).astype(f32)
    qkv_grad = jnp.stack([attend_grad[:, i * cols : (i + 1) * cols] for i in range(3)], 1)
    return (
        result,
        tokens_grad,
        qkv_grad[None],
        sides[: 2 * cols].reshape(1, 2, cols),
        attend_grad[:, 3 * cols :].T[None],
        feed_grad[:, :units][None],
        sides[2 * cols :][None],
        feed_grad[:, units:].T[None],
        res_out,
        gain_out,
        offset_out,
        table_out,
        in_out[None],
        hid_out[None],
        shift_out,
        kernel[None],
    )


def solution(mesh):
    return jax.shard_map(
        per_device,
        mesh=mesh,
        in_specs=(
            P(("dp", "mp"), None),
            P(("dp", "mp"), None),
            P(("dp", "mp"), None),
            P(("dp", "mp")),
            P(None, None, None, "mp"),
            P(None, None, "mp"),
            P(None, "mp", None),
            P(None, None, "mp"),
            P(None, "mp"),
            P(None, "mp", None),
            P(),
            P(),
            P(),
            P(),
            P(),
            P(),
            P(),
            P(),
        ),
        out_specs=(
            P(("dp", "mp"), None),
            P(("dp", "mp"), None),
            P(None, "dp", None, "mp"),
            P(None, None, "mp"),
            P(None, "mp", "dp"),
            P(None, "dp", "mp"),
            P(None, "mp"),
            P(None, "mp", "dp"),
            P(),
            P(),
            P(),
            P(),
            P(),
            P(),
            P(),
            P(None, None, "dp", None),
        ),
        check_vma=False,
    )
```

```python
import jax
import jax.numpy as jnp
from jax import lax
from jax.experimental import pallas as pl
from jax.experimental.pallas import tpu as pltpu
from jax.sharding import PartitionSpec as P

HD = 64
EPSILON = 1e-05
bf16 = jnp.bfloat16
f32 = jnp.float32


def dot(left, right):
    return jnp.dot(left, right, preferred_element_type=f32)


def dot_t(left, right):
    return lax.dot_general(left, right, (((0,), (0,)), ((), ())), preferred_element_type=f32)


def dot_r(left, right):
    return lax.dot_general(left, right, (((1,), (1,)), ((), ())), preferred_element_type=f32)


def sigmoid(x):
    return 0.5 * jnp.tanh(0.5 * x) + 0.5


class Far:
    def __init__(self, value):
        self.value = value


class Block:
    def __init__(self, value):
        self.value = value


class Side:
    def __init__(self, value, bit, stays):
        self.value, self.bit, self.stays = value, bit, stays


class Sequence:
    def __init__(self, place):
        self.place = place
        self.last = None

    def call(self, kernel, ins, outs, scratch=(), limit=24, name="step", token=0):
        once = dict(pipeline_mode=pl.Buffered(1))
        whole = lambda n: lambda i, p: (0,) * n
        operands, specs = [], []
        for item in ins:
            if isinstance(item, Far):
                operands.append(item.value)
                specs.append(pl.BlockSpec(memory_space=pltpu.HBM))
            elif isinstance(item, Side):
                shape = item.value.shape

                def index(i, p, item=item):
                    mine = (p[0] >> item.bit) & 1
                    return (0, mine if item.stays else 1 - mine, 0, 0)

                operands.append(item.value)
                specs.append(pl.BlockSpec((shape[0], 1) + shape[2:], index, **once))
            elif isinstance(item, Block):
                operands.append(item.value)
                specs.append(pl.BlockSpec(item.value.shape, whole(item.value.ndim), **once))
            else:
                operands.append(item)
                specs.append(pl.BlockSpec(memory_space=pltpu.VMEM))
        out_specs, out_shape = [], []
        for item in outs:
            shape, dtype = item.value if isinstance(item, (Far, Block)) else item
            out_shape.append(jax.ShapeDtypeStruct(shape, dtype))
            if isinstance(item, Far):
                out_specs.append(pl.BlockSpec(memory_space=pltpu.HBM))
            elif isinstance(item, Block):
                out_specs.append(pl.BlockSpec(shape, whole(len(shape)), **once))
            else:
                out_specs.append(pl.BlockSpec(memory_space=pltpu.VMEM))
        count = len(ins)
        held = self.last is not None
        if held:
            operands.append(self.last)
            specs.append(pl.BlockSpec(memory_space=pl.ANY))

        def body(place, *refs):
            kernel(place, *refs[:count], *refs[count + held :])

        out = pl.pallas_call(
            body,
            grid_spec=pltpu.PrefetchScalarGridSpec(
                num_scalar_prefetch=1, grid=(1,), in_specs=specs, out_specs=out_specs, scratch_shapes=list(scratch)
            ),
            out_shape=out_shape,
            compiler_params=pltpu.CompilerParams(vmem_limit_bytes=limit << 20),
            cost_estimate=pl.CostEstimate(flops=1 << 20, bytes_accessed=1 << 10, transcendentals=0),
            name=name,
        )(self.place, *operands)
        self.last = out[token]
        return out


def fetch(pairs, sem):
    copies = [pltpu.make_async_copy(far, near, sem.at[i]) for i, (far, near) in enumerate(pairs)]
    for copy in copies:
        copy.start()
    return lambda i: copies[i].wait()


RING = 4


def gru_fwd(place, emb_far, lens_row, win_far, whid_far, bias, c_ref, co_far, hpt_far, *rest):
    emb, win, whid, co, hpt, h_ref, wsem, sems = rest
    slots, rows, _ = emb.shape
    gh = h_ref.shape[1]
    core = place[1]
    wait = fetch([(win_far.at[core], win), (whid_far.at[core], whid), (emb_far, emb)], wsem)
    h_ref[...] = jnp.zeros_like(h_ref)
    shift = bias[core].astype(f32)
    lens = lens_row[...].astype(f32).T
    for i in range(3):
        wait(i)

    def slot_of(s):
        return jnp.where(core == 0, s, slots - 1 - s)

    def out_copies(s):
        row = pl.multiple_of(s * rows, rows)
        at = pl.multiple_of(slot_of(s) * rows, rows)
        i = s % RING
        return (
            pltpu.make_async_copy(co.at[i], co_far.at[pl.ds(row, rows)], sems.at[0, i]),
            pltpu.make_async_copy(hpt.at[i], hpt_far.at[:, pl.ds(at, rows)], sems.at[1, i]),
        )

    def step(s, carry):
        @pl.when(s >= RING)
        def _():
            for copy in out_copies(s - RING):
                copy.wait()

        i = s % RING
        h = h_ref[...]
        hpt[i] = h.T.astype(bf16)
        mask = (slot_of(s).astype(f32) < lens).astype(f32)
        g = dot(emb[slot_of(s)], win[...]) + shift[0:1]
        y = dot(h.astype(bf16), whid[...]) + shift[1:2]
        r = sigmoid(g[:, :gh] + y[:, :gh])
        z = sigmoid(g[:, gh : 2 * gh] + y[:, gh : 2 * gh])
        yn = y[:, 2 * gh :]
        fresh = jnp.tanh(g[:, 2 * gh :] + r * yn)
        keep = mask * (1.0 - z)
        moved = keep * (h - fresh)
        h_ref[...] = h - moved
        an = keep * (1.0 - fresh * fresh)
        ay = an * r
        ar = ay * yn * (1.0 - r)
        for k, value in enumerate((ay, ar, moved * z, an, keep)):
            co[i, :, k * gh : (k + 1) * gh] = value.astype(bf16)
        for copy in out_copies(s):
            copy.start()
        return carry

    lax.fori_loop(0, slots, step, 0)
    c_ref[...] = h_ref[...].astype(bf16)
    for s in range(max(slots - RING, 0), slots):
        for copy in out_copies(s):
            copy.wait()


AHEAD = 4
SMALL = 9


def split_pack(pack, place, bit, gone_ref, kept_ref):
    half = pack.shape[0] // 2
    mine = (place[0] >> bit) & 1
    gone_ref[...] = pack[pl.ds(pl.multiple_of((1 - mine) * half, 16), half), :]
    kept_ref[...] = pack[pl.ds(pl.multiple_of(mine * half, 16), half), :]


def gru_back(bit, place, dc, whid_far, co_far, hpt_far, g_ref, bias_ref, gone_ref, kept_ref, *rest):
    dh_ref, whid, wht, acc, hpt, co, pack, sem, csem = rest
    rows, gh = dh_ref.shape
    slots = g_ref.shape[0] // rows
    core = place[1]
    wait = fetch([(whid_far.at[core], whid), (hpt_far, hpt)], sem)

    def co_copy(i):
        row = pl.multiple_of((slots - 1 - i) * rows, rows)
        return pltpu.make_async_copy(co_far.at[pl.ds(row, rows)], co.at[i % AHEAD], csem.at[i % AHEAD])

    for i in range(AHEAD - 1):
        co_copy(i).start()
    dh_ref[...] = dc[...]
    acc[...] = jnp.zeros_like(acc)
    wait(0)
    wht[...] = whid[...].T

    def step(i, carry):
        co_copy(i).wait()

        @pl.when(i + AHEAD - 1 < slots)
        def _():
            co_copy(i + AHEAD - 1).start()

        s = slots - 1 - i
        slot = jnp.where(core == 0, s, slots - 1 - s)
        row = pl.multiple_of(slot * rows, rows)
        dh = dh_ref[...]
        held = co.at[i % AHEAD]
        low = []
        for k in range(4):
            part = dh * held[:, k * gh : (k + 1) * gh].astype(f32)
            acc[:, k * gh : (k + 1) * gh] += part.reshape(-1, 8, gh).sum(0)
            low.append(part.astype(bf16))
            g_ref[pl.ds(row, rows), k * gh : (k + 1) * gh] = low[k]
        dy = jnp.concatenate([low[1], low[2], low[0]], 1)
        dh_ref[...] = dh - dh * held[:, 4 * gh :].astype(f32) + dot(dy, wht[...])
        return carry

    lax.fori_loop(0, slots, step, 0)
    wait(1)
    d_hid = dot(hpt[...], g_ref[:, : 3 * gh]).astype(bf16)
    pack[:, 2 * gh :] = d_hid[:, :gh]
    pack[:, : 2 * gh] = d_hid[:, gh:]
    split_pack(pack, place, bit, gone_ref, kept_ref)
    b = acc[...].sum(0, keepdims=True)
    bias_ref[...] = jnp.concatenate([b[:, gh:], b[:, gh : 3 * gh], b[:, :gh]], 1)


def gru_rest(bit, place, g, table, win_far, ids, b, sums_a, sums_b, q_shift, up_shift, *rest):
    gone_ref, kept_ref, win, pack, sem = rest
    embed, gates = win.shape
    vocab = table.shape[0]
    at = g.shape[1] - gates
    core = place[1]
    wait = fetch([(win_far.at[core], win)], sem)
    chosen = (lax.broadcasted_iota(jnp.int32, (vocab, ids.shape[1]), 0) == ids[...]).astype(bf16)
    by_char = dot(chosen, g[:, at:]).astype(bf16)
    pack[:embed] = dot_t(table[...], by_char).astype(bf16)
    wait(0)
    table = dot_r(by_char, win[...]).astype(bf16)
    long = vocab // 4
    for k in range(4):
        pack[embed:, k * embed : (k + 1) * embed] = table[k * long : (k + 1) * long]
    flat = [sums_a[0:1], sums_b[0:1], sums_b[1:2], sums_a[1:2], sums_b[2:3], sums_b[3:4], sums_a[2:3], sums_b[4:5], sums_b[5:6]]
    flat += [b[...], q_shift[0:1], q_shift[1:2], up_shift[...]]
    lanes = jnp.concatenate(flat, 1)
    count = lanes.shape[1] // 128
    tall = [lanes[:, k * 128 : (k + 1) * 128] for k in range(count)]
    tall += [jnp.zeros((1, 128), f32)] * (long - count)
    pack[embed:, 4 * embed :] = jnp.concatenate(tall, 0).astype(bf16)
    split_pack(pack, place, bit, gone_ref, kept_ref)


def rows_in_order(place, bit, own, got):
    low = ((place[0] >> bit) & 1) == 0
    own, got = own[...].astype(f32), got[...].astype(f32)
    return jnp.where(low, own, got), jnp.where(low, got, own)


def unpack_hid(bit, place, own, got, own_other, got_other, out):
    half = own.shape[0]
    for pair, d in (((own, got), place[1]), ((own_other, got_other), 1 - place[1])):
        first, second = rows_in_order(place, bit, *pair)
        out[d, :half] = first
        out[d, half:] = second


def unpack(bit, place, own, got, own_other, got_other, in_ref, table_ref, res_ref, gain_ref, off_ref, bias_ref, q_ref, up_ref):
    core = place[1]
    embed = in_ref.shape[1]
    gates = in_ref.shape[2]
    long = table_ref.shape[0] // 4
    half = own.shape[0]
    tails = []
    for pair, d in (((own, got), core), ((own_other, got_other), 1 - core)):
        first, second = rows_in_order(place, bit, *pair)
        in_ref[d, :half] = first
        in_ref[d, half:] = second[: embed - half]
        tails.append(second[embed - half :])
    mine, other = tails
    both = mine + other
    for k in range(4):
        table_ref[k * long : (k + 1) * long] = both[:, k * embed : (k + 1) * embed]
    line = lambda value, at, count: jnp.concatenate(
        [value[k : k + 1, 4 * embed :] for k in range(at // 128, (at + count) // 128)], 1
    )
    width = res_ref.shape[2]
    for k, ref in enumerate((res_ref, gain_ref, off_ref)):
        for i in range(3):
            ref[i] = line(both, (3 * k + i) * width, width)
    at = SMALL * width
    for value, d in ((mine, core), (other, 1 - core)):
        for i in range(2):
            bias_ref[d, pl.ds(i, 1)] = line(value, at + gates * i, gates)
    at += 2 * gates
    cols = q_ref.shape[1]
    for i in range(2):
        q_ref[i : i + 1] = line(mine, at + i * cols, cols)
    up_ref[...] = line(mine, at + 2 * cols, up_ref.shape[1])


GELU_A = 0.7978845608028654
GELU_B = 0.044715


def norm_stats(total):
    centre = jnp.mean(total, -1, keepdims=True)
    centred = total - centre
    scale = lax.rsqrt(jnp.mean(centred * centred, -1, keepdims=True) + EPSILON)
    return centred * scale, scale


def norm_back(grad, hat, scale, gain):
    scaled = grad * gain
    inner = jnp.mean(scaled, -1, keepdims=True)
    along = jnp.mean(scaled * hat, -1, keepdims=True)
    return (scaled - inner - hat * along) * scale


def gelu_pair(u):
    square = u * u
    t = jnp.tanh(GELU_A * (u + GELU_B * u * square))
    half = 0.5 * (1.0 + t)
    slope = half + 0.5 * u * (1.0 - t * t) * (GELU_A + 3.0 * GELU_A * GELU_B * square)
    return u * half, slope


def turned(values):
    rows = values.shape[0] // 2
    return jnp.concatenate([values[rows:], values[:rows]], 0)


def own_sum(values):
    return jnp.sum(values[: values.shape[0] // 2], 0, keepdims=True)


def pair_of(left, right):
    return jnp.concatenate([left, right], 0)


class Halves:
    def __init__(self, length, bit):
        self.count = lax.axis_size("dp")
        self.length, self.bit = length, bit
        self.chunk = length // self.count
        self.direct = self.chunk % 16 == 0

    def operands(self):
        if self.direct:
            return []
        mine = (lax.axis_index("dp") >> self.bit) & 1
        where = jnp.arange(self.length, dtype=jnp.int32)
        kept = where.reshape(self.count >> (self.bit + 1), 2, -1)
        pick = lambda side: jax.nn.one_hot(
            lax.dynamic_index_in_dim(kept, side, 1, keepdims=False).reshape(-1), self.length, dtype=bf16
        )
        return [pick(1 - mine), pick(mine)]

    def scratch(self, rows):
        return [pltpu.VMEM((self.length, rows), bf16)]

    def sides(self, values, turned_ref, place, picks):
        if not self.direct:
            return [dot_r(pick[...], values).astype(bf16) for pick in picks]
        turned_ref[...] = values.T
        mine = (place[0] >> self.bit) & 1
        out = []
        for side in (1 - mine, mine):
            parts = []
            for k in range(self.count):
                if not (k >> self.bit) & 1:
                    start = pl.multiple_of((k + (side << self.bit)) * self.chunk, 16)
                    parts.append(turned_ref[pl.ds(start, self.chunk), :])
            out.append(jnp.concatenate(parts, 0))
        return out


def attend_fwd(place, mine, other, wqkv_far, bqkv, wout_far, vec, *rest):
    q_ref, k_ref, v_ref, p_ref, m_ref, base_ref, send_ref, wqkv, wout, sem = rest
    wait = fetch([(wqkv_far, wqkv), (wout_far, wout)], sem)
    x = pair_of(mine[...], other[...])
    bias = bqkv[...].astype(f32)
    wait(0)
    q = (dot(x, wqkv[0]) + bias[0:1]).astype(bf16)
    k = dot(x, wqkv[1]).astype(bf16)
    v = (dot(x, wqkv[2]) + bias[1:2]).astype(bf16)
    q_ref[...], k_ref[...], v_ref[...] = q, k, v
    mixed = []
    for h in range(p_ref.shape[0]):
        at = slice(h * HD, (h + 1) * HD)
        s = dot_r(q[:, at], k[:, at]) * HD**-0.5
        e = jnp.exp(s - jnp.max(s, -1, keepdims=True))
        p = (e / jnp.sum(e, -1, keepdims=True)).astype(bf16)
        p_ref[h] = p
        mixed.append(dot(p, v[:, at]).astype(bf16))
    mixed = jnp.concatenate(mixed, 1)
    m_ref[...] = mixed
    wait(1)
    part = dot(mixed, wout[...])
    send_ref[...] = part.astype(bf16)
    base_ref[...] = x.astype(f32) + part + vec[0:1]


def feed_fwd(place, base, got, wup_far, bup, wdown_far, vec, *rest):
    hat_ref, scale_ref, act_ref, slope_ref, out_ref, send_ref, wup, wdown, sem = rest
    wait = fetch([(wup_far, wup), (wdown_far, wdown)], sem)
    hat, scale = norm_stats(base[...] + turned(got[...]).astype(f32))
    hat_ref[...], scale_ref[...] = hat, scale
    h1 = hat * vec[3:4] + vec[6:7]
    wait(0)
    act, slope = gelu_pair(dot(h1.astype(bf16), wup[...]) + bup[...].astype(f32))
    act = act.astype(bf16)
    act_ref[...] = act
    slope_ref[...] = slope.astype(bf16)
    wait(1)
    part = dot(act, wdown[...])
    send_ref[...] = part.astype(bf16)
    out_ref[...] = h1 + part + vec[1:2]


def unite(halves, place, base, got, cm, co, conv_far, tm, to, vec, *rest):
    picks, rest = rest[: 0 if halves.direct else 2], rest[0 if halves.direct else 2 :]
    res_ref, dc_ref, dr_ref, sums_ref, gone_ref, kept_ref, turned_ref, cat_ref, conv, sem = rest
    core = place[1]
    wait = fetch([(conv_far.at[i], conv.at[i]) for i in range(3)], sem)
    hat2, scale2 = norm_stats(base[...] + turned(got[...]).astype(f32))
    h2 = hat2 * vec[4:5] + vec[7:8]
    first = core == 0
    own, theirs = cm[...], turned(co[...])
    chars = [jnp.where(first, own, theirs), jnp.where(first, theirs, own)]
    joined = jnp.concatenate([h2.astype(bf16)] + chars, 1)
    rows = joined.shape[0]
    width = h2.shape[1]
    spot = lax.broadcasted_iota(jnp.int32, (rows, 1), 0)
    half = rows // 2
    not_first = (spot != core * half).astype(f32)
    not_last = (spot != (rows - 1 + core * half) % rows).astype(f32)
    later = lambda a: pltpu.roll(a, 1, 0) * not_first
    sooner = lambda a: pltpu.roll(a, rows - 1, 0) * not_last
    raw = vec[2:3]
    for i, move in enumerate((later, lambda a: a, sooner)):
        wait(i)
        raw = raw + move(dot(joined, conv[i]))
    act, slope = gelu_pair(raw)
    hat3, scale3 = norm_stats(h2 + act)
    res_ref[...] = (hat3 * vec[5:6] + vec[8:9])[:half].astype(bf16)
    cot = pair_of(tm[...], to[...]).astype(f32)
    d_r3 = norm_back(cot, hat3, scale3, vec[5:6])
    d_f = (d_r3 * slope).astype(bf16).astype(f32)
    d_fs = [sooner(d_f).astype(bf16), d_f.astype(bf16), later(d_f).astype(bf16)]
    gh = width // 2
    mine = pl.ds(pl.multiple_of(width + core * gh, 128), gh)
    d_h2 = d_r3 + sum(dot_r(d_fs[i], conv[i, :width]) for i in range(3))
    dc_ref[...] = sum(dot_r(d_fs[i], conv[i, mine]) for i in range(3))
    d_r2 = norm_back(d_h2, hat2, scale2, vec[4:5])
    dr_ref[...] = d_r2
    sums = [own_sum(d_r2), own_sum(d_f), own_sum(d_h2 * hat2), own_sum(cot * hat3), own_sum(d_h2), own_sum(cot)]
    for i, value in enumerate(sums):
        sums_ref[i : i + 1] = value
    span = width // 2
    gone, kept = halves.sides(joined, turned_ref, place, picks)
    for i in range(3):
        cat_ref[i] = d_fs[i]
        part = cat_ref[i, :, pl.ds(pl.multiple_of(core * span, 128), span)]
        gone_ref[:, i * span : (i + 1) * span] = dot(gone, part).astype(bf16)
        kept_ref[:, i * span : (i + 1) * span] = dot(kept, part).astype(bf16)


def feed_back(halves, place, dr, act, slope, hat, wup_far, wdown_far, vec, *rest):
    picks, rest = rest[: 0 if halves[0].direct else 4], rest[0 if halves[0].direct else 4 :]
    base_ref, send_ref, sum_ref = rest[:3]
    turned_ref, wup, wdown, sem = rest[-4:]
    wait = fetch([(wdown_far, wdown), (wup_far, wup)], sem)
    low = dr[...].astype(bf16)
    wait(0)
    d_u = (dot_r(low, wdown[...]) * slope[...].astype(f32)).astype(bf16)
    sum_ref[...] = jnp.sum(d_u.astype(f32), 0, keepdims=True)
    wait(1)
    part = dot_r(d_u, wup[...])
    send_ref[...] = part.astype(bf16)
    base_ref[...] = dr[...] + part
    h1 = (hat[...] * vec[3:4] + vec[6:7]).astype(bf16)
    units = d_u.shape[1]
    if TOGETHER:
        gone_up = gone_down = rest[3]
        kept_up = kept_down = rest[4]
    else:
        gone_up, kept_up, gone_down, kept_down = rest[3:7]
    for i, (left, right, gone_ref, kept_ref) in enumerate(
        ((h1, d_u, gone_up, kept_up), (low, act[...], gone_down, kept_down))
    ):
        at = slice(i * units, (i + 1) * units) if TOGETHER else slice(None)
        gone, kept = halves[i].sides(left, turned_ref, place, picks[2 * i : 2 * i + 2])
        gone_ref[:, at] = dot(gone, right).astype(bf16)
        kept_ref[:, at] = dot(kept, right).astype(bf16)


def attend_back(halves, place, base, got, hat, scale, q, k, v, p, mixed, mine, other, wqkv_far, wout_far, vec, *rest):
    picks, rest = rest[: 0 if halves.direct else 2], rest[0 if halves.direct else 2 :]
    base_ref, send_ref, sums_ref, shift_ref, gone_ref, kept_ref, turned_ref, wqkv, wout, sem = rest
    wait = fetch([(wout_far, wout), (wqkv_far, wqkv)], sem)
    d_h1 = base[...] + turned(got[...]).astype(f32)
    d_r1 = norm_back(d_h1, hat[...], scale[...], vec[3:4])
    for i, value in enumerate((own_sum(d_r1), own_sum(d_h1 * hat[...]), own_sum(d_h1))):
        sums_ref[i : i + 1] = value
    low = d_r1.astype(bf16)
    wait(0)
    d_mixed = dot_r(low, wout[...]).astype(bf16)
    d_q, d_k, d_v = [], [], []
    for h in range(p.shape[0]):
        at = slice(h * HD, (h + 1) * HD)
        prob = p[h].astype(f32)
        d_p = dot_r(d_mixed[:, at], v[:, at])
        d_v.append(dot_t(p[h], d_mixed[:, at]).astype(bf16))
        d_s = (prob * (d_p - jnp.sum(prob * d_p, -1, keepdims=True))).astype(bf16)
        d_q.append((dot(d_s, k[:, at]) * HD**-0.5).astype(bf16))
        d_k.append((dot_t(d_s, q[:, at]) * HD**-0.5).astype(bf16))
    d_proj = [jnp.concatenate(a, 1) for a in (d_q, d_k, d_v)]
    shift_ref[0:1] = jnp.sum(d_proj[0].astype(f32), 0, keepdims=True)
    shift_ref[1:2] = jnp.sum(d_proj[2].astype(f32), 0, keepdims=True)
    wait(1)
    part = sum(dot_r(d_proj[i], wqkv[i]) for i in range(3))
    rows = part.shape[0] // 2
    base_ref[...] = d_r1[:rows] + part[:rows]
    send_ref[...] = part[rows:].astype(bf16)
    span = d_mixed.shape[1]
    x = pair_of(mine[...], other[...])
    gone, kept = halves.sides(x, turned_ref, place, picks)
    for i in range(3):
        gone_ref[:, i * span : (i + 1) * span] = dot(gone, d_proj[i]).astype(bf16)
        kept_ref[:, i * span : (i + 1) * span] = dot(kept, d_proj[i]).astype(bf16)
    gone, kept = halves.sides(low, turned_ref, place, picks)
    gone_ref[:, 3 * span :] = dot(gone, mixed[...]).astype(bf16)
    kept_ref[:, 3 * span :] = dot(kept, mixed[...]).astype(bf16)


def swap(values):
    return lax.ppermute(values, "mp", [(0, 1), (1, 0)])


def flip(values, bit):
    count = lax.axis_size("dp")
    return lax.ppermute(values, "dp", [(i, i ^ (1 << bit)) for i in range(count)])


def added(left, right):
    return left.astype(f32) + right.astype(f32)


def high_groups():
    count = lax.axis_size("dp")
    return [[low + high for high in range(0, count, 4)] for low in range(4)]


class Sum:
    def __init__(self, gone, kept, order):
        self.order = order
        self.stage = 0
        self.kept = kept
        self.rows = kept.shape[0] * 2 // lax.axis_size("dp")
        self.got = flip(gone, order[0])

    def view(self):
        bits = range(lax.axis_size("dp").bit_length() - 1)
        left = [bit for bit in bits[::-1] if bit not in self.order[: self.stage + 1]]
        axis = left.index(self.order[self.stage + 1])
        return 1 << axis, self.rows << (len(left) - 1 - axis)

    def halving(self):
        return self.stage < len(self.order) - 1

    def add(self, seq, name):
        def kernel(place, kept, got, out):
            out[...] = added(kept[...], got[...]).astype(bf16)

        (out,) = seq.call(
            kernel, [Block(self.kept), Block(self.got)], [Block((self.kept.shape, bf16))], limit=16, name=name
        )
        return out


    def close(self, seq, name):
        self.total = self.add(seq, name)


class SumByColumn(Sum):
    def close(self, seq, name):
        total = self.add(seq, name)
        self.total = lax.psum_scatter(
            total, "dp", scatter_dimension=0, axis_index_groups=high_groups(), tiled=True
        )


class SumForAll(Sum):
    def __init__(self, gone, kept, order):
        super().__init__(gone, kept, order)
        self.left = list(range(2, lax.axis_size("dp").bit_length() - 1))

    def view(self):
        return 1, self.kept.shape[0] // 2

    def next(self, seq, name):
        if self.left is not None:
            self.kept = self.add(seq, f"{name}_sum_{len(self.left)}")
            if self.left:
                self.got = flip(self.kept, self.left.pop(0))
            else:
                self.left = None
                self.got = flip(self.kept, self.order[1])
            return False
        bit = self.order[1]

        def kernel(place, own, other, out):
            mine = (place[0] >> bit) & 1
            out[mine] = own[...]
            out[1 - mine] = other[...]

        shape = self.kept.shape
        (out,) = seq.call(
            kernel, [Block(self.kept), Block(self.got)], [Block(((2,) + shape, bf16))], limit=16, name=name + "_join"
        )
        self.block = out.reshape(2 * shape[0], shape[1])
        got = flip(self.block, self.order[0])
        self.quarters = [self.block, got, swap(self.block), swap(got)]
        return True


def halve(seq, sums, name):
    ins, outs = [], []
    for item in sums:
        outer, rows = item.view()
        cols = item.kept.shape[-1]
        bit = item.order[item.stage + 1]
        for stays in (False, True):
            for value in (item.kept, item.got):
                ins.append(Side(value.reshape(outer, 2, rows, cols), bit, stays))
        outs += [Block(((outer * rows, cols), bf16))] * 2

    def kernel(place, *refs):
        for i in range(len(sums)):
            for j in range(2):
                left, right = refs[4 * i + 2 * j : 4 * i + 2 * j + 2]
                out = refs[4 * len(sums) + 2 * i + j]
                out[...] = added(left[:, 0], right[:, 0]).astype(bf16).reshape(out.shape)

    out = seq.call(kernel, ins, outs, limit=24, name=name, token=1)
    for i, item in enumerate(sums):
        item.stage += 1
        item.got = flip(out[2 * i], item.order[item.stage])
        item.kept = out[2 * i + 1]


def finish_rows(place, *refs):
    count = 2 if refs[0].shape == refs[1].shape and refs[0].dtype == refs[1].dtype else 1
    total = added(refs[0][...], refs[1][...]) if count == 2 else refs[0][...].astype(f32)
    at = 0
    for out in refs[count:]:
        parts = [out] if len(out.shape) == 2 else [out.at[i] for i in range(out.shape[0])]
        for part in parts:
            part[...] = total[:, at : at + part.shape[1]].astype(part.dtype)
            at += part.shape[1]


def finish_kernel(place, own, got, out):
    span = own.shape[1] // 3
    first = place[1] == 0
    for i in range(3):
        at = slice(i * span, (i + 1) * span)
        mine, other = own[:, at].astype(f32), got[:, at].astype(f32)
        out[i, :, :span] = jnp.where(first, mine, other)
        out[i, :, span:] = jnp.where(first, other, mine)


ORDERS = (
    (1, 0, 2, 3),
    (2, 1, 0, 3),
    (0, 1, 2, 3),
    (2, 0, 1, 3),
    (0, 1),
    (0, 1),
)
PLAN = (
    "feed", "gru", "attend_back", "rest", "up", "conv", "hid", "down",
    "in", "hid", "attend", "in", "hid", "in", "conv", "tokens",
    "hid", "up", "in", "down", "hid", "attend", "up", "in",
    "conv", "conv", "conv_out", "down", "attend", "up", "hid_out", "down",
    "attend",
)
BY_COLUMN = ()
TOGETHER = False


def per_device(
    tokens,
    cotangent,
    char_ids,
    char_lens,
    w_qkv,
    b_qkv,
    w_out,
    w_up,
    up_bias,
    w_down,
    res_bias,
    norm_gain,
    norm_bias,
    char_table,
    gru_in,
    gru_hid,
    gru_bias,
    conv_w,
):
    core = lax.axis_index("mp")
    seq = Sequence(jnp.stack([lax.axis_index("dp"), core]).astype(jnp.int32))
    rows, width = tokens.shape
    both = 2 * rows
    slots = char_ids.shape[1]
    vocab, embed = char_table.shape
    gh = gru_hid.shape[2]
    count = lax.axis_size("dp")
    bits = list(range(count.bit_length() - 1))
    first = lambda *lead: list(lead) + [b for b in bits if b not in lead]
    wqkv = w_qkv[0].swapaxes(0, 1)
    cols = wqkv.shape[2]
    wout, wup, wdown, conv = w_out[0], w_up[0], w_down[0], conv_w[0]
    units = wup.shape[1]
    vec = jnp.concatenate([res_bias[0], norm_gain[0], norm_bias[0]], 0).astype(f32)
    heads = cols // HD
    dma = pltpu.SemaphoreType.DMA
    near = lambda a, dtype=bf16: pltpu.VMEM(a, dtype)

    letters = jnp.concatenate([char_ids.T, char_lens[None]], 0)
    letters_other = swap(letters)
    tokens_other = swap(tokens)
    cot_other = swap(cotangent)
    letters = jnp.concatenate([letters, letters_other], 1)
    q, k, v, p, mixed, base, send = seq.call(
        attend_fwd,
        [tokens, tokens_other, Far(wqkv), b_qkv[0], Far(wout), vec],
        [((both, cols), bf16)] * 3
        + [((heads, both, both), bf16), ((both, cols), bf16), ((both, width), f32), ((both, width), bf16)],
        [near(wqkv.shape), near(wout.shape), dma((2,))],
        name="attend_fwd",
        token=6,
        limit=24,
    )
    got = swap(send)
    tall = slots * both
    ids = letters[:slots].reshape(1, tall)
    one_hot = (ids.reshape(-1, 1) == jnp.arange(vocab, dtype=jnp.int32)[None, :]).astype(bf16)
    emb = dot(one_hot, char_table).astype(bf16)
    chars, co, hpt = seq.call(
        gru_fwd,
        [Far(emb.reshape(slots, both, embed)), letters[slots:], Far(gru_in[0]), Far(gru_hid[0]), gru_bias[0]],
        [((both, gh), bf16), Far(((3 * tall, 5 * gh), bf16)), Far(((gh, tall), bf16))],
        [near((slots, both, embed)), near(gru_in.shape[2:]), near(gru_hid.shape[2:]), near((RING, both, 5 * gh))]
        + [near((RING, gh, both)), near((both, gh), f32), dma((3,)), dma((2, RING))],
        limit=20,
        name="gru_fwd",
    )
    chars_other = swap(chars)
    hat1, scale1, act, slope, base, send = seq.call(
        feed_fwd,
        [base, got, Far(wup), up_bias, Far(wdown), vec],
        [((both, width), f32), ((both, 1), f32), ((both, units), bf16), ((both, units), bf16)]
        + [((both, width), f32), ((both, width), bf16)],
        [near(wup.shape), near(wdown.shape), dma((2,))],
        name="feed_fwd",
        token=5,
        limit=24,
    )
    orders = [first(*order) for order in ORDERS]
    conv_order, up_order, down_order, attend_order, hid_order, in_order = orders
    halves = Halves(2 * width, conv_order[0])
    span = 3 * width // 2
    result, d_chars, d_r2, sums_b, gone, kept = seq.call(
        lambda *refs: unite(halves, *refs),
        [base, swap(send), chars, chars_other, Far(conv), cotangent, cot_other, vec, *halves.operands()],
        [Block(((rows, width), bf16)), ((both, gh), f32), ((both, width), f32), ((6, width), f32)]
        + [Block(((width, span), bf16))] * 2,
        halves.scratch(both) + [near((3, both, width)), near(conv.shape), dma((3,))],
        limit=32,
        name="unite",
        token=3,
    )
    def summed(name, gone, kept, order):
        sums[name] = SumByColumn(gone, kept, order[:2]) if name in BY_COLUMN else Sum(gone, kept, order)

    sums = {}
    summed("conv", gone, kept, conv_order)
    done = {}
    chunk = width // count

    def feed():
        halves = (Halves(width, up_order[0]), Halves(width, down_order[0]))
        sizes = [Block(((width // 2, units), bf16))] * 4
        if TOGETHER:
            sizes = [Block(((width // 2, 2 * units), bf16))] * 2
        out = seq.call(
            lambda *refs: feed_back(halves, *refs),
            [d_r2, act, slope, hat1, Far(wup), Far(wdown), vec, *halves[0].operands(), *halves[1].operands()],
            [((both, width), f32), ((both, width), bf16), ((1, units), f32)] + sizes,
            halves[0].scratch(both) + [near(wup.shape), near(wdown.shape), dma((2,))],
            name="feed_back",
            token=2,
        )
        base, send, done["up_shift"] = out[:3]
        done["feed"] = base, swap(send)
        if TOGETHER:
            summed("ud", *out[3:], up_order)
        else:
            summed("up", *out[3:5], up_order)
            summed("down", *out[5:], down_order)

    def attend():
        halves = Halves(width, attend_order[0])
        base, send, done["sums"], done["q_shift"], gone, kept = seq.call(
            lambda *refs: attend_back(halves, *refs),
            [*done["feed"], hat1, scale1, q, k, v, p, mixed, tokens, tokens_other, Far(wqkv), Far(wout), vec]
            + halves.operands(),
            [((rows, width), f32), ((rows, width), bf16), ((3, width), f32), ((2, cols), f32)]
            + [Block(((width // 2, 4 * cols), bf16))] * 2,
            halves.scratch(both) + [near(wqkv.shape), near(wout.shape), dma((2,))],
            name="attend_back",
            token=2,
            limit=24,
        )
        done["attend"] = base, swap(send)
        summed("attend", gone, kept, attend_order)

    def tokens_end():
        def kernel(place, base, got, out):
            out[...] = added(base[...], got[...])

        (done["tokens"],) = seq.call(
            kernel, [Block(a) for a in done["attend"]], [Block(((rows, width), f32))], name="tokens_end"
        )

    def chars_back():
        done["g"], done["bias"], gone, kept = seq.call(
            lambda *refs: gru_back(hid_order[0], *refs),
            [d_chars, Far(gru_hid[0]), Far(co), Far(hpt)],
            [((tall, 4 * gh), bf16), ((1, 6 * gh), f32)] + [Block(((gh // 2, 3 * gh), bf16))] * 2,
            [near((both, gh), f32), near(gru_hid.shape[2:]), near((3 * gh, gh))]
            + [near((8, 4 * gh), f32), near((gh, tall)), near((AHEAD, both, 5 * gh)), near((gh, 3 * gh))]
            + [dma((2,)), dma((AHEAD,))],
            name="gru_back",
            token=1,
        )
        sums["hid"] = SumForAll(gone, kept, hid_order[:2])

    def chars_rest():
        pack = embed + vocab // 4
        gone, kept = seq.call(
            lambda *refs: gru_rest(in_order[0], *refs),
            [done["g"], char_table, Far(gru_in[0]), ids, done["bias"], done["sums"], sums_b]
            + [done["q_shift"], done["up_shift"]],
            [Block(((pack // 2, 3 * gh), bf16))] * 2,
            [near(gru_in.shape[2:]), near((pack, 3 * gh)), dma((1,))],
            name="gru_rest",
        )
        sums["in"] = SumForAll(gone, kept, in_order[:2])

    def finish(name):
        item = sums[name]
        left = [Block(item.total)] if isinstance(item, SumByColumn) else [Block(item.kept), Block(item.got)]
        wide = done.setdefault("wide", {})
        shapes = {
            "attend": [(3, chunk, cols), (chunk, cols)],
            "up": [(chunk, units)],
            "down": [(chunk, units)],
            "ud": [(chunk, units)] * 2,
        }[name]
        wide[name] = seq.call(finish_rows, left, [Block((shape, f32)) for shape in shapes], name=name + "_end")

    def conv_out():
        own = sums["conv"].total
        (done["kernel"],) = seq.call(
            finish_kernel, [Block(own), Block(done["conv"])], [Block(((3, 2 * chunk, width), f32))], name="conv_out"
        )

    def hid_out():
        (done["hid"],) = seq.call(
            lambda *refs: unpack_hid(hid_order[0], *refs),
            [Block(a) for a in sums["hid"].quarters],
            [Block(((2, gh, 3 * gh), f32))],
            name="hid_out",
        )

    steps = {
        "feed": feed,
        "attend_back": attend,
        "tokens": tokens_end,
        "gru": chars_back,
        "rest": chars_rest,
        "conv_out": conv_out,
        "hid_out": hid_out,
    }
    ended = set()

    def ready(name):
        return {"conv_out": "conv", "hid_out": "hid"}.get(name, name) in ended if name.endswith("_out") else name not in ended

    def advance(name):
        if name in steps:
            ended.add(name)
            return steps[name]()
        item = sums[name]
        if item.halving():
            return halve(seq, [item], f"{name}_{item.stage}")
        if isinstance(item, SumForAll):
            if item.next(seq, name):
                ended.add(name)
        elif (name == "conv" or isinstance(item, SumByColumn)) and not hasattr(item, "total"):
            item.close(seq, name + "_sum")
            if name == "conv":
                done["conv"] = swap(item.total)
                ended.add(name)
        else:
            finish(name)
            ended.add(name)

    for name in PLAN:
        if ready(name):
            advance(name)
    while True:
        left = [n for n in sums if n not in ended]
        if not left:
            break
        for n in left:
            advance(n)
    for name in ("conv_out", "hid_out"):
        if name not in ended:
            advance(name)
    in_out, table_out, res_out, gain_out, offset_out, bias_out, q_out, up_out = seq.call(
        lambda *refs: unpack(in_order[0], *refs),
        [Block(a) for a in sums["in"].quarters],
        [Block(((2, embed, 3 * gh), f32)), Block(((vocab, embed), f32))]
        + [Block(((3, 1, width), f32))] * 3
        + [Block(((2, 2, 3 * gh), f32)), Block(((2, cols), f32)), Block(((1, units), f32))],
        name="unpack",
    )
    hid_grad = done["hid"]
    qkv_grad, out_grad = done["wide"]["attend"]
    up_grad, down_grad = done["wide"]["ud"] if "ud" in sums else done["wide"]["up"] + done["wide"]["down"]
    return (
        result,
        done["tokens"],
        qkv_grad.swapaxes(0, 1)[None],
        q_out[None],
        out_grad.T[None],
        up_grad[None],
        up_out,
        down_grad.T[None],
        res_out.swapaxes(0, 1),
        gain_out.swapaxes(0, 1),
        offset_out.swapaxes(0, 1),
        table_out,
        in_out[None],
        hid_grad[None],
        bias_out[None],
        done["kernel"][None],
    )


def solution(mesh):
    return jax.shard_map(
        per_device,
        mesh=mesh,
        in_specs=(
            P(("dp", "mp"), None),
            P(("dp", "mp"), None),
            P(("dp", "mp"), None),
            P(("dp", "mp")),
            P(None, None, None, "mp"),
            P(None, None, "mp"),
            P(None, "mp", None),
            P(None, None, "mp"),
            P(None, "mp"),
            P(None, "mp", None),
            P(),
            P(),
            P(),
            P(),
            P(),
            P(),
            P(),
            P(),
        ),
        out_specs=(
            P(("dp", "mp"), None),
            P(("dp", "mp"), None),
            P(None, "dp", None, "mp"),
            P(None, None, "mp"),
            P(None, "mp", "dp"),
            P(None, "dp", "mp"),
            P(None, "mp"),
            P(None, "mp", "dp"),
            P(),
            P(),
            P(),
            P(),
            P(),
            P(),
            P(),
            P(None, None, "dp", None),
        ),
        check_vma=False,
    )
```

```python
import jax
import jax.numpy as jnp
from jax import lax
from jax.experimental import pallas as pl
from jax.experimental.pallas import tpu as pltpu
from jax.sharding import PartitionSpec as P

HD = 64
EPSILON = 1e-05
bf16 = jnp.bfloat16
f32 = jnp.float32


def dot(left, right):
    return jnp.dot(left, right, preferred_element_type=f32)


def dot_t(left, right):
    return lax.dot_general(left, right, (((0,), (0,)), ((), ())), preferred_element_type=f32)


def dot_r(left, right):
    return lax.dot_general(left, right, (((1,), (1,)), ((), ())), preferred_element_type=f32)


def sigmoid(x):
    return 0.5 * jnp.tanh(0.5 * x) + 0.5


class Far:
    def __init__(self, value):
        self.value = value


class Block:
    def __init__(self, value):
        self.value = value


class Side:
    def __init__(self, value, bit, stays):
        self.value, self.bit, self.stays = value, bit, stays


class Sequence:
    def __init__(self, place):
        self.place = place
        self.before = []

    def tie(self, value):
        return lax.optimization_barrier((value, *self.before))[0]

    def after(self, value):
        self.before.append(value)
        return value

    def call(self, kernel, ins, outs, scratch=(), limit=24, name="step", token=0):
        once = dict(pipeline_mode=pl.Buffered(1))
        whole = lambda n: lambda i, p: (0,) * n
        operands, specs = [], []
        for item in ins:
            if isinstance(item, Far):
                operands.append(item.value)
                specs.append(pl.BlockSpec(memory_space=pltpu.HBM))
            elif isinstance(item, Side):
                shape = item.value.shape

                def index(i, p, item=item):
                    mine = (p[0] >> item.bit) & 1
                    return (0, mine if item.stays else 1 - mine, 0, 0)

                operands.append(item.value)
                specs.append(pl.BlockSpec((shape[0], 1) + shape[2:], index, **once))
            elif isinstance(item, Block):
                operands.append(item.value)
                specs.append(pl.BlockSpec(item.value.shape, whole(item.value.ndim), **once))
            else:
                operands.append(item)
                specs.append(pl.BlockSpec(memory_space=pltpu.VMEM))
        out_specs, out_shape = [], []
        for item in outs:
            shape, dtype = item.value if isinstance(item, (Far, Block)) else item
            out_shape.append(jax.ShapeDtypeStruct(shape, dtype))
            if isinstance(item, Far):
                out_specs.append(pl.BlockSpec(memory_space=pltpu.HBM))
            elif isinstance(item, Block):
                out_specs.append(pl.BlockSpec(shape, whole(len(shape)), **once))
            else:
                out_specs.append(pl.BlockSpec(memory_space=pltpu.VMEM))
        count = len(ins)
        held = len(self.before)
        operands += self.before
        specs += [pl.BlockSpec(memory_space=pl.ANY)] * held

        def body(place, *refs):
            kernel(place, *refs[:count], *refs[count + held :])

        out = pl.pallas_call(
            body,
            grid_spec=pltpu.PrefetchScalarGridSpec(
                num_scalar_prefetch=1, grid=(1,), in_specs=specs, out_specs=out_specs, scratch_shapes=list(scratch)
            ),
            out_shape=out_shape,
            compiler_params=pltpu.CompilerParams(vmem_limit_bytes=limit << 20),
            cost_estimate=pl.CostEstimate(flops=1 << 20, bytes_accessed=1 << 10, transcendentals=0),
            name=name,
        )(self.place, *operands)
        self.before = [out[token]]
        return out


def fetch(pairs, sem):
    copies = [pltpu.make_async_copy(far, near, sem.at[i]) for i, (far, near) in enumerate(pairs)]
    for copy in copies:
        copy.start()
    return lambda i: copies[i].wait()


RING = 4


def gru_fwd(place, emb_far, lens_row, win_far, whid_far, bias, c_ref, co_far, hpt_far, *rest):
    emb, win, whid, co, hpt, h_ref, wsem, sems = rest
    slots, rows, _ = emb.shape
    gh = h_ref.shape[1]
    core = place[1]
    wait = fetch([(win_far.at[core], win), (whid_far.at[core], whid), (emb_far, emb)], wsem)
    h_ref[...] = jnp.zeros_like(h_ref)
    shift = bias[core].astype(f32)
    lens = lens_row[...].astype(f32).T
    for i in range(3):
        wait(i)

    def slot_of(s):
        return jnp.where(core == 0, s, slots - 1 - s)

    def out_copies(s):
        row = pl.multiple_of(s * rows, rows)
        at = pl.multiple_of(slot_of(s) * rows, rows)
        i = s % RING
        return (
            pltpu.make_async_copy(co.at[i], co_far.at[pl.ds(row, rows)], sems.at[0, i]),
            pltpu.make_async_copy(hpt.at[i], hpt_far.at[:, pl.ds(at, rows)], sems.at[1, i]),
        )

    def step(s, carry):
        @pl.when(s >= RING)
        def _():
            for copy in out_copies(s - RING):
                copy.wait()

        i = s % RING
        h = h_ref[...]
        hpt[i] = h.T.astype(bf16)
        mask = (slot_of(s).astype(f32) < lens).astype(f32)
        g = dot(emb[slot_of(s)], win[...]) + shift[0:1]
        y = dot(h.astype(bf16), whid[...]) + shift[1:2]
        r = sigmoid(g[:, :gh] + y[:, :gh])
        z = sigmoid(g[:, gh : 2 * gh] + y[:, gh : 2 * gh])
        yn = y[:, 2 * gh :]
        fresh = jnp.tanh(g[:, 2 * gh :] + r * yn)
        keep = mask * (1.0 - z)
        moved = keep * (h - fresh)
        h_ref[...] = h - moved
        an = keep * (1.0 - fresh * fresh)
        ay = an * r
        ar = ay * yn * (1.0 - r)
        for k, value in enumerate((ay, ar, moved * z, an, keep)):
            co[i, :, k * gh : (k + 1) * gh] = value.astype(bf16)
        for copy in out_copies(s):
            copy.start()
        return carry

    lax.fori_loop(0, slots, step, 0)
    c_ref[...] = h_ref[...].astype(bf16)
    for s in range(max(slots - RING, 0), slots):
        for copy in out_copies(s):
            copy.wait()


AHEAD = 4
SMALL = 9


def split_pack(pack, place, bit, gone_ref, kept_ref):
    half = pack.shape[0] // 2
    mine = (place[0] >> bit) & 1
    gone_ref[...] = pack[pl.ds(pl.multiple_of((1 - mine) * half, 16), half), :]
    kept_ref[...] = pack[pl.ds(pl.multiple_of(mine * half, 16), half), :]


def gru_back(bit, place, dc, whid_far, co_far, hpt_far, g_ref, bias_ref, gone_ref, kept_ref, *rest):
    dh_ref, whid, wht, acc, hpt, co, pack, sem, csem = rest
    rows, gh = dh_ref.shape
    slots = g_ref.shape[0] // rows
    core = place[1]
    wait = fetch([(whid_far.at[core], whid), (hpt_far, hpt)], sem)

    def co_copy(i):
        row = pl.multiple_of((slots - 1 - i) * rows, rows)
        return pltpu.make_async_copy(co_far.at[pl.ds(row, rows)], co.at[i % AHEAD], csem.at[i % AHEAD])

    for i in range(AHEAD - 1):
        co_copy(i).start()
    dh_ref[...] = dc[...]
    acc[...] = jnp.zeros_like(acc)
    wait(0)
    wht[...] = whid[...].T

    def step(i, carry):
        co_copy(i).wait()

        @pl.when(i + AHEAD - 1 < slots)
        def _():
            co_copy(i + AHEAD - 1).start()

        s = slots - 1 - i
        slot = jnp.where(core == 0, s, slots - 1 - s)
        row = pl.multiple_of(slot * rows, rows)
        dh = dh_ref[...]
        held = co.at[i % AHEAD]
        low = []
        for k in range(4):
            part = dh * held[:, k * gh : (k + 1) * gh].astype(f32)
            acc[:, k * gh : (k + 1) * gh] += part.reshape(-1, 8, gh).sum(0)
            low.append(part.astype(bf16))
            g_ref[pl.ds(row, rows), k * gh : (k + 1) * gh] = low[k]
        dy = jnp.concatenate([low[1], low[2], low[0]], 1)
        dh_ref[...] = dh - dh * held[:, 4 * gh :].astype(f32) + dot(dy, wht[...])
        return carry

    lax.fori_loop(0, slots, step, 0)
    wait(1)
    d_hid = dot(hpt[...], g_ref[:, : 3 * gh]).astype(bf16)
    pack[:, 2 * gh :] = d_hid[:, :gh]
    pack[:, : 2 * gh] = d_hid[:, gh:]
    split_pack(pack, place, bit, gone_ref, kept_ref)
    b = acc[...].sum(0, keepdims=True)
    bias_ref[...] = jnp.concatenate([b[:, gh:], b[:, gh : 3 * gh], b[:, :gh]], 1)


def gru_rest(bit, place, g, table, win_far, ids, b, sums_a, sums_b, q_shift, up_shift, *rest):
    gone_ref, kept_ref, win, pack, sem = rest
    embed, gates = win.shape
    vocab = table.shape[0]
    at = g.shape[1] - gates
    core = place[1]
    wait = fetch([(win_far.at[core], win)], sem)
    chosen = (lax.broadcasted_iota(jnp.int32, (vocab, ids.shape[1]), 0) == ids[...]).astype(bf16)
    by_char = dot(chosen, g[:, at:]).astype(bf16)
    pack[:embed] = dot_t(table[...], by_char).astype(bf16)
    wait(0)
    table = dot_r(by_char, win[...]).astype(bf16)
    long = vocab // 4
    for k in range(4):
        pack[embed:, k * embed : (k + 1) * embed] = table[k * long : (k + 1) * long]
    flat = [sums_a[0:1], sums_b[0:1], sums_b[1:2], sums_a[1:2], sums_b[2:3], sums_b[3:4], sums_a[2:3], sums_b[4:5], sums_b[5:6]]
    flat += [b[...], q_shift[0:1], q_shift[1:2], up_shift[...]]
    lanes = jnp.concatenate(flat, 1)
    count = lanes.shape[1] // 128
    tall = [lanes[:, k * 128 : (k + 1) * 128] for k in range(count)]
    tall += [jnp.zeros((1, 128), f32)] * (long - count)
    pack[embed:, 4 * embed :] = jnp.concatenate(tall, 0).astype(bf16)
    split_pack(pack, place, bit, gone_ref, kept_ref)


def rows_in_order(place, bit, own, got):
    low = ((place[0] >> bit) & 1) == 0
    own, got = own[...].astype(f32), got[...].astype(f32)
    return jnp.where(low, own, got), jnp.where(low, got, own)


def unpack_hid(bit, place, own, got, own_other, got_other, out):
    half = own.shape[0]
    for pair, d in (((own, got), place[1]), ((own_other, got_other), 1 - place[1])):
        first, second = rows_in_order(place, bit, *pair)
        out[d, :half] = first
        out[d, half:] = second


def unpack(bit, place, own, got, own_other, got_other, in_ref, table_ref, res_ref, gain_ref, off_ref, bias_ref, q_ref, up_ref):
    core = place[1]
    embed = in_ref.shape[1]
    gates = in_ref.shape[2]
    long = table_ref.shape[0] // 4
    half = own.shape[0]
    tails = []
    for pair, d in (((own, got), core), ((own_other, got_other), 1 - core)):
        first, second = rows_in_order(place, bit, *pair)
        in_ref[d, :half] = first
        in_ref[d, half:] = second[: embed - half]
        tails.append(second[embed - half :])
    mine, other = tails
    both = mine + other
    for k in range(4):
        table_ref[k * long : (k + 1) * long] = both[:, k * embed : (k + 1) * embed]
    line = lambda value, at, count: jnp.concatenate(
        [value[k : k + 1, 4 * embed :] for k in range(at // 128, (at + count) // 128)], 1
    )
    width = res_ref.shape[2]
    for k, ref in enumerate((res_ref, gain_ref, off_ref)):
        for i in range(3):
            ref[i] = line(both, (3 * k + i) * width, width)
    at = SMALL * width
    for value, d in ((mine, core), (other, 1 - core)):
        for i in range(2):
            bias_ref[d, pl.ds(i, 1)] = line(value, at + gates * i, gates)
    at += 2 * gates
    cols = q_ref.shape[1]
    for i in range(2):
        q_ref[i : i + 1] = line(mine, at + i * cols, cols)
    up_ref[...] = line(mine, at + 2 * cols, up_ref.shape[1])


GELU_A = 0.7978845608028654
GELU_B = 0.044715


def norm_stats(total):
    centre = jnp.mean(total, -1, keepdims=True)
    centred = total - centre
    scale = lax.rsqrt(jnp.mean(centred * centred, -1, keepdims=True) + EPSILON)
    return centred * scale, scale


def norm_back(grad, hat, scale, gain):
    scaled = grad * gain
    inner = jnp.mean(scaled, -1, keepdims=True)
    along = jnp.mean(scaled * hat, -1, keepdims=True)
    return (scaled - inner - hat * along) * scale


def gelu_pair(u):
    square = u * u
    t = jnp.tanh(GELU_A * (u + GELU_B * u * square))
    half = 0.5 * (1.0 + t)
    slope = half + 0.5 * u * (1.0 - t * t) * (GELU_A + 3.0 * GELU_A * GELU_B * square)
    return u * half, slope


def turned(values):
    rows = values.shape[0] // 2
    return jnp.concatenate([values[rows:], values[:rows]], 0)


def own_sum(values):
    return jnp.sum(values[: values.shape[0] // 2], 0, keepdims=True)


def pair_of(left, right):
    return jnp.concatenate([left, right], 0)


class Halves:
    def __init__(self, length, bit):
        self.count = lax.axis_size("dp")
        self.length, self.bit = length, bit
        self.chunk = length // self.count
        self.direct = self.chunk % 16 == 0

    def operands(self):
        if self.direct:
            return []
        mine = (lax.axis_index("dp") >> self.bit) & 1
        where = jnp.arange(self.length, dtype=jnp.int32)
        kept = where.reshape(self.count >> (self.bit + 1), 2, -1)
        pick = lambda side: jax.nn.one_hot(
            lax.dynamic_index_in_dim(kept, side, 1, keepdims=False).reshape(-1), self.length, dtype=bf16
        )
        return [pick(1 - mine), pick(mine)]

    def scratch(self, rows):
        return [pltpu.VMEM((self.length, rows), bf16)]

    def sides(self, values, turned_ref, place, picks):
        if not self.direct:
            return [dot_r(pick[...], values).astype(bf16) for pick in picks]
        turned_ref[...] = values.T
        mine = (place[0] >> self.bit) & 1
        out = []
        for side in (1 - mine, mine):
            parts = []
            for k in range(self.count):
                if not (k >> self.bit) & 1:
                    start = pl.multiple_of((k + (side << self.bit)) * self.chunk, 16)
                    parts.append(turned_ref[pl.ds(start, self.chunk), :])
            out.append(jnp.concatenate(parts, 0))
        return out


def attend_fwd(place, mine, other, wqkv_far, bqkv, wout_far, vec, *rest):
    q_ref, k_ref, v_ref, p_ref, m_ref, base_ref, send_ref, wqkv, wout, sem = rest
    wait = fetch([(wqkv_far, wqkv), (wout_far, wout)], sem)
    x = pair_of(mine[...], other[...])
    bias = bqkv[...].astype(f32)
    wait(0)
    q = (dot(x, wqkv[0]) + bias[0:1]).astype(bf16)
    k = dot(x, wqkv[1]).astype(bf16)
    v = (dot(x, wqkv[2]) + bias[1:2]).astype(bf16)
    q_ref[...], k_ref[...], v_ref[...] = q, k, v
    mixed = []
    for h in range(p_ref.shape[0]):
        at = slice(h * HD, (h + 1) * HD)
        s = dot_r(q[:, at], k[:, at]) * HD**-0.5
        e = jnp.exp(s - jnp.max(s, -1, keepdims=True))
        p = (e / jnp.sum(e, -1, keepdims=True)).astype(bf16)
        p_ref[h] = p
        mixed.append(dot(p, v[:, at]).astype(bf16))
    mixed = jnp.concatenate(mixed, 1)
    m_ref[...] = mixed
    wait(1)
    part = dot(mixed, wout[...])
    send_ref[...] = part.astype(bf16)
    base_ref[...] = x.astype(f32) + part + vec[0:1]


def feed_fwd(place, base, got, wup_far, bup, wdown_far, vec, *rest):
    hat_ref, scale_ref, act_ref, slope_ref, out_ref, send_ref, wup, wdown, sem = rest
    wait = fetch([(wup_far, wup), (wdown_far, wdown)], sem)
    hat, scale = norm_stats(base[...] + turned(got[...]).astype(f32))
    hat_ref[...], scale_ref[...] = hat, scale
    h1 = hat * vec[3:4] + vec[6:7]
    wait(0)
    act, slope = gelu_pair(dot(h1.astype(bf16), wup[...]) + bup[...].astype(f32))
    act = act.astype(bf16)
    act_ref[...] = act
    slope_ref[...] = slope.astype(bf16)
    wait(1)
    part = dot(act, wdown[...])
    send_ref[...] = part.astype(bf16)
    out_ref[...] = h1 + part + vec[1:2]


def unite(halves, place, base, got, cm, co, conv_far, tm, to, vec, *rest):
    picks, rest = rest[: 0 if halves.direct else 2], rest[0 if halves.direct else 2 :]
    res_ref, dc_ref, dr_ref, sums_ref, gone_ref, kept_ref, turned_ref, cat_ref, conv, sem = rest
    core = place[1]
    wait = fetch([(conv_far.at[i], conv.at[i]) for i in range(3)], sem)
    hat2, scale2 = norm_stats(base[...] + turned(got[...]).astype(f32))
    h2 = hat2 * vec[4:5] + vec[7:8]
    first = core == 0
    own, theirs = cm[...], turned(co[...])
    chars = [jnp.where(first, own, theirs), jnp.where(first, theirs, own)]
    joined = jnp.concatenate([h2.astype(bf16)] + chars, 1)
    rows = joined.shape[0]
    width = h2.shape[1]
    spot = lax.broadcasted_iota(jnp.int32, (rows, 1), 0)
    half = rows // 2
    not_first = (spot != core * half).astype(f32)
    not_last = (spot != (rows - 1 + core * half) % rows).astype(f32)
    later = lambda a: pltpu.roll(a, 1, 0) * not_first
    sooner = lambda a: pltpu.roll(a, rows - 1, 0) * not_last
    raw = vec[2:3]
    for i, move in enumerate((later, lambda a: a, sooner)):
        wait(i)
        raw = raw + move(dot(joined, conv[i]))
    act, slope = gelu_pair(raw)
    hat3, scale3 = norm_stats(h2 + act)
    res_ref[...] = (hat3 * vec[5:6] + vec[8:9])[:half].astype(bf16)
    cot = pair_of(tm[...], to[...]).astype(f32)
    d_r3 = norm_back(cot, hat3, scale3, vec[5:6])
    d_f = (d_r3 * slope).astype(bf16).astype(f32)
    d_fs = [sooner(d_f).astype(bf16), d_f.astype(bf16), later(d_f).astype(bf16)]
    gh = width // 2
    mine = pl.ds(pl.multiple_of(width + core * gh, 128), gh)
    d_h2 = d_r3 + sum(dot_r(d_fs[i], conv[i, :width]) for i in range(3))
    dc_ref[...] = sum(dot_r(d_fs[i], conv[i, mine]) for i in range(3))
    d_r2 = norm_back(d_h2, hat2, scale2, vec[4:5])
    dr_ref[...] = d_r2
    sums = [own_sum(d_r2), own_sum(d_f), own_sum(d_h2 * hat2), own_sum(cot * hat3), own_sum(d_h2), own_sum(cot)]
    for i, value in enumerate(sums):
        sums_ref[i : i + 1] = value
    span = width // 2
    gone, kept = halves.sides(joined, turned_ref, place, picks)
    for i in range(3):
        cat_ref[i] = d_fs[i]
        part = cat_ref[i, :, pl.ds(pl.multiple_of(core * span, 128), span)]
        gone_ref[:, i * span : (i + 1) * span] = dot(gone, part).astype(bf16)
        kept_ref[:, i * span : (i + 1) * span] = dot(kept, part).astype(bf16)


def feed_back(halves, place, dr, act, slope, hat, wup_far, wdown_far, vec, *rest):
    picks, rest = rest[: 0 if halves[0].direct else 4], rest[0 if halves[0].direct else 4 :]
    base_ref, send_ref, sum_ref = rest[:3]
    turned_ref, wup, wdown, sem = rest[-4:]
    wait = fetch([(wdown_far, wdown), (wup_far, wup)], sem)
    low = dr[...].astype(bf16)
    wait(0)
    d_u = (dot_r(low, wdown[...]) * slope[...].astype(f32)).astype(bf16)
    sum_ref[...] = jnp.sum(d_u.astype(f32), 0, keepdims=True)
    wait(1)
    part = dot_r(d_u, wup[...])
    send_ref[...] = part.astype(bf16)
    base_ref[...] = dr[...] + part
    h1 = (hat[...] * vec[3:4] + vec[6:7]).astype(bf16)
    units = d_u.shape[1]
    if TOGETHER:
        gone_up = gone_down = rest[3]
        kept_up = kept_down = rest[4]
    else:
        gone_up, kept_up, gone_down, kept_down = rest[3:7]
    for i, (left, right, gone_ref, kept_ref) in enumerate(
        ((h1, d_u, gone_up, kept_up), (low, act[...], gone_down, kept_down))
    ):
        at = slice(i * units, (i + 1) * units) if TOGETHER else slice(None)
        gone, kept = halves[i].sides(left, turned_ref, place, picks[2 * i : 2 * i + 2])
        gone_ref[:, at] = dot(gone, right).astype(bf16)
        kept_ref[:, at] = dot(kept, right).astype(bf16)


def attend_back(halves, place, base, got, hat, scale, q, k, v, p, mixed, mine, other, wqkv_far, wout_far, vec, *rest):
    picks, rest = rest[: 0 if halves.direct else 2], rest[0 if halves.direct else 2 :]
    base_ref, send_ref, sums_ref, shift_ref, gone_ref, kept_ref, turned_ref, wqkv, wout, sem = rest
    wait = fetch([(wout_far, wout), (wqkv_far, wqkv)], sem)
    d_h1 = base[...] + turned(got[...]).astype(f32)
    d_r1 = norm_back(d_h1, hat[...], scale[...], vec[3:4])
    for i, value in enumerate((own_sum(d_r1), own_sum(d_h1 * hat[...]), own_sum(d_h1))):
        sums_ref[i : i + 1] = value
    low = d_r1.astype(bf16)
    wait(0)
    d_mixed = dot_r(low, wout[...]).astype(bf16)
    d_q, d_k, d_v = [], [], []
    for h in range(p.shape[0]):
        at = slice(h * HD, (h + 1) * HD)
        prob = p[h].astype(f32)
        d_p = dot_r(d_mixed[:, at], v[:, at])
        d_v.append(dot_t(p[h], d_mixed[:, at]).astype(bf16))
        d_s = (prob * (d_p - jnp.sum(prob * d_p, -1, keepdims=True))).astype(bf16)
        d_q.append((dot(d_s, k[:, at]) * HD**-0.5).astype(bf16))
        d_k.append((dot_t(d_s, q[:, at]) * HD**-0.5).astype(bf16))
    d_proj = [jnp.concatenate(a, 1) for a in (d_q, d_k, d_v)]
    shift_ref[0:1] = jnp.sum(d_proj[0].astype(f32), 0, keepdims=True)
    shift_ref[1:2] = jnp.sum(d_proj[2].astype(f32), 0, keepdims=True)
    wait(1)
    part = sum(dot_r(d_proj[i], wqkv[i]) for i in range(3))
    rows = part.shape[0] // 2
    base_ref[...] = d_r1[:rows] + part[:rows]
    send_ref[...] = part[rows:].astype(bf16)
    span = d_mixed.shape[1]
    x = pair_of(mine[...], other[...])
    gone, kept = halves.sides(x, turned_ref, place, picks)
    for i in range(3):
        gone_ref[:, i * span : (i + 1) * span] = dot(gone, d_proj[i]).astype(bf16)
        kept_ref[:, i * span : (i + 1) * span] = dot(kept, d_proj[i]).astype(bf16)
    gone, kept = halves.sides(low, turned_ref, place, picks)
    gone_ref[:, 3 * span :] = dot(gone, mixed[...]).astype(bf16)
    kept_ref[:, 3 * span :] = dot(kept, mixed[...]).astype(bf16)


def swap(values):
    return lax.ppermute(values, "mp", [(0, 1), (1, 0)])


def flip(values, bit):
    count = lax.axis_size("dp")
    return lax.ppermute(values, "dp", [(i, i ^ (1 << bit)) for i in range(count)])


def added(left, right):
    return left.astype(f32) + right.astype(f32)


def high_groups():
    count = lax.axis_size("dp")
    return [[low + high for high in range(0, count, 4)] for low in range(4)]


class Sum:
    def __init__(self, gone, kept, order):
        self.order = order
        self.stage = 0
        self.kept = kept
        self.rows = kept.shape[0] * 2 // lax.axis_size("dp")
        self.got = flip(gone, order[0])

    def view(self):
        bits = range(lax.axis_size("dp").bit_length() - 1)
        left = [bit for bit in bits[::-1] if bit not in self.order[: self.stage + 1]]
        axis = left.index(self.order[self.stage + 1])
        return 1 << axis, self.rows << (len(left) - 1 - axis)

    def halving(self):
        return self.stage < len(self.order) - 1

    def add(self, seq, name):
        def kernel(place, kept, got, out):
            out[...] = added(kept[...], got[...]).astype(bf16)

        (out,) = seq.call(
            kernel, [Block(self.kept), Block(self.got)], [Block((self.kept.shape, bf16))], limit=16, name=name
        )
        return out


    def close(self, seq, name):
        self.total = self.add(seq, name)


class SumByColumn(Sum):
    def close(self, seq, name):
        total = self.add(seq, name)
        self.total = lax.psum_scatter(
            total, "dp", scatter_dimension=0, axis_index_groups=high_groups(), tiled=True
        )


class SumForAll(Sum):
    def __init__(self, gone, kept, order):
        super().__init__(gone, kept, order)
        self.left = list(range(2, lax.axis_size("dp").bit_length() - 1))

    def view(self):
        return 1, self.kept.shape[0] // 2

    def next(self, seq, name):
        if hasattr(self, "block"):
            return self.last(seq, name)
        if self.left is not None:
            self.kept = self.add(seq, f"{name}_sum_{len(self.left)}")
            if self.left:
                self.got = flip(self.kept, self.left.pop(0))
            else:
                self.left = None
                self.got = flip(self.kept, self.order[1])
            return False
        bit = self.order[1]

        def kernel(place, own, other, out):
            mine = (place[0] >> bit) & 1
            out[mine] = own[...]
            out[1 - mine] = other[...]

        shape = self.kept.shape
        (out,) = seq.call(
            kernel, [Block(self.kept), Block(self.got)], [Block(((2,) + shape, bf16))], limit=16, name=name + "_join"
        )
        self.block = out.reshape(2 * shape[0], shape[1])
        self.got = flip(self.block, self.order[0])
        self.other = swap(self.block)
        return False

    def last(self, seq, name):
        def kernel(place, got, out):
            out[...] = got[...]

        (got,) = seq.call(kernel, [Block(self.got)], [Block((self.got.shape, bf16))], limit=8, name=name + "_pass")
        self.quarters = [self.block, got, self.other, swap(got)]
        return True


def halve(seq, sums, name):
    ins, outs = [], []
    for item in sums:
        outer, rows = item.view()
        cols = item.kept.shape[-1]
        bit = item.order[item.stage + 1]
        for stays in (False, True):
            for value in (item.kept, item.got):
                ins.append(Side(value.reshape(outer, 2, rows, cols), bit, stays))
        outs += [Block(((outer * rows, cols), bf16))] * 2

    def kernel(place, *refs):
        for i in range(len(sums)):
            for j in range(2):
                left, right = refs[4 * i + 2 * j : 4 * i + 2 * j + 2]
                out = refs[4 * len(sums) + 2 * i + j]
                out[...] = added(left[:, 0], right[:, 0]).astype(bf16).reshape(out.shape)

    out = seq.call(kernel, ins, outs, limit=12, name=name, token=1)
    for i, item in enumerate(sums):
        item.stage += 1
        item.got = flip(out[2 * i], item.order[item.stage])
        item.kept = out[2 * i + 1]


def finish_rows(place, *refs):
    count = 2 if refs[0].shape == refs[1].shape and refs[0].dtype == refs[1].dtype else 1
    total = added(refs[0][...], refs[1][...]) if count == 2 else refs[0][...].astype(f32)
    at = 0
    for out in refs[count:]:
        parts = [out] if len(out.shape) == 2 else [out.at[i] for i in range(out.shape[0])]
        for part in parts:
            part[...] = total[:, at : at + part.shape[1]].astype(part.dtype)
            at += part.shape[1]


def finish_kernel(place, own, got, out):
    span = own.shape[1] // 3
    first = place[1] == 0
    for i in range(3):
        at = slice(i * span, (i + 1) * span)
        mine, other = own[:, at].astype(f32), got[:, at].astype(f32)
        out[i, :, :span] = jnp.where(first, mine, other)
        out[i, :, span:] = jnp.where(first, other, mine)


ORDERS = (
    (1, 0, 2, 3),
    (2, 0, 1, 3),
    (0, 1, 2, 3),
    (2, 0, 1, 3),
    (0, 1),
    (0, 1),
)
PLAN = (
    "feed", "gru", "attend_back", "rest", "up", "hid", "conv", "down",
    "in", "hid", "in", "hid", "in", "attend", "hid", "conv",
    "tokens", "up", "down", "in", "hid", "in", "conv", "attend",
    "up", "down", "hid", "conv", "attend", "in", "up", "conv_out",
    "hid_out", "attend", "down",
)
BY_COLUMN = ()
TOGETHER = False


def per_device(
    tokens,
    cotangent,
    char_ids,
    char_lens,
    w_qkv,
    b_qkv,
    w_out,
    w_up,
    up_bias,
    w_down,
    res_bias,
    norm_gain,
    norm_bias,
    char_table,
    gru_in,
    gru_hid,
    gru_bias,
    conv_w,
):
    core = lax.axis_index("mp")
    seq = Sequence(jnp.stack([lax.axis_index("dp"), core]).astype(jnp.int32))
    rows, width = tokens.shape
    both = 2 * rows
    slots = char_ids.shape[1]
    vocab, embed = char_table.shape
    gh = gru_hid.shape[2]
    count = lax.axis_size("dp")
    bits = list(range(count.bit_length() - 1))
    first = lambda *lead: list(lead) + [b for b in bits if b not in lead]
    wqkv = w_qkv[0].swapaxes(0, 1)
    cols = wqkv.shape[2]
    wout, wup, wdown, conv = w_out[0], w_up[0], w_down[0], conv_w[0]
    units = wup.shape[1]
    vec = jnp.concatenate([res_bias[0], norm_gain[0], norm_bias[0]], 0).astype(f32)
    heads = cols // HD
    dma = pltpu.SemaphoreType.DMA
    near = lambda a, dtype=bf16: pltpu.VMEM(a, dtype)

    letters = jnp.concatenate([char_ids.T, char_lens[None]], 0)
    letters_other = swap(letters)
    tokens_other = swap(tokens)
    cot_other = swap(cotangent)
    letters = jnp.concatenate([letters, letters_other], 1)
    tall = slots * both
    ids = letters[:slots].reshape(1, tall)
    one_hot = (ids.reshape(-1, 1) == jnp.arange(vocab, dtype=jnp.int32)[None, :]).astype(bf16)
    emb = seq.after(dot(one_hot, char_table).astype(bf16))

    seq.after(cot_other)

    q, k, v, p, mixed, base, send = seq.call(
        attend_fwd,
        [tokens, tokens_other, Far(wqkv), b_qkv[0], Far(wout), vec],
        [((both, cols), bf16)] * 3
        + [((heads, both, both), bf16), ((both, cols), bf16), ((both, width), f32), ((both, width), bf16)],
        [near(wqkv.shape), near(wout.shape), dma((2,))],
        name="attend_fwd",
        token=6,
        limit=14,
    )
    got = swap(send)
    chars, co, hpt = seq.call(
        gru_fwd,
        [Far(emb.reshape(slots, both, embed)), letters[slots:], Far(gru_in[0]), Far(gru_hid[0]), gru_bias[0]],
        [((both, gh), bf16), Far(((3 * tall, 5 * gh), bf16)), Far(((gh, tall), bf16))],
        [near((slots, both, embed)), near(gru_in.shape[2:]), near(gru_hid.shape[2:]), near((RING, both, 5 * gh))]
        + [near((RING, gh, both)), near((both, gh), f32), dma((3,)), dma((2, RING))],
        limit=16,
        name="gru_fwd",
    )
    chars_other = swap(chars)
    hat1, scale1, act, slope, base, send = seq.call(
        feed_fwd,
        [base, got, Far(wup), up_bias, Far(wdown), vec],
        [((both, width), f32), ((both, 1), f32), ((both, units), bf16), ((both, units), bf16)]
        + [((both, width), f32), ((both, width), bf16)],
        [near(wup.shape), near(wdown.shape), dma((2,))],
        name="feed_fwd",
        token=5,
        limit=14,
    )
    orders = [first(*order) for order in ORDERS]
    conv_order, up_order, down_order, attend_order, hid_order, in_order = orders
    halves = Halves(2 * width, conv_order[0])
    span = 3 * width // 2
    result, d_chars, d_r2, sums_b, gone, kept = seq.call(
        lambda *refs: unite(halves, *refs),
        [base, swap(send), chars, chars_other, Far(conv), cotangent, cot_other, vec, *halves.operands()],
        [Block(((rows, width), bf16)), ((both, gh), f32), ((both, width), f32), ((6, width), f32)]
        + [Block(((width, span), bf16))] * 2,
        halves.scratch(both) + [near((3, both, width)), near(conv.shape), dma((3,))],
        limit=26,
        name="unite",
        token=3,
    )
    def summed(name, gone, kept, order):
        sums[name] = SumByColumn(gone, kept, order[:2]) if name in BY_COLUMN else Sum(gone, kept, order)

    sums = {}
    summed("conv", gone, kept, conv_order)
    done = {}
    chunk = width // count

    def feed():
        halves = (Halves(width, up_order[0]), Halves(width, down_order[0]))
        sizes = [Block(((width // 2, units), bf16))] * 4
        if TOGETHER:
            sizes = [Block(((width // 2, 2 * units), bf16))] * 2
        out = seq.call(
            lambda *refs: feed_back(halves, *refs),
            [d_r2, act, slope, hat1, Far(wup), Far(wdown), vec, *halves[0].operands(), *halves[1].operands()],
            [((both, width), f32), ((both, width), bf16), ((1, units), f32)] + sizes,
            halves[0].scratch(both) + [near(wup.shape), near(wdown.shape), dma((2,))],
            limit=16,
        name="feed_back",
            token=2,
        )
        base, send, done["up_shift"] = out[:3]
        done["feed"] = base, swap(send)
        if TOGETHER:
            summed("ud", *out[3:], up_order)
        else:
            summed("up", *out[3:5], up_order)
            summed("down", *out[5:], down_order)

    def attend():
        halves = Halves(width, attend_order[0])
        base, send, done["sums"], done["q_shift"], gone, kept = seq.call(
            lambda *refs: attend_back(halves, *refs),
            [*done["feed"], hat1, scale1, q, k, v, p, mixed, tokens, tokens_other, Far(wqkv), Far(wout), vec]
            + halves.operands(),
            [((rows, width), f32), ((rows, width), bf16), ((3, width), f32), ((2, cols), f32)]
            + [Block(((width // 2, 4 * cols), bf16))] * 2,
            halves.scratch(both) + [near(wqkv.shape), near(wout.shape), dma((2,))],
            name="attend_back",
            token=2,
            limit=16,
        )
        done["attend"] = base, swap(send)
        summed("attend", gone, kept, attend_order)

    def tokens_end():
        base, got = done["attend"]
        done["tokens"] = seq.after(added(seq.tie(base), got))

    def chars_back():
        done["g"], done["bias"], gone, kept = seq.call(
            lambda *refs: gru_back(hid_order[0], *refs),
            [d_chars, Far(gru_hid[0]), Far(co), Far(hpt)],
            [((tall, 4 * gh), bf16), ((1, 6 * gh), f32)] + [Block(((gh // 2, 3 * gh), bf16))] * 2,
            [near((both, gh), f32), near(gru_hid.shape[2:]), near((3 * gh, gh))]
            + [near((8, 4 * gh), f32), near((gh, tall)), near((AHEAD, both, 5 * gh)), near((gh, 3 * gh))]
            + [dma((2,)), dma((AHEAD,))],
            limit=18,
        name="gru_back",
            token=1,
        )
        sums["hid"] = SumForAll(gone, kept, hid_order[:2])

    def chars_rest():
        pack = embed + vocab // 4
        gone, kept = seq.call(
            lambda *refs: gru_rest(in_order[0], *refs),
            [done["g"], char_table, Far(gru_in[0]), ids, done["bias"], done["sums"], sums_b]
            + [done["q_shift"], done["up_shift"]],
            [Block(((pack // 2, 3 * gh), bf16))] * 2,
            [near(gru_in.shape[2:]), near((pack, 3 * gh)), dma((1,))],
            limit=18,
        name="gru_rest",
        )
        sums["in"] = SumForAll(gone, kept, in_order[:2])

    def finish(name):
        item = sums[name]
        wide = done.setdefault("wide", {})
        if name != "attend":
            total = item.total.astype(f32) if isinstance(item, SumByColumn) else added(seq.tie(item.kept), item.got)
            total = seq.after(total)
            wide[name] = [total[:, i : i + units] for i in range(0, total.shape[1], units)]
            return
        left = [Block(item.total)] if isinstance(item, SumByColumn) else [Block(item.kept), Block(item.got)]
        shapes = [(3, chunk, cols), (chunk, cols)]
        wide[name] = seq.call(finish_rows, left, [Block((shape, f32)) for shape in shapes], name=name + "_end")

    def conv_out():
        own = sums["conv"].total
        (done["kernel"],) = seq.call(
            finish_kernel, [Block(own), Block(done["conv"])], [Block(((3, 2 * chunk, width), f32))], name="conv_out"
        )

    def hid_out():
        (done["hid"],) = seq.call(
            lambda *refs: unpack_hid(hid_order[0], *refs),
            [Block(a) for a in sums["hid"].quarters],
            [Block(((2, gh, 3 * gh), f32))],
            name="hid_out",
        )

    steps = {
        "feed": feed,
        "attend_back": attend,
        "tokens": tokens_end,
        "gru": chars_back,
        "rest": chars_rest,
        "conv_out": conv_out,
        "hid_out": hid_out,
    }
    ended = set()

    def ready(name):
        return {"conv_out": "conv", "hid_out": "hid"}.get(name, name) in ended if name.endswith("_out") else name not in ended

    def advance(name):
        if name in steps:
            ended.add(name)
            return steps[name]()
        item = sums[name]
        if item.halving():
            return halve(seq, [item], f"{name}_{item.stage}")
        if isinstance(item, SumForAll):
            if item.next(seq, name):
                ended.add(name)
        elif (name == "conv" or isinstance(item, SumByColumn)) and not hasattr(item, "total"):
            item.close(seq, name + "_sum")
            if name == "conv":
                done["conv"] = swap(item.total)
                ended.add(name)
        else:
            finish(name)
            ended.add(name)

    for name in PLAN:
        if ready(name):
            advance(name)
    while True:
        left = [n for n in sums if n not in ended]
        if not left:
            break
        for n in left:
            advance(n)
    for name in ("conv_out", "hid_out"):
        if name not in ended:
            advance(name)
    in_out, table_out, res_out, gain_out, offset_out, bias_out, q_out, up_out = seq.call(
        lambda *refs: unpack(in_order[0], *refs),
        [Block(a) for a in sums["in"].quarters],
        [Block(((2, embed, 3 * gh), f32)), Block(((vocab, embed), f32))]
        + [Block(((3, 1, width), f32))] * 3
        + [Block(((2, 2, 3 * gh), f32)), Block(((2, cols), f32)), Block(((1, units), f32))],
        limit=16,
        name="unpack",
    )
    hid_grad = done["hid"]
    qkv_grad, out_grad = done["wide"]["attend"]
    up_grad, down_grad = done["wide"]["ud"] if "ud" in sums else done["wide"]["up"] + done["wide"]["down"]
    return (
        result,
        done["tokens"],
        qkv_grad.swapaxes(0, 1)[None],
        q_out[None],
        out_grad.T[None],
        up_grad[None],
        up_out,
        down_grad.T[None],
        res_out.swapaxes(0, 1),
        gain_out.swapaxes(0, 1),
        offset_out.swapaxes(0, 1),
        table_out,
        in_out[None],
        hid_grad[None],
        bias_out[None],
        done["kernel"][None],
    )


def solution(mesh):
    return jax.shard_map(
        per_device,
        mesh=mesh,
        in_specs=(
            P(("dp", "mp"), None),
            P(("dp", "mp"), None),
            P(("dp", "mp"), None),
            P(("dp", "mp")),
            P(None, None, None, "mp"),
            P(None, None, "mp"),
            P(None, "mp", None),
            P(None, None, "mp"),
            P(None, "mp"),
            P(None, "mp", None),
            P(),
            P(),
            P(),
            P(),
            P(),
            P(),
            P(),
            P(),
        ),
        out_specs=(
            P(("dp", "mp"), None),
            P(("dp", "mp"), None),
            P(None, "dp", None, "mp"),
            P(None, None, "mp"),
            P(None, "mp", "dp"),
            P(None, "dp", "mp"),
            P(None, "mp"),
            P(None, "mp", "dp"),
            P(),
            P(),
            P(),
            P(),
            P(),
            P(),
            P(),
            P(None, None, "dp", None),
        ),
        check_vma=False,
    )
```

```python
import jax
import jax.numpy as jnp
from jax import lax
from jax.experimental import pallas as pl
from jax.experimental.pallas import tpu as pltpu
from jax.sharding import PartitionSpec as P

HD = 64
EPSILON = 1e-05
bf16 = jnp.bfloat16
f32 = jnp.float32


def dot(left, right):
    return jnp.dot(left, right, preferred_element_type=f32)


def dot_t(left, right):
    return lax.dot_general(left, right, (((0,), (0,)), ((), ())), preferred_element_type=f32)


def dot_r(left, right):
    return lax.dot_general(left, right, (((1,), (1,)), ((), ())), preferred_element_type=f32)


def sigmoid(x):
    return 0.5 * jnp.tanh(0.5 * x) + 0.5


class Far:
    def __init__(self, value):
        self.value = value


class Block:
    def __init__(self, value):
        self.value = value


class Side:
    def __init__(self, value, bit, stays):
        self.value, self.bit, self.stays = value, bit, stays


class Sequence:
    def __init__(self, place):
        self.place = place
        self.before = []

    def tie(self, value):
        return lax.optimization_barrier((value, *self.before))[0]

    def after(self, value):
        self.before.append(value)
        return value

    def call(self, kernel, ins, outs, scratch=(), limit=24, name="step", token=0):
        once = dict(pipeline_mode=pl.Buffered(1))
        whole = lambda n: lambda i, p: (0,) * n
        operands, specs = [], []
        for item in ins:
            if isinstance(item, Far):
                operands.append(item.value)
                specs.append(pl.BlockSpec(memory_space=pltpu.HBM))
            elif isinstance(item, Side):
                shape = item.value.shape

                def index(i, p, item=item):
                    mine = (p[0] >> item.bit) & 1
                    return (0, mine if item.stays else 1 - mine, 0, 0)

                operands.append(item.value)
                specs.append(pl.BlockSpec((shape[0], 1) + shape[2:], index, **once))
            elif isinstance(item, Block):
                operands.append(item.value)
                specs.append(pl.BlockSpec(item.value.shape, whole(item.value.ndim), **once))
            else:
                operands.append(item)
                specs.append(pl.BlockSpec(memory_space=pltpu.VMEM))
        out_specs, out_shape = [], []
        for item in outs:
            shape, dtype = item.value if isinstance(item, (Far, Block)) else item
            out_shape.append(jax.ShapeDtypeStruct(shape, dtype))
            if isinstance(item, Far):
                out_specs.append(pl.BlockSpec(memory_space=pltpu.HBM))
            elif isinstance(item, Block):
                out_specs.append(pl.BlockSpec(shape, whole(len(shape)), **once))
            else:
                out_specs.append(pl.BlockSpec(memory_space=pltpu.VMEM))
        count = len(ins)
        held = len(self.before)
        operands += self.before
        specs += [pl.BlockSpec(memory_space=pl.ANY)] * held

        def body(place, *refs):
            kernel(place, *refs[:count], *refs[count + held :])

        out = pl.pallas_call(
            body,
            grid_spec=pltpu.PrefetchScalarGridSpec(
                num_scalar_prefetch=1, grid=(1,), in_specs=specs, out_specs=out_specs, scratch_shapes=list(scratch)
            ),
            out_shape=out_shape,
            compiler_params=pltpu.CompilerParams(vmem_limit_bytes=limit << 20),
            cost_estimate=pl.CostEstimate(flops=1 << 20, bytes_accessed=1 << 10, transcendentals=0),
            name=name,
        )(self.place, *operands)
        self.before = [out[token]]
        return out


def fetch(pairs, sem):
    copies = [pltpu.make_async_copy(far, near, sem.at[i]) for i, (far, near) in enumerate(pairs)]
    for copy in copies:
        copy.start()
    return lambda i: copies[i].wait()


RING = 4


def gru_fwd(place, emb_far, lens_row, win_far, whid_far, bias, c_ref, co_far, hpt_far, *rest):
    emb, win, whid, co, hpt, h_ref, wsem, sems = rest
    slots, rows, _ = emb.shape
    gh = h_ref.shape[1]
    core = place[1]
    wait = fetch([(win_far.at[core], win), (whid_far.at[core], whid), (emb_far, emb)], wsem)
    h_ref[...] = jnp.zeros_like(h_ref)
    shift = bias[core].astype(f32)
    lens = lens_row[...].astype(f32).T
    for i in range(3):
        wait(i)

    def slot_of(s):
        return jnp.where(core == 0, s, slots - 1 - s)

    def out_copies(s):
        row = pl.multiple_of(s * rows, rows)
        at = pl.multiple_of(slot_of(s) * rows, rows)
        i = s % RING
        return (
            pltpu.make_async_copy(co.at[i], co_far.at[pl.ds(row, rows)], sems.at[0, i]),
            pltpu.make_async_copy(hpt.at[i], hpt_far.at[:, pl.ds(at, rows)], sems.at[1, i]),
        )

    def step(s, carry):
        @pl.when(s >= RING)
        def _():
            for copy in out_copies(s - RING):
                copy.wait()

        i = s % RING
        h = h_ref[...]
        hpt[i] = h.T.astype(bf16)
        mask = (slot_of(s).astype(f32) < lens).astype(f32)
        g = dot(emb[slot_of(s)], win[...]) + shift[0:1]
        y = dot(h.astype(bf16), whid[...]) + shift[1:2]
        r = sigmoid(g[:, :gh] + y[:, :gh])
        z = sigmoid(g[:, gh : 2 * gh] + y[:, gh : 2 * gh])
        yn = y[:, 2 * gh :]
        fresh = jnp.tanh(g[:, 2 * gh :] + r * yn)
        keep = mask * (1.0 - z)
        moved = keep * (h - fresh)
        h_ref[...] = h - moved
        an = keep * (1.0 - fresh * fresh)
        ay = an * r
        ar = ay * yn * (1.0 - r)
        for k, value in enumerate((ay, ar, moved * z, an, keep)):
            co[i, :, k * gh : (k + 1) * gh] = value.astype(bf16)
        for copy in out_copies(s):
            copy.start()
        return carry

    lax.fori_loop(0, slots, step, 0)
    c_ref[...] = h_ref[...].astype(bf16)
    for s in range(max(slots - RING, 0), slots):
        for copy in out_copies(s):
            copy.wait()


AHEAD = 4
SMALL = 9


def split_pack(pack, place, bit, gone_ref, kept_ref):
    half = pack.shape[0] // 2
    mine = (place[0] >> bit) & 1
    gone_ref[...] = pack[pl.ds(pl.multiple_of((1 - mine) * half, 16), half), :]
    kept_ref[...] = pack[pl.ds(pl.multiple_of(mine * half, 16), half), :]


def gru_back(bit, place, dc, whid_far, co_far, hpt_far, g_ref, bias_ref, gone_ref, kept_ref, *rest):
    dh_ref, whid, wht, acc, hpt, co, pack, sem, csem = rest
    rows, gh = dh_ref.shape
    slots = g_ref.shape[0] // rows
    core = place[1]
    wait = fetch([(whid_far.at[core], whid), (hpt_far, hpt)], sem)

    def co_copy(i):
        row = pl.multiple_of((slots - 1 - i) * rows, rows)
        return pltpu.make_async_copy(co_far.at[pl.ds(row, rows)], co.at[i % AHEAD], csem.at[i % AHEAD])

    for i in range(AHEAD - 1):
        co_copy(i).start()
    dh_ref[...] = dc[...]
    acc[...] = jnp.zeros_like(acc)
    wait(0)
    wht[...] = whid[...].T

    def step(i, carry):
        co_copy(i).wait()

        @pl.when(i + AHEAD - 1 < slots)
        def _():
            co_copy(i + AHEAD - 1).start()

        s = slots - 1 - i
        slot = jnp.where(core == 0, s, slots - 1 - s)
        row = pl.multiple_of(slot * rows, rows)
        dh = dh_ref[...]
        held = co.at[i % AHEAD]
        low = []
        for k in range(4):
            part = dh * held[:, k * gh : (k + 1) * gh].astype(f32)
            acc[:, k * gh : (k + 1) * gh] += part.reshape(-1, 8, gh).sum(0)
            low.append(part.astype(bf16))
            g_ref[pl.ds(row, rows), k * gh : (k + 1) * gh] = low[k]
        dy = jnp.concatenate([low[1], low[2], low[0]], 1)
        dh_ref[...] = dh - dh * held[:, 4 * gh :].astype(f32) + dot(dy, wht[...])
        return carry

    lax.fori_loop(0, slots, step, 0)
    wait(1)
    d_hid = dot(hpt[...], g_ref[:, : 3 * gh]).astype(bf16)
    pack[:, 2 * gh :] = d_hid[:, :gh]
    pack[:, : 2 * gh] = d_hid[:, gh:]
    split_pack(pack, place, bit, gone_ref, kept_ref)
    b = acc[...].sum(0, keepdims=True)
    bias_ref[...] = jnp.concatenate([b[:, gh:], b[:, gh : 3 * gh], b[:, :gh]], 1)


def gru_rest(bit, place, g, table, win_far, ids, b, sums_a, sums_b, q_shift, up_shift, *rest):
    gone_ref, kept_ref, win, pack, sem = rest
    embed, gates = win.shape
    vocab = table.shape[0]
    at = g.shape[1] - gates
    core = place[1]
    wait = fetch([(win_far.at[core], win)], sem)
    chosen = (lax.broadcasted_iota(jnp.int32, (vocab, ids.shape[1]), 0) == ids[...]).astype(bf16)
    by_char = dot(chosen, g[:, at:]).astype(bf16)
    pack[:embed] = dot_t(table[...], by_char).astype(bf16)
    wait(0)
    table = dot_r(by_char, win[...]).astype(bf16)
    long = vocab // 4
    for k in range(4):
        pack[embed:, k * embed : (k + 1) * embed] = table[k * long : (k + 1) * long]
    flat = [sums_a[0:1], sums_b[0:1], sums_b[1:2], sums_a[1:2], sums_b[2:3], sums_b[3:4], sums_a[2:3], sums_b[4:5], sums_b[5:6]]
    flat += [b[...], q_shift[0:1], q_shift[1:2], up_shift[...]]
    lanes = jnp.concatenate(flat, 1)
    count = lanes.shape[1] // 128
    tall = [lanes[:, k * 128 : (k + 1) * 128] for k in range(count)]
    tall += [jnp.zeros((1, 128), f32)] * (long - count)
    pack[embed:, 4 * embed :] = jnp.concatenate(tall, 0).astype(bf16)
    split_pack(pack, place, bit, gone_ref, kept_ref)


def rows_in_order(place, bit, own, got):
    low = ((place[0] >> bit) & 1) == 0
    own, got = own[...].astype(f32), got[...].astype(f32)
    return jnp.where(low, own, got), jnp.where(low, got, own)


def unpack_hid(bit, place, own, got, own_other, got_other, out):
    half = own.shape[0]
    for pair, d in (((own, got), place[1]), ((own_other, got_other), 1 - place[1])):
        first, second = rows_in_order(place, bit, *pair)
        out[d, :half] = first
        out[d, half:] = second


def unpack(bit, place, own, got, own_other, got_other, in_ref, table_ref, res_ref, gain_ref, off_ref, bias_ref, q_ref, up_ref):
    core = place[1]
    embed = in_ref.shape[1]
    gates = in_ref.shape[2]
    long = table_ref.shape[0] // 4
    half = own.shape[0]
    tails = []
    for pair, d in (((own, got), core), ((own_other, got_other), 1 - core)):
        first, second = rows_in_order(place, bit, *pair)
        in_ref[d, :half] = first
        in_ref[d, half:] = second[: embed - half]
        tails.append(second[embed - half :])
    mine, other = tails
    both = mine + other
    for k in range(4):
        table_ref[k * long : (k + 1) * long] = both[:, k * embed : (k + 1) * embed]
    line = lambda value, at, count: jnp.concatenate(
        [value[k : k + 1, 4 * embed :] for k in range(at // 128, (at + count) // 128)], 1
    )
    width = res_ref.shape[2]
    for k, ref in enumerate((res_ref, gain_ref, off_ref)):
        for i in range(3):
            ref[i] = line(both, (3 * k + i) * width, width)
    at = SMALL * width
    for value, d in ((mine, core), (other, 1 - core)):
        for i in range(2):
            bias_ref[d, pl.ds(i, 1)] = line(value, at + gates * i, gates)
    at += 2 * gates
    cols = q_ref.shape[1]
    for i in range(2):
        q_ref[i : i + 1] = line(mine, at + i * cols, cols)
    up_ref[...] = line(mine, at + 2 * cols, up_ref.shape[1])


GELU_A = 0.7978845608028654
GELU_B = 0.044715


def norm_stats(total):
    centre = jnp.mean(total, -1, keepdims=True)
    centred = total - centre
    scale = lax.rsqrt(jnp.mean(centred * centred, -1, keepdims=True) + EPSILON)
    return centred * scale, scale


def norm_back(grad, hat, scale, gain):
    scaled = grad * gain
    inner = jnp.mean(scaled, -1, keepdims=True)
    along = jnp.mean(scaled * hat, -1, keepdims=True)
    return (scaled - inner - hat * along) * scale


def gelu_pair(u):
    square = u * u
    t = jnp.tanh(GELU_A * (u + GELU_B * u * square))
    half = 0.5 * (1.0 + t)
    slope = half + 0.5 * u * (1.0 - t * t) * (GELU_A + 3.0 * GELU_A * GELU_B * square)
    return u * half, slope


def turned(values):
    rows = values.shape[0] // 2
    return jnp.concatenate([values[rows:], values[:rows]], 0)


def own_sum(values):
    return jnp.sum(values[: values.shape[0] // 2], 0, keepdims=True)


def pair_of(left, right):
    return jnp.concatenate([left, right], 0)


class Halves:
    def __init__(self, length, bit):
        self.count = lax.axis_size("dp")
        self.length, self.bit = length, bit
        self.chunk = length // self.count
        self.direct = self.chunk % 16 == 0

    def operands(self):
        if self.direct:
            return []
        mine = (lax.axis_index("dp") >> self.bit) & 1
        where = jnp.arange(self.length, dtype=jnp.int32)
        kept = where.reshape(self.count >> (self.bit + 1), 2, -1)
        pick = lambda side: jax.nn.one_hot(
            lax.dynamic_index_in_dim(kept, side, 1, keepdims=False).reshape(-1), self.length, dtype=bf16
        )
        return [pick(1 - mine), pick(mine)]

    def scratch(self, rows):
        return [pltpu.VMEM((self.length, rows), bf16)]

    def sides(self, values, turned_ref, place, picks):
        if not self.direct:
            return [dot_r(pick[...], values).astype(bf16) for pick in picks]
        turned_ref[...] = values.T
        mine = (place[0] >> self.bit) & 1
        out = []
        for side in (1 - mine, mine):
            parts = []
            for k in range(self.count):
                if not (k >> self.bit) & 1:
                    start = pl.multiple_of((k + (side << self.bit)) * self.chunk, 16)
                    parts.append(turned_ref[pl.ds(start, self.chunk), :])
            out.append(jnp.concatenate(parts, 0))
        return out


def attend_fwd(place, mine, other, wqkv_far, bqkv, wout_far, vec, *rest):
    q_ref, k_ref, v_ref, p_ref, m_ref, base_ref, send_ref, wqkv, wout, sem = rest
    wait = fetch([(wqkv_far, wqkv), (wout_far, wout)], sem)
    x = pair_of(mine[...], other[...])
    bias = bqkv[...].astype(f32)
    wait(0)
    q = (dot(x, wqkv[0]) + bias[0:1]).astype(bf16)
    k = dot(x, wqkv[1]).astype(bf16)
    v = (dot(x, wqkv[2]) + bias[1:2]).astype(bf16)
    q_ref[...], k_ref[...], v_ref[...] = q, k, v
    mixed = []
    for h in range(p_ref.shape[0]):
        at = slice(h * HD, (h + 1) * HD)
        s = dot_r(q[:, at], k[:, at]) * HD**-0.5
        e = jnp.exp(s - jnp.max(s, -1, keepdims=True))
        p = (e / jnp.sum(e, -1, keepdims=True)).astype(bf16)
        p_ref[h] = p
        mixed.append(dot(p, v[:, at]).astype(bf16))
    mixed = jnp.concatenate(mixed, 1)
    m_ref[...] = mixed
    wait(1)
    part = dot(mixed, wout[...])
    send_ref[...] = part.astype(bf16)
    base_ref[...] = x.astype(f32) + part + vec[0:1]


def feed_fwd(place, base, got, wup_far, bup, wdown_far, vec, *rest):
    hat_ref, scale_ref, act_ref, slope_ref, out_ref, send_ref, wup, wdown, sem = rest
    wait = fetch([(wup_far, wup), (wdown_far, wdown)], sem)
    hat, scale = norm_stats(base[...] + turned(got[...]).astype(f32))
    hat_ref[...], scale_ref[...] = hat, scale
    h1 = hat * vec[3:4] + vec[6:7]
    wait(0)
    act, slope = gelu_pair(dot(h1.astype(bf16), wup[...]) + bup[...].astype(f32))
    act = act.astype(bf16)
    act_ref[...] = act
    slope_ref[...] = slope.astype(bf16)
    wait(1)
    part = dot(act, wdown[...])
    send_ref[...] = part.astype(bf16)
    out_ref[...] = h1 + part + vec[1:2]


def unite(halves, place, base, got, cm, co, conv_far, tm, to, vec, *rest):
    picks, rest = rest[: 0 if halves.direct else 2], rest[0 if halves.direct else 2 :]
    res_ref, dc_ref, dr_ref, sums_ref, gone_ref, kept_ref, turned_ref, cat_ref, conv, sem = rest
    core = place[1]
    wait = fetch([(conv_far.at[i], conv.at[i]) for i in range(3)], sem)
    hat2, scale2 = norm_stats(base[...] + turned(got[...]).astype(f32))
    h2 = hat2 * vec[4:5] + vec[7:8]
    first = core == 0
    own, theirs = cm[...], turned(co[...])
    chars = [jnp.where(first, own, theirs), jnp.where(first, theirs, own)]
    joined = jnp.concatenate([h2.astype(bf16)] + chars, 1)
    rows = joined.shape[0]
    width = h2.shape[1]
    spot = lax.broadcasted_iota(jnp.int32, (rows, 1), 0)
    half = rows // 2
    not_first = (spot != core * half).astype(f32)
    not_last = (spot != (rows - 1 + core * half) % rows).astype(f32)
    later = lambda a: pltpu.roll(a, 1, 0) * not_first
    sooner = lambda a: pltpu.roll(a, rows - 1, 0) * not_last
    raw = vec[2:3]
    for i, move in enumerate((later, lambda a: a, sooner)):
        wait(i)
        raw = raw + move(dot(joined, conv[i]))
    act, slope = gelu_pair(raw)
    hat3, scale3 = norm_stats(h2 + act)
    res_ref[...] = (hat3 * vec[5:6] + vec[8:9])[:half].astype(bf16)
    cot = pair_of(tm[...], to[...]).astype(f32)
    d_r3 = norm_back(cot, hat3, scale3, vec[5:6])
    d_f = (d_r3 * slope).astype(bf16).astype(f32)
    d_fs = [sooner(d_f).astype(bf16), d_f.astype(bf16), later(d_f).astype(bf16)]
    gh = width // 2
    mine = pl.ds(pl.multiple_of(width + core * gh, 128), gh)
    d_h2 = d_r3 + sum(dot_r(d_fs[i], conv[i, :width]) for i in range(3))
    dc_ref[...] = sum(dot_r(d_fs[i], conv[i, mine]) for i in range(3))
    d_r2 = norm_back(d_h2, hat2, scale2, vec[4:5])
    dr_ref[...] = d_r2
    sums = [own_sum(d_r2), own_sum(d_f), own_sum(d_h2 * hat2), own_sum(cot * hat3), own_sum(d_h2), own_sum(cot)]
    for i, value in enumerate(sums):
        sums_ref[i : i + 1] = value
    span = width // 2
    gone, kept = halves.sides(joined, turned_ref, place, picks)
    for i in range(3):
        cat_ref[i] = d_fs[i]
        part = cat_ref[i, :, pl.ds(pl.multiple_of(core * span, 128), span)]
        gone_ref[:, i * span : (i + 1) * span] = dot(gone, part).astype(bf16)
        kept_ref[:, i * span : (i + 1) * span] = dot(kept, part).astype(bf16)


def feed_back(halves, place, dr, act, slope, hat, wup_far, wdown_far, vec, *rest):
    picks, rest = rest[: 0 if halves[0].direct else 4], rest[0 if halves[0].direct else 4 :]
    base_ref, send_ref, sum_ref = rest[:3]
    turned_ref, wup, wdown, sem = rest[-4:]
    wait = fetch([(wdown_far, wdown), (wup_far, wup)], sem)
    low = dr[...].astype(bf16)
    wait(0)
    d_u = (dot_r(low, wdown[...]) * slope[...].astype(f32)).astype(bf16)
    sum_ref[...] = jnp.sum(d_u.astype(f32), 0, keepdims=True)
    wait(1)
    part = dot_r(d_u, wup[...])
    send_ref[...] = part.astype(bf16)
    base_ref[...] = dr[...] + part
    h1 = (hat[...] * vec[3:4] + vec[6:7]).astype(bf16)
    units = d_u.shape[1]
    if TOGETHER:
        gone_up = gone_down = rest[3]
        kept_up = kept_down = rest[4]
    else:
        gone_up, kept_up, gone_down, kept_down = rest[3:7]
    for i, (left, right, gone_ref, kept_ref) in enumerate(
        ((h1, d_u, gone_up, kept_up), (low, act[...], gone_down, kept_down))
    ):
        at = slice(i * units, (i + 1) * units) if TOGETHER else slice(None)
        gone, kept = halves[i].sides(left, turned_ref, place, picks[2 * i : 2 * i + 2])
        gone_ref[:, at] = dot(gone, right).astype(bf16)
        kept_ref[:, at] = dot(kept, right).astype(bf16)


def attend_back(halves, place, base, got, hat, scale, q, k, v, p, mixed, mine, other, wqkv_far, wout_far, vec, *rest):
    picks, rest = rest[: 0 if halves.direct else 2], rest[0 if halves.direct else 2 :]
    base_ref, send_ref, sums_ref, shift_ref, gone_ref, kept_ref, turned_ref, wqkv, wout, sem = rest
    wait = fetch([(wout_far, wout), (wqkv_far, wqkv)], sem)
    d_h1 = base[...] + turned(got[...]).astype(f32)
    d_r1 = norm_back(d_h1, hat[...], scale[...], vec[3:4])
    for i, value in enumerate((own_sum(d_r1), own_sum(d_h1 * hat[...]), own_sum(d_h1))):
        sums_ref[i : i + 1] = value
    low = d_r1.astype(bf16)
    wait(0)
    d_mixed = dot_r(low, wout[...]).astype(bf16)
    d_q, d_k, d_v = [], [], []
    for h in range(p.shape[0]):
        at = slice(h * HD, (h + 1) * HD)
        prob = p[h].astype(f32)
        d_p = dot_r(d_mixed[:, at], v[:, at])
        d_v.append(dot_t(p[h], d_mixed[:, at]).astype(bf16))
        d_s = (prob * (d_p - jnp.sum(prob * d_p, -1, keepdims=True))).astype(bf16)
        d_q.append((dot(d_s, k[:, at]) * HD**-0.5).astype(bf16))
        d_k.append((dot_t(d_s, q[:, at]) * HD**-0.5).astype(bf16))
    d_proj = [jnp.concatenate(a, 1) for a in (d_q, d_k, d_v)]
    shift_ref[0:1] = jnp.sum(d_proj[0].astype(f32), 0, keepdims=True)
    shift_ref[1:2] = jnp.sum(d_proj[2].astype(f32), 0, keepdims=True)
    wait(1)
    part = sum(dot_r(d_proj[i], wqkv[i]) for i in range(3))
    rows = part.shape[0] // 2
    base_ref[...] = d_r1[:rows] + part[:rows]
    send_ref[...] = part[rows:].astype(bf16)
    span = d_mixed.shape[1]
    x = pair_of(mine[...], other[...])
    gone, kept = halves.sides(x, turned_ref, place, picks)
    for i in range(3):
        gone_ref[:, i * span : (i + 1) * span] = dot(gone, d_proj[i]).astype(bf16)
        kept_ref[:, i * span : (i + 1) * span] = dot(kept, d_proj[i]).astype(bf16)
    gone, kept = halves.sides(low, turned_ref, place, picks)
    gone_ref[:, 3 * span :] = dot(gone, mixed[...]).astype(bf16)
    kept_ref[:, 3 * span :] = dot(kept, mixed[...]).astype(bf16)


def swap(values):
    return lax.ppermute(values, "mp", [(0, 1), (1, 0)])


def flip(values, bit):
    count = lax.axis_size("dp")
    return lax.ppermute(values, "dp", [(i, i ^ (1 << bit)) for i in range(count)])


def added(left, right):
    return left.astype(f32) + right.astype(f32)


def high_groups():
    count = lax.axis_size("dp")
    return [[low + high for high in range(0, count, 4)] for low in range(4)]


class Sum:
    def __init__(self, gone, kept, order):
        self.order = order
        self.stage = 0
        self.kept = kept
        self.rows = kept.shape[0] * 2 // lax.axis_size("dp")
        self.got = flip(gone, order[0])

    def view(self):
        bits = range(lax.axis_size("dp").bit_length() - 1)
        left = [bit for bit in bits[::-1] if bit not in self.order[: self.stage + 1]]
        axis = left.index(self.order[self.stage + 1])
        return 1 << axis, self.rows << (len(left) - 1 - axis)

    def halving(self):
        return self.stage < len(self.order) - 1

    def add(self, seq, name):
        def kernel(place, kept, got, out):
            out[...] = added(kept[...], got[...]).astype(bf16)

        (out,) = seq.call(
            kernel, [Block(self.kept), Block(self.got)], [Block((self.kept.shape, bf16))], limit=16, name=name
        )
        return out


    def close(self, seq, name):
        self.total = self.add(seq, name)


class SumByColumn(Sum):
    def close(self, seq, name):
        total = self.add(seq, name)
        self.total = lax.psum_scatter(
            total, "dp", scatter_dimension=0, axis_index_groups=high_groups(), tiled=True
        )


class SumForAll(Sum):
    def __init__(self, gone, kept, order):
        super().__init__(gone, kept, order)
        self.left = list(range(2, lax.axis_size("dp").bit_length() - 1))

    def view(self):
        return 1, self.kept.shape[0] // 2

    def next(self, seq, name):
        if hasattr(self, "block"):
            return self.last(seq, name)
        if self.left is not None:
            self.kept = self.add(seq, f"{name}_sum_{len(self.left)}")
            if self.left:
                self.got = flip(self.kept, self.left.pop(0))
            else:
                self.left = None
                self.got = flip(self.kept, self.order[1])
            return False
        bit = self.order[1]

        def kernel(place, own, other, out):
            mine = (place[0] >> bit) & 1
            out[mine] = own[...]
            out[1 - mine] = other[...]

        shape = self.kept.shape
        (out,) = seq.call(
            kernel, [Block(self.kept), Block(self.got)], [Block(((2,) + shape, bf16))], limit=16, name=name + "_join"
        )
        self.block = out.reshape(2 * shape[0], shape[1])
        self.got = flip(self.block, self.order[0])
        self.other = swap(self.block)
        return False

    def last(self, seq, name):
        def kernel(place, got, out):
            out[...] = got[...]

        (got,) = seq.call(kernel, [Block(self.got)], [Block((self.got.shape, bf16))], limit=8, name=name + "_pass")
        self.quarters = [self.block, got, self.other, swap(got)]
        return True


def halve(seq, sums, name):
    ins, outs = [], []
    for item in sums:
        outer, rows = item.view()
        cols = item.kept.shape[-1]
        bit = item.order[item.stage + 1]
        for stays in (False, True):
            for value in (item.kept, item.got):
                ins.append(Side(value.reshape(outer, 2, rows, cols), bit, stays))
        outs += [Block(((outer * rows, cols), bf16))] * 2

    def kernel(place, *refs):
        for i in range(len(sums)):
            for j in range(2):
                left, right = refs[4 * i + 2 * j : 4 * i + 2 * j + 2]
                out = refs[4 * len(sums) + 2 * i + j]
                out[...] = added(left[:, 0], right[:, 0]).astype(bf16).reshape(out.shape)

    out = seq.call(kernel, ins, outs, limit=12, name=name, token=1)
    for i, item in enumerate(sums):
        item.stage += 1
        item.got = flip(out[2 * i], item.order[item.stage])
        item.kept = out[2 * i + 1]


def finish_rows(place, *refs):
    count = 2 if refs[0].shape == refs[1].shape and refs[0].dtype == refs[1].dtype else 1
    total = added(refs[0][...], refs[1][...]) if count == 2 else refs[0][...].astype(f32)
    at = 0
    for out in refs[count:]:
        parts = [out] if len(out.shape) == 2 else [out.at[i] for i in range(out.shape[0])]
        for part in parts:
            part[...] = total[:, at : at + part.shape[1]].astype(part.dtype)
            at += part.shape[1]


def finish_kernel(place, own, got, out):
    span = own.shape[1] // 3
    first = place[1] == 0
    for i in range(3):
        at = slice(i * span, (i + 1) * span)
        mine, other = own[:, at].astype(f32), got[:, at].astype(f32)
        out[i, :, :span] = jnp.where(first, mine, other)
        out[i, :, span:] = jnp.where(first, other, mine)


ORDERS = (
    (0, 1, 2, 3),
    (1, 0, 2, 3),
    (2, 1, 0, 3),
    (2, 0, 1, 3),
    (1, 0),
    (1, 0),
)
PLAN = (
    "feed", "gru", "attend_back", "up", "rest", "down", "conv", "hid",
    "tokens", "up", "in", "attend", "hid", "up", "in", "hid",
    "in", "hid", "attend", "conv", "in", "hid", "down", "attend",
    "in", "conv", "attend", "hid", "up", "in", "down", "conv",
    "hid_out", "conv_out", "down",
)
BY_COLUMN = ()
TOGETHER = False


def per_device(
    tokens,
    cotangent,
    char_ids,
    char_lens,
    w_qkv,
    b_qkv,
    w_out,
    w_up,
    up_bias,
    w_down,
    res_bias,
    norm_gain,
    norm_bias,
    char_table,
    gru_in,
    gru_hid,
    gru_bias,
    conv_w,
):
    core = lax.axis_index("mp")
    seq = Sequence(jnp.stack([lax.axis_index("dp"), core]).astype(jnp.int32))
    rows, width = tokens.shape
    both = 2 * rows
    slots = char_ids.shape[1]
    vocab, embed = char_table.shape
    gh = gru_hid.shape[2]
    count = lax.axis_size("dp")
    bits = list(range(count.bit_length() - 1))
    first = lambda *lead: list(lead) + [b for b in bits if b not in lead]
    wqkv = w_qkv[0].swapaxes(0, 1)
    cols = wqkv.shape[2]
    wout, wup, wdown, conv = w_out[0], w_up[0], w_down[0], conv_w[0]
    units = wup.shape[1]
    vec = jnp.concatenate([res_bias[0], norm_gain[0], norm_bias[0]], 0).astype(f32)
    heads = cols // HD
    dma = pltpu.SemaphoreType.DMA
    near = lambda a, dtype=bf16: pltpu.VMEM(a, dtype)

    letters = jnp.concatenate([char_ids.T, char_lens[None]], 0)
    letters_other = swap(letters)
    tokens_other = swap(tokens)
    cot_other = swap(cotangent)
    letters = jnp.concatenate([letters, letters_other], 1)
    tall = slots * both
    ids = letters[:slots].reshape(1, tall)
    one_hot = (ids.reshape(-1, 1) == jnp.arange(vocab, dtype=jnp.int32)[None, :]).astype(bf16)
    emb = seq.after(dot(one_hot, char_table).astype(bf16))

    seq.after(cot_other)

    q, k, v, p, mixed, base, send = seq.call(
        attend_fwd,
        [tokens, tokens_other, Far(wqkv), b_qkv[0], Far(wout), vec],
        [((both, cols), bf16)] * 3
        + [((heads, both, both), bf16), ((both, cols), bf16), ((both, width), f32), ((both, width), bf16)],
        [near(wqkv.shape), near(wout.shape), dma((2,))],
        name="attend_fwd",
        token=6,
        limit=14,
    )
    got = swap(send)
    chars, co, hpt = seq.call(
        gru_fwd,
        [Far(emb.reshape(slots, both, embed)), letters[slots:], Far(gru_in[0]), Far(gru_hid[0]), gru_bias[0]],
        [((both, gh), bf16), Far(((3 * tall, 5 * gh), bf16)), Far(((gh, tall), bf16))],
        [near((slots, both, embed)), near(gru_in.shape[2:]), near(gru_hid.shape[2:]), near((RING, both, 5 * gh))]
        + [near((RING, gh, both)), near((both, gh), f32), dma((3,)), dma((2, RING))],
        limit=16,
        name="gru_fwd",
    )
    chars_other = swap(chars)
    hat1, scale1, act, slope, base, send = seq.call(
        feed_fwd,
        [base, got, Far(wup), up_bias, Far(wdown), vec],
        [((both, width), f32), ((both, 1), f32), ((both, units), bf16), ((both, units), bf16)]
        + [((both, width), f32), ((both, width), bf16)],
        [near(wup.shape), near(wdown.shape), dma((2,))],
        name="feed_fwd",
        token=5,
        limit=14,
    )
    orders = [first(*order) for order in ORDERS]
    conv_order, up_order, down_order, attend_order, hid_order, in_order = orders
    halves = Halves(2 * width, conv_order[0])
    span = 3 * width // 2
    result, d_chars, d_r2, sums_b, gone, kept = seq.call(
        lambda *refs: unite(halves, *refs),
        [base, swap(send), chars, chars_other, Far(conv), cotangent, cot_other, vec, *halves.operands()],
        [Block(((rows, width), bf16)), ((both, gh), f32), ((both, width), f32), ((6, width), f32)]
        + [Block(((width, span), bf16))] * 2,
        halves.scratch(both) + [near((3, both, width)), near(conv.shape), dma((3,))],
        limit=26,
        name="unite",
        token=3,
    )
    def summed(name, gone, kept, order):
        sums[name] = SumByColumn(gone, kept, order[:2]) if name in BY_COLUMN else Sum(gone, kept, order)

    sums = {}
    summed("conv", gone, kept, conv_order)
    done = {}
    chunk = width // count

    def feed():
        halves = (Halves(width, up_order[0]), Halves(width, down_order[0]))
        sizes = [Block(((width // 2, units), bf16))] * 4
        if TOGETHER:
            sizes = [Block(((width // 2, 2 * units), bf16))] * 2
        out = seq.call(
            lambda *refs: feed_back(halves, *refs),
            [d_r2, act, slope, hat1, Far(wup), Far(wdown), vec, *halves[0].operands(), *halves[1].operands()],
            [((both, width), f32), ((both, width), bf16), ((1, units), f32)] + sizes,
            halves[0].scratch(both) + [near(wup.shape), near(wdown.shape), dma((2,))],
            limit=16,
        name="feed_back",
            token=2,
        )
        base, send, done["up_shift"] = out[:3]
        done["feed"] = base, swap(send)
        if TOGETHER:
            summed("ud", *out[3:], up_order)
        else:
            summed("up", *out[3:5], up_order)
            summed("down", *out[5:], down_order)

    def attend():
        halves = Halves(width, attend_order[0])
        base, send, done["sums"], done["q_shift"], gone, kept = seq.call(
            lambda *refs: attend_back(halves, *refs),
            [*done["feed"], hat1, scale1, q, k, v, p, mixed, tokens, tokens_other, Far(wqkv), Far(wout), vec]
            + halves.operands(),
            [((rows, width), f32), ((rows, width), bf16), ((3, width), f32), ((2, cols), f32)]
            + [Block(((width // 2, 4 * cols), bf16))] * 2,
            halves.scratch(both) + [near(wqkv.shape), near(wout.shape), dma((2,))],
            name="attend_back",
            token=2,
            limit=16,
        )
        done["attend"] = base, swap(send)
        summed("attend", gone, kept, attend_order)

    def tokens_end():
        base, got = done["attend"]
        done["tokens"] = seq.after(added(seq.tie(base), got))

    def chars_back():
        done["g"], done["bias"], gone, kept = seq.call(
            lambda *refs: gru_back(hid_order[0], *refs),
            [d_chars, Far(gru_hid[0]), Far(co), Far(hpt)],
            [((tall, 4 * gh), bf16), ((1, 6 * gh), f32)] + [Block(((gh // 2, 3 * gh), bf16))] * 2,
            [near((both, gh), f32), near(gru_hid.shape[2:]), near((3 * gh, gh))]
            + [near((8, 4 * gh), f32), near((gh, tall)), near((AHEAD, both, 5 * gh)), near((gh, 3 * gh))]
            + [dma((2,)), dma((AHEAD,))],
            limit=18,
        name="gru_back",
            token=1,
        )
        sums["hid"] = SumForAll(gone, kept, hid_order[:2])

    def chars_rest():
        pack = embed + vocab // 4
        gone, kept = seq.call(
            lambda *refs: gru_rest(in_order[0], *refs),
            [done["g"], char_table, Far(gru_in[0]), ids, done["bias"], done["sums"], sums_b]
            + [done["q_shift"], done["up_shift"]],
            [Block(((pack // 2, 3 * gh), bf16))] * 2,
            [near(gru_in.shape[2:]), near((pack, 3 * gh)), dma((1,))],
            limit=18,
        name="gru_rest",
        )
        sums["in"] = SumForAll(gone, kept, in_order[:2])

    def finish(name):
        item = sums[name]
        wide = done.setdefault("wide", {})
        if name != "attend":
            total = item.total.astype(f32) if isinstance(item, SumByColumn) else added(seq.tie(item.kept), item.got)
            total = seq.after(total)
            wide[name] = [total[:, i : i + units] for i in range(0, total.shape[1], units)]
            return
        left = [Block(item.total)] if isinstance(item, SumByColumn) else [Block(item.kept), Block(item.got)]
        shapes = [(3, chunk, cols), (chunk, cols)]
        wide[name] = seq.call(finish_rows, left, [Block((shape, f32)) for shape in shapes], name=name + "_end")

    def conv_out():
        own = sums["conv"].total
        (done["kernel"],) = seq.call(
            finish_kernel, [Block(own), Block(done["conv"])], [Block(((3, 2 * chunk, width), f32))], name="conv_out"
        )

    def hid_out():
        (done["hid"],) = seq.call(
            lambda *refs: unpack_hid(hid_order[0], *refs),
            [Block(a) for a in sums["hid"].quarters],
            [Block(((2, gh, 3 * gh), f32))],
            name="hid_out",
        )

    steps = {
        "feed": feed,
        "attend_back": attend,
        "tokens": tokens_end,
        "gru": chars_back,
        "rest": chars_rest,
        "conv_out": conv_out,
        "hid_out": hid_out,
    }
    ended = set()

    def ready(name):
        return {"conv_out": "conv", "hid_out": "hid"}.get(name, name) in ended if name.endswith("_out") else name not in ended

    def advance(name):
        if name in steps:
            ended.add(name)
            return steps[name]()
        item = sums[name]
        if item.halving():
            return halve(seq, [item], f"{name}_{item.stage}")
        if isinstance(item, SumForAll):
            if item.next(seq, name):
                ended.add(name)
        elif (name == "conv" or isinstance(item, SumByColumn)) and not hasattr(item, "total"):
            item.close(seq, name + "_sum")
            if name == "conv":
                done["conv"] = swap(item.total)
                ended.add(name)
        else:
            finish(name)
            ended.add(name)

    for name in PLAN:
        if ready(name):
            advance(name)
    while True:
        left = [n for n in sums if n not in ended]
        if not left:
            break
        for n in left:
            advance(n)
    for name in ("conv_out", "hid_out"):
        if name not in ended:
            advance(name)
    in_out, table_out, res_out, gain_out, offset_out, bias_out, q_out, up_out = seq.call(
        lambda *refs: unpack(in_order[0], *refs),
        [Block(a) for a in sums["in"].quarters],
        [Block(((2, embed, 3 * gh), f32)), Block(((vocab, embed), f32))]
        + [Block(((3, 1, width), f32))] * 3
        + [Block(((2, 2, 3 * gh), f32)), Block(((2, cols), f32)), Block(((1, units), f32))],
        limit=16,
        name="unpack",
    )
    hid_grad = done["hid"]
    qkv_grad, out_grad = done["wide"]["attend"]
    up_grad, down_grad = done["wide"]["ud"] if "ud" in sums else done["wide"]["up"] + done["wide"]["down"]
    return (
        result,
        done["tokens"],
        qkv_grad.swapaxes(0, 1)[None],
        q_out[None],
        out_grad.T[None],
        up_grad[None],
        up_out,
        down_grad.T[None],
        res_out.swapaxes(0, 1),
        gain_out.swapaxes(0, 1),
        offset_out.swapaxes(0, 1),
        table_out,
        in_out[None],
        hid_grad[None],
        bias_out[None],
        done["kernel"][None],
    )


def solution(mesh):
    return jax.shard_map(
        per_device,
        mesh=mesh,
        in_specs=(
            P(("dp", "mp"), None),
            P(("dp", "mp"), None),
            P(("dp", "mp"), None),
            P(("dp", "mp")),
            P(None, None, None, "mp"),
            P(None, None, "mp"),
            P(None, "mp", None),
            P(None, None, "mp"),
            P(None, "mp"),
            P(None, "mp", None),
            P(),
            P(),
            P(),
            P(),
            P(),
            P(),
            P(),
            P(),
        ),
        out_specs=(
            P(("dp", "mp"), None),
            P(("dp", "mp"), None),
            P(None, "dp", None, "mp"),
            P(None, None, "mp"),
            P(None, "mp", "dp"),
            P(None, "dp", "mp"),
            P(None, "mp"),
            P(None, "mp", "dp"),
            P(),
            P(),
            P(),
            P(),
            P(),
            P(),
            P(),
            P(None, None, "dp", None),
        ),
        check_vma=False,
    )
```

```python
import jax
import jax.numpy as jnp
from jax import lax
from jax.experimental import pallas as pl
from jax.experimental.pallas import tpu as pltpu
from jax.sharding import PartitionSpec as P

HD = 64
EPSILON = 1e-05
bf16 = jnp.bfloat16
f32 = jnp.float32


def dot(left, right):
    return jnp.dot(left, right, preferred_element_type=f32)


def dot_t(left, right):
    return lax.dot_general(left, right, (((0,), (0,)), ((), ())), preferred_element_type=f32)


def dot_r(left, right):
    return lax.dot_general(left, right, (((1,), (1,)), ((), ())), preferred_element_type=f32)


def sigmoid(x):
    return 0.5 * jnp.tanh(0.5 * x) + 0.5


class Far:
    def __init__(self, value):
        self.value = value


class Block:
    def __init__(self, value):
        self.value = value


class Side:
    def __init__(self, value, bit, stays):
        self.value, self.bit, self.stays = value, bit, stays


class Sequence:
    def __init__(self, place):
        self.place = place
        self.before = []

    def tie(self, value):
        return lax.optimization_barrier((value, *self.before))[0]

    def after(self, value):
        self.before.append(value)
        return value

    def call(self, kernel, ins, outs, scratch=(), limit=24, name="step", token=0):
        once = dict(pipeline_mode=pl.Buffered(1))
        whole = lambda n: lambda i, p: (0,) * n
        operands, specs = [], []
        for item in ins:
            if isinstance(item, Far):
                operands.append(item.value)
                specs.append(pl.BlockSpec(memory_space=pltpu.HBM))
            elif isinstance(item, Side):
                shape = item.value.shape

                def index(i, p, item=item):
                    mine = (p[0] >> item.bit) & 1
                    return (0, mine if item.stays else 1 - mine, 0, 0)

                operands.append(item.value)
                specs.append(pl.BlockSpec((shape[0], 1) + shape[2:], index, **once))
            elif isinstance(item, Block):
                operands.append(item.value)
                specs.append(pl.BlockSpec(item.value.shape, whole(item.value.ndim), **once))
            else:
                operands.append(item)
                specs.append(pl.BlockSpec(memory_space=pltpu.VMEM))
        out_specs, out_shape = [], []
        for item in outs:
            shape, dtype = item.value if isinstance(item, (Far, Block)) else item
            out_shape.append(jax.ShapeDtypeStruct(shape, dtype))
            if isinstance(item, Far):
                out_specs.append(pl.BlockSpec(memory_space=pltpu.HBM))
            elif isinstance(item, Block):
                out_specs.append(pl.BlockSpec(shape, whole(len(shape)), **once))
            else:
                out_specs.append(pl.BlockSpec(memory_space=pltpu.VMEM))
        count = len(ins)
        held = len(self.before)
        operands += self.before
        specs += [pl.BlockSpec(memory_space=pl.ANY)] * held

        def body(place, *refs):
            kernel(place, *refs[:count], *refs[count + held :])

        out = pl.pallas_call(
            body,
            grid_spec=pltpu.PrefetchScalarGridSpec(
                num_scalar_prefetch=1, grid=(1,), in_specs=specs, out_specs=out_specs, scratch_shapes=list(scratch)
            ),
            out_shape=out_shape,
            compiler_params=pltpu.CompilerParams(vmem_limit_bytes=limit << 20),
            cost_estimate=pl.CostEstimate(flops=1 << 20, bytes_accessed=1 << 10, transcendentals=0),
            name=name,
        )(self.place, *operands)
        self.before = [out[token]]
        return out


def fetch(pairs, sem):
    copies = [pltpu.make_async_copy(far, near, sem.at[i]) for i, (far, near) in enumerate(pairs)]
    for copy in copies:
        copy.start()
    return lambda i: copies[i].wait()


RING = 4


def gru_fwd(place, emb_far, lens_row, win_far, whid_far, bias, c_ref, co_far, hpt_far, *rest):
    emb, win, whid, co, hpt, h_ref, wsem, sems = rest
    slots, rows, _ = emb.shape
    gh = h_ref.shape[1]
    core = place[1]
    wait = fetch([(win_far.at[core], win), (whid_far.at[core], whid), (emb_far, emb)], wsem)
    h_ref[...] = jnp.zeros_like(h_ref)
    shift = bias[core].astype(f32)
    lens = lens_row[...].astype(f32).T
    for i in range(3):
        wait(i)

    def slot_of(s):
        return jnp.where(core == 0, s, slots - 1 - s)

    def out_copies(s):
        row = pl.multiple_of(s * rows, rows)
        at = pl.multiple_of(slot_of(s) * rows, rows)
        i = s % RING
        return (
            pltpu.make_async_copy(co.at[i], co_far.at[pl.ds(row, rows)], sems.at[0, i]),
            pltpu.make_async_copy(hpt.at[i], hpt_far.at[:, pl.ds(at, rows)], sems.at[1, i]),
        )

    def step(s, carry):
        @pl.when(s >= RING)
        def _():
            for copy in out_copies(s - RING):
                copy.wait()

        i = s % RING
        h = h_ref[...]
        hpt[i] = h.T.astype(bf16)
        mask = (slot_of(s).astype(f32) < lens).astype(f32)
        g = dot(emb[slot_of(s)], win[...]) + shift[0:1]
        y = dot(h.astype(bf16), whid[...]) + shift[1:2]
        r = sigmoid(g[:, :gh] + y[:, :gh])
        z = sigmoid(g[:, gh : 2 * gh] + y[:, gh : 2 * gh])
        yn = y[:, 2 * gh :]
        fresh = jnp.tanh(g[:, 2 * gh :] + r * yn)
        keep = mask * (1.0 - z)
        moved = keep * (h - fresh)
        h_ref[...] = h - moved
        an = keep * (1.0 - fresh * fresh)
        ay = an * r
        ar = ay * yn * (1.0 - r)
        for k, value in enumerate((ay, ar, moved * z, an, keep)):
            co[i, :, k * gh : (k + 1) * gh] = value.astype(bf16)
        for copy in out_copies(s):
            copy.start()
        return carry

    lax.fori_loop(0, slots, step, 0)
    c_ref[...] = h_ref[...].astype(bf16)
    for s in range(max(slots - RING, 0), slots):
        for copy in out_copies(s):
            copy.wait()


AHEAD = 4
SMALL = 9


def split_pack(pack, place, bit, gone_ref, kept_ref):
    half = pack.shape[0] // 2
    mine = (place[0] >> bit) & 1
    gone_ref[...] = pack[pl.ds(pl.multiple_of((1 - mine) * half, 16), half), :]
    kept_ref[...] = pack[pl.ds(pl.multiple_of(mine * half, 16), half), :]


def gru_back(bit, place, dc, whid_far, co_far, hpt_far, g_ref, bias_ref, gone_ref, kept_ref, *rest):
    dh_ref, whid, wht, acc, hpt, co, pack, sem, csem = rest
    rows, gh = dh_ref.shape
    slots = g_ref.shape[0] // rows
    core = place[1]
    wait = fetch([(whid_far.at[core], whid), (hpt_far, hpt)], sem)

    def co_copy(i):
        row = pl.multiple_of((slots - 1 - i) * rows, rows)
        return pltpu.make_async_copy(co_far.at[pl.ds(row, rows)], co.at[i % AHEAD], csem.at[i % AHEAD])

    for i in range(AHEAD - 1):
        co_copy(i).start()
    dh_ref[...] = dc[...]
    acc[...] = jnp.zeros_like(acc)
    wait(0)
    wht[...] = whid[...].T

    def step(i, carry):
        co_copy(i).wait()

        @pl.when(i + AHEAD - 1 < slots)
        def _():
            co_copy(i + AHEAD - 1).start()

        s = slots - 1 - i
        slot = jnp.where(core == 0, s, slots - 1 - s)
        row = pl.multiple_of(slot * rows, rows)
        dh = dh_ref[...]
        held = co.at[i % AHEAD]
        low = []
        for k in range(4):
            part = dh * held[:, k * gh : (k + 1) * gh].astype(f32)
            acc[:, k * gh : (k + 1) * gh] += part.reshape(-1, 8, gh).sum(0)
            low.append(part.astype(bf16))
            g_ref[pl.ds(row, rows), k * gh : (k + 1) * gh] = low[k]
        dy = jnp.concatenate([low[1], low[2], low[0]], 1)
        dh_ref[...] = dh - dh * held[:, 4 * gh :].astype(f32) + dot(dy, wht[...])
        return carry

    lax.fori_loop(0, slots, step, 0)
    wait(1)
    d_hid = dot(hpt[...], g_ref[:, : 3 * gh]).astype(bf16)
    pack[:, 2 * gh :] = d_hid[:, :gh]
    pack[:, : 2 * gh] = d_hid[:, gh:]
    split_pack(pack, place, bit, gone_ref, kept_ref)
    b = acc[...].sum(0, keepdims=True)
    bias_ref[...] = jnp.concatenate([b[:, gh:], b[:, gh : 3 * gh], b[:, :gh]], 1)


def gru_rest(bit, place, g, table, win_far, ids, b, sums_a, sums_b, q_shift, up_shift, *rest):
    gone_ref, kept_ref, win, pack, sem = rest
    embed, gates = win.shape
    vocab = table.shape[0]
    at = g.shape[1] - gates
    core = place[1]
    wait = fetch([(win_far.at[core], win)], sem)
    chosen = (lax.broadcasted_iota(jnp.int32, (vocab, ids.shape[1]), 0) == ids[...]).astype(bf16)
    by_char = dot(chosen, g[:, at:]).astype(bf16)
    pack[:embed] = dot_t(table[...], by_char).astype(bf16)
    wait(0)
    table = dot_r(by_char, win[...]).astype(bf16)
    long = vocab // 4
    for k in range(4):
        pack[embed:, k * embed : (k + 1) * embed] = table[k * long : (k + 1) * long]
    flat = [sums_a[0:1], sums_b[0:1], sums_b[1:2], sums_a[1:2], sums_b[2:3], sums_b[3:4], sums_a[2:3], sums_b[4:5], sums_b[5:6]]
    flat += [b[...], q_shift[0:1], q_shift[1:2], up_shift[...]]
    lanes = jnp.concatenate(flat, 1)
    count = lanes.shape[1] // 128
    tall = [lanes[:, k * 128 : (k + 1) * 128] for k in range(count)]
    tall += [jnp.zeros((1, 128), f32)] * (long - count)
    pack[embed:, 4 * embed :] = jnp.concatenate(tall, 0).astype(bf16)
    split_pack(pack, place, bit, gone_ref, kept_ref)


def rows_in_order(place, bit, own, got):
    low = ((place[0] >> bit) & 1) == 0
    own, got = own[...].astype(f32), got[...].astype(f32)
    return jnp.where(low, own, got), jnp.where(low, got, own)


def unpack_hid(bit, place, own, got, own_other, got_other, out):
    half = own.shape[0]
    for pair, d in (((own, got), place[1]), ((own_other, got_other), 1 - place[1])):
        first, second = rows_in_order(place, bit, *pair)
        out[d, :half] = first
        out[d, half:] = second


def unpack(bit, place, own, got, own_other, got_other, in_ref, table_ref, res_ref, gain_ref, off_ref, bias_ref, q_ref, up_ref):
    core = place[1]
    embed = in_ref.shape[1]
    gates = in_ref.shape[2]
    long = table_ref.shape[0] // 4
    half = own.shape[0]
    tails = []
    for pair, d in (((own, got), core), ((own_other, got_other), 1 - core)):
        first, second = rows_in_order(place, bit, *pair)
        in_ref[d, :half] = first
        in_ref[d, half:] = second[: embed - half]
        tails.append(second[embed - half :])
    mine, other = tails
    both = mine + other
    for k in range(4):
        table_ref[k * long : (k + 1) * long] = both[:, k * embed : (k + 1) * embed]
    line = lambda value, at, count: jnp.concatenate(
        [value[k : k + 1, 4 * embed :] for k in range(at // 128, (at + count) // 128)], 1
    )
    width = res_ref.shape[2]
    for k, ref in enumerate((res_ref, gain_ref, off_ref)):
        for i in range(3):
            ref[i] = line(both, (3 * k + i) * width, width)
    at = SMALL * width
    for value, d in ((mine, core), (other, 1 - core)):
        for i in range(2):
            bias_ref[d, pl.ds(i, 1)] = line(value, at + gates * i, gates)
    at += 2 * gates
    cols = q_ref.shape[1]
    for i in range(2):
        q_ref[i : i + 1] = line(mine, at + i * cols, cols)
    up_ref[...] = line(mine, at + 2 * cols, up_ref.shape[1])


GELU_A = 0.7978845608028654
GELU_B = 0.044715


def norm_stats(total):
    centre = jnp.mean(total, -1, keepdims=True)
    centred = total - centre
    scale = lax.rsqrt(jnp.mean(centred * centred, -1, keepdims=True) + EPSILON)
    return centred * scale, scale


def norm_back(grad, hat, scale, gain):
    scaled = grad * gain
    inner = jnp.mean(scaled, -1, keepdims=True)
    along = jnp.mean(scaled * hat, -1, keepdims=True)
    return (scaled - inner - hat * along) * scale


def gelu_pair(u):
    square = u * u
    t = jnp.tanh(GELU_A * (u + GELU_B * u * square))
    half = 0.5 * (1.0 + t)
    slope = half + 0.5 * u * (1.0 - t * t) * (GELU_A + 3.0 * GELU_A * GELU_B * square)
    return u * half, slope


def turned(values):
    rows = values.shape[0] // 2
    return jnp.concatenate([values[rows:], values[:rows]], 0)


def own_sum(values):
    return jnp.sum(values[: values.shape[0] // 2], 0, keepdims=True)


def pair_of(left, right):
    return jnp.concatenate([left, right], 0)


class Halves:
    def __init__(self, length, bit):
        self.count = lax.axis_size("dp")
        self.length, self.bit = length, bit
        self.chunk = length // self.count
        self.direct = self.chunk % 16 == 0

    def operands(self):
        if self.direct:
            return []
        mine = (lax.axis_index("dp") >> self.bit) & 1
        where = jnp.arange(self.length, dtype=jnp.int32)
        kept = where.reshape(self.count >> (self.bit + 1), 2, -1)
        pick = lambda side: jax.nn.one_hot(
            lax.dynamic_index_in_dim(kept, side, 1, keepdims=False).reshape(-1), self.length, dtype=bf16
        )
        return [pick(1 - mine), pick(mine)]

    def scratch(self, rows):
        return [pltpu.VMEM((self.length, rows), bf16)]

    def sides(self, values, turned_ref, place, picks):
        if not self.direct:
            return [dot_r(pick[...], values).astype(bf16) for pick in picks]
        turned_ref[...] = values.T
        mine = (place[0] >> self.bit) & 1
        out = []
        for side in (1 - mine, mine):
            parts = []
            for k in range(self.count):
                if not (k >> self.bit) & 1:
                    start = pl.multiple_of((k + (side << self.bit)) * self.chunk, 16)
                    parts.append(turned_ref[pl.ds(start, self.chunk), :])
            out.append(jnp.concatenate(parts, 0))
        return out


def attend_fwd(place, mine, other, wqkv_far, bqkv, wout_far, vec, *rest):
    q_ref, k_ref, v_ref, p_ref, m_ref, base_ref, send_ref, wqkv, wout, sem = rest
    wait = fetch([(wqkv_far, wqkv), (wout_far, wout)], sem)
    x = pair_of(mine[...], other[...])
    bias = bqkv[...].astype(f32)
    wait(0)
    q = (dot(x, wqkv[0]) + bias[0:1]).astype(bf16)
    k = dot(x, wqkv[1]).astype(bf16)
    v = (dot(x, wqkv[2]) + bias[1:2]).astype(bf16)
    q_ref[...], k_ref[...], v_ref[...] = q, k, v
    mixed = []
    for h in range(p_ref.shape[0]):
        at = slice(h * HD, (h + 1) * HD)
        s = dot_r(q[:, at], k[:, at]) * HD**-0.5
        e = jnp.exp(s - jnp.max(s, -1, keepdims=True))
        p = (e / jnp.sum(e, -1, keepdims=True)).astype(bf16)
        p_ref[h] = p
        mixed.append(dot(p, v[:, at]).astype(bf16))
    mixed = jnp.concatenate(mixed, 1)
    m_ref[...] = mixed
    wait(1)
    part = dot(mixed, wout[...])
    send_ref[...] = part.astype(bf16)
    base_ref[...] = x.astype(f32) + part + vec[0:1]


def feed_fwd(place, base, got, wup_far, bup, wdown_far, vec, *rest):
    hat_ref, scale_ref, act_ref, slope_ref, out_ref, send_ref, wup, wdown, sem = rest
    wait = fetch([(wup_far, wup), (wdown_far, wdown)], sem)
    hat, scale = norm_stats(base[...] + turned(got[...]).astype(f32))
    hat_ref[...], scale_ref[...] = hat, scale
    h1 = hat * vec[3:4] + vec[6:7]
    wait(0)
    act, slope = gelu_pair(dot(h1.astype(bf16), wup[...]) + bup[...].astype(f32))
    act = act.astype(bf16)
    act_ref[...] = act
    slope_ref[...] = slope.astype(bf16)
    wait(1)
    part = dot(act, wdown[...])
    send_ref[...] = part.astype(bf16)
    out_ref[...] = h1 + part + vec[1:2]


def unite(halves, place, base, got, cm, co, conv_far, tm, to, vec, *rest):
    picks, rest = rest[: 0 if halves.direct else 2], rest[0 if halves.direct else 2 :]
    res_ref, dc_ref, dr_ref, sums_ref, gone_ref, kept_ref, turned_ref, cat_ref, conv, sem = rest
    core = place[1]
    wait = fetch([(conv_far.at[i], conv.at[i]) for i in range(3)], sem)
    hat2, scale2 = norm_stats(base[...] + turned(got[...]).astype(f32))
    h2 = hat2 * vec[4:5] + vec[7:8]
    first = core == 0
    own, theirs = cm[...], turned(co[...])
    chars = [jnp.where(first, own, theirs), jnp.where(first, theirs, own)]
    joined = jnp.concatenate([h2.astype(bf16)] + chars, 1)
    rows = joined.shape[0]
    width = h2.shape[1]
    spot = lax.broadcasted_iota(jnp.int32, (rows, 1), 0)
    half = rows // 2
    not_first = (spot != core * half).astype(f32)
    not_last = (spot != (rows - 1 + core * half) % rows).astype(f32)
    later = lambda a: pltpu.roll(a, 1, 0) * not_first
    sooner = lambda a: pltpu.roll(a, rows - 1, 0) * not_last
    raw = vec[2:3]
    for i, move in enumerate((later, lambda a: a, sooner)):
        wait(i)
        raw = raw + move(dot(joined, conv[i]))
    act, slope = gelu_pair(raw)
    hat3, scale3 = norm_stats(h2 + act)
    res_ref[...] = (hat3 * vec[5:6] + vec[8:9])[:half].astype(bf16)
    cot = pair_of(tm[...], to[...]).astype(f32)
    d_r3 = norm_back(cot, hat3, scale3, vec[5:6])
    d_f = (d_r3 * slope).astype(bf16).astype(f32)
    d_fs = [sooner(d_f).astype(bf16), d_f.astype(bf16), later(d_f).astype(bf16)]
    gh = width // 2
    mine = pl.ds(pl.multiple_of(width + core * gh, 128), gh)
    d_h2 = d_r3 + sum(dot_r(d_fs[i], conv[i, :width]) for i in range(3))
    dc_ref[...] = sum(dot_r(d_fs[i], conv[i, mine]) for i in range(3))
    d_r2 = norm_back(d_h2, hat2, scale2, vec[4:5])
    dr_ref[...] = d_r2
    sums = [own_sum(d_r2), own_sum(d_f), own_sum(d_h2 * hat2), own_sum(cot * hat3), own_sum(d_h2), own_sum(cot)]
    for i, value in enumerate(sums):
        sums_ref[i : i + 1] = value
    span = width // 2
    gone, kept = halves.sides(joined, turned_ref, place, picks)
    for i in range(3):
        cat_ref[i] = d_fs[i]
        part = cat_ref[i, :, pl.ds(pl.multiple_of(core * span, 128), span)]
        gone_ref[:, i * span : (i + 1) * span] = dot(gone, part).astype(bf16)
        kept_ref[:, i * span : (i + 1) * span] = dot(kept, part).astype(bf16)


def feed_back(halves, place, dr, act, slope, hat, wup_far, wdown_far, vec, *rest):
    picks, rest = rest[: 0 if halves[0].direct else 4], rest[0 if halves[0].direct else 4 :]
    base_ref, send_ref, sum_ref = rest[:3]
    turned_ref, wup, wdown, sem = rest[-4:]
    wait = fetch([(wdown_far, wdown), (wup_far, wup)], sem)
    low = dr[...].astype(bf16)
    wait(0)
    d_u = (dot_r(low, wdown[...]) * slope[...].astype(f32)).astype(bf16)
    sum_ref[...] = jnp.sum(d_u.astype(f32), 0, keepdims=True)
    wait(1)
    part = dot_r(d_u, wup[...])
    send_ref[...] = part.astype(bf16)
    base_ref[...] = dr[...] + part
    h1 = (hat[...] * vec[3:4] + vec[6:7]).astype(bf16)
    units = d_u.shape[1]
    if TOGETHER:
        gone_up = gone_down = rest[3]
        kept_up = kept_down = rest[4]
    else:
        gone_up, kept_up, gone_down, kept_down = rest[3:7]
    for i, (left, right, gone_ref, kept_ref) in enumerate(
        ((h1, d_u, gone_up, kept_up), (low, act[...], gone_down, kept_down))
    ):
        at = slice(i * units, (i + 1) * units) if TOGETHER else slice(None)
        gone, kept = halves[i].sides(left, turned_ref, place, picks[2 * i : 2 * i + 2])
        gone_ref[:, at] = dot(gone, right).astype(bf16)
        kept_ref[:, at] = dot(kept, right).astype(bf16)


def attend_back(halves, place, base, got, hat, scale, q, k, v, p, mixed, mine, other, wqkv_far, wout_far, vec, *rest):
    picks, rest = rest[: 0 if halves.direct else 2], rest[0 if halves.direct else 2 :]
    base_ref, send_ref, sums_ref, shift_ref, gone_ref, kept_ref, turned_ref, wqkv, wout, sem = rest
    wait = fetch([(wout_far, wout), (wqkv_far, wqkv)], sem)
    d_h1 = base[...] + turned(got[...]).astype(f32)
    d_r1 = norm_back(d_h1, hat[...], scale[...], vec[3:4])
    for i, value in enumerate((own_sum(d_r1), own_sum(d_h1 * hat[...]), own_sum(d_h1))):
        sums_ref[i : i + 1] = value
    low = d_r1.astype(bf16)
    wait(0)
    d_mixed = dot_r(low, wout[...]).astype(bf16)
    d_q, d_k, d_v = [], [], []
    for h in range(p.shape[0]):
        at = slice(h * HD, (h + 1) * HD)
        prob = p[h].astype(f32)
        d_p = dot_r(d_mixed[:, at], v[:, at])
        d_v.append(dot_t(p[h], d_mixed[:, at]).astype(bf16))
        d_s = (prob * (d_p - jnp.sum(prob * d_p, -1, keepdims=True))).astype(bf16)
        d_q.append((dot(d_s, k[:, at]) * HD**-0.5).astype(bf16))
        d_k.append((dot_t(d_s, q[:, at]) * HD**-0.5).astype(bf16))
    d_proj = [jnp.concatenate(a, 1) for a in (d_q, d_k, d_v)]
    shift_ref[0:1] = jnp.sum(d_proj[0].astype(f32), 0, keepdims=True)
    shift_ref[1:2] = jnp.sum(d_proj[2].astype(f32), 0, keepdims=True)
    wait(1)
    part = sum(dot_r(d_proj[i], wqkv[i]) for i in range(3))
    rows = part.shape[0] // 2
    base_ref[...] = d_r1[:rows] + part[:rows]
    send_ref[...] = part[rows:].astype(bf16)
    span = d_mixed.shape[1]
    x = pair_of(mine[...], other[...])
    gone, kept = halves.sides(x, turned_ref, place, picks)
    for i in range(3):
        gone_ref[:, i * span : (i + 1) * span] = dot(gone, d_proj[i]).astype(bf16)
        kept_ref[:, i * span : (i + 1) * span] = dot(kept, d_proj[i]).astype(bf16)
    gone, kept = halves.sides(low, turned_ref, place, picks)
    gone_ref[:, 3 * span :] = dot(gone, mixed[...]).astype(bf16)
    kept_ref[:, 3 * span :] = dot(kept, mixed[...]).astype(bf16)


def swap(values):
    return lax.ppermute(values, "mp", [(0, 1), (1, 0)])


def flip(values, bit):
    count = lax.axis_size("dp")
    return lax.ppermute(values, "dp", [(i, i ^ (1 << bit)) for i in range(count)])


def added(left, right):
    return left.astype(f32) + right.astype(f32)


def high_groups():
    count = lax.axis_size("dp")
    return [[low + high for high in range(0, count, 4)] for low in range(4)]


class Sum:
    def __init__(self, gone, kept, order):
        self.order = order
        self.stage = 0
        self.kept = kept
        self.rows = kept.shape[0] * 2 // lax.axis_size("dp")
        self.got = flip(gone, order[0])

    def view(self):
        bits = range(lax.axis_size("dp").bit_length() - 1)
        left = [bit for bit in bits[::-1] if bit not in self.order[: self.stage + 1]]
        axis = left.index(self.order[self.stage + 1])
        return 1 << axis, self.rows << (len(left) - 1 - axis)

    def halving(self):
        return self.stage < len(self.order) - 1

    def add(self, seq, name):
        def kernel(place, kept, got, out):
            out[...] = added(kept[...], got[...]).astype(bf16)

        (out,) = seq.call(
            kernel, [Block(self.kept), Block(self.got)], [Block((self.kept.shape, bf16))], limit=16, name=name
        )
        return out


    def close(self, seq, name):
        self.total = self.add(seq, name)


class SumByColumn(Sum):
    def close(self, seq, name):
        total = self.add(seq, name)
        self.total = lax.psum_scatter(
            total, "dp", scatter_dimension=0, axis_index_groups=high_groups(), tiled=True
        )


class SumForAll(Sum):
    def __init__(self, gone, kept, order):
        super().__init__(gone, kept, order)
        self.left = list(range(2, lax.axis_size("dp").bit_length() - 1))

    def view(self):
        return 1, self.kept.shape[0] // 2

    def next(self, seq, name):
        if hasattr(self, "block"):
            return self.last(seq, name)
        if self.left is not None:
            self.kept = self.add(seq, f"{name}_sum_{len(self.left)}")
            if self.left:
                self.got = flip(self.kept, self.left.pop(0))
            else:
                self.left = None
                self.got = flip(self.kept, self.order[1])
            return False
        bit = self.order[1]

        def kernel(place, own, other, out):
            mine = (place[0] >> bit) & 1
            out[mine] = own[...]
            out[1 - mine] = other[...]

        shape = self.kept.shape
        (out,) = seq.call(
            kernel, [Block(self.kept), Block(self.got)], [Block(((2,) + shape, bf16))], limit=16, name=name + "_join"
        )
        self.block = out.reshape(2 * shape[0], shape[1])
        self.got = flip(self.block, self.order[0])
        self.other = swap(self.block)
        return False

    def last(self, seq, name):
        def kernel(place, got, out):
            out[...] = got[...]

        (got,) = seq.call(kernel, [Block(self.got)], [Block((self.got.shape, bf16))], limit=8, name=name + "_pass")
        self.quarters = [self.block, got, self.other, swap(got)]
        return True


def halve(seq, sums, name):
    ins, outs = [], []
    for item in sums:
        outer, rows = item.view()
        cols = item.kept.shape[-1]
        bit = item.order[item.stage + 1]
        for stays in (False, True):
            for value in (item.kept, item.got):
                ins.append(Side(value.reshape(outer, 2, rows, cols), bit, stays))
        outs += [Block(((outer * rows, cols), bf16))] * 2

    def kernel(place, *refs):
        for i in range(len(sums)):
            for j in range(2):
                left, right = refs[4 * i + 2 * j : 4 * i + 2 * j + 2]
                out = refs[4 * len(sums) + 2 * i + j]
                out[...] = added(left[:, 0], right[:, 0]).astype(bf16).reshape(out.shape)

    out = seq.call(kernel, ins, outs, limit=12, name=name, token=1)
    for i, item in enumerate(sums):
        item.stage += 1
        item.got = flip(out[2 * i], item.order[item.stage])
        item.kept = out[2 * i + 1]


def finish_rows(place, *refs):
    count = 2 if refs[0].shape == refs[1].shape and refs[0].dtype == refs[1].dtype else 1
    total = added(refs[0][...], refs[1][...]) if count == 2 else refs[0][...].astype(f32)
    at = 0
    for out in refs[count:]:
        parts = [out] if len(out.shape) == 2 else [out.at[i] for i in range(out.shape[0])]
        for part in parts:
            part[...] = total[:, at : at + part.shape[1]].astype(part.dtype)
            at += part.shape[1]


def finish_kernel(place, own, got, out):
    span = own.shape[1] // 3
    first = place[1] == 0
    for i in range(3):
        at = slice(i * span, (i + 1) * span)
        mine, other = own[:, at].astype(f32), got[:, at].astype(f32)
        out[i, :, :span] = jnp.where(first, mine, other)
        out[i, :, span:] = jnp.where(first, other, mine)


ORDERS = (
    (0, 1, 2, 3),
    (1, 0, 2, 3),
    (2, 1, 0, 3),
    (2, 0, 1, 3),
    (1, 0),
    (1, 0),
)
PLAN = (
    "feed", "gru", "attend_back", "up", "rest", "down", "conv", "hid",
    "tokens", "up", "in", "attend", "hid", "up", "in", "hid",
    "in", "hid", "attend", "conv", "in", "hid", "down", "attend",
    "in", "conv", "attend", "hid", "up", "in", "down", "conv",
    "hid_out", "conv_out", "down",
)
BY_COLUMN = ()
TOGETHER = False


def per_device(
    tokens,
    cotangent,
    char_ids,
    char_lens,
    w_qkv,
    b_qkv,
    w_out,
    w_up,
    up_bias,
    w_down,
    res_bias,
    norm_gain,
    norm_bias,
    char_table,
    gru_in,
    gru_hid,
    gru_bias,
    conv_w,
):
    core = lax.axis_index("mp")
    seq = Sequence(jnp.stack([lax.axis_index("dp"), core]).astype(jnp.int32))
    rows, width = tokens.shape
    both = 2 * rows
    slots = char_ids.shape[1]
    vocab, embed = char_table.shape
    gh = gru_hid.shape[2]
    count = lax.axis_size("dp")
    bits = list(range(count.bit_length() - 1))
    first = lambda *lead: list(lead) + [b for b in bits if b not in lead]
    wqkv = w_qkv[0].swapaxes(0, 1)
    cols = wqkv.shape[2]
    wout, wup, wdown, conv = w_out[0], w_up[0], w_down[0], conv_w[0]
    units = wup.shape[1]
    vec = jnp.concatenate([res_bias[0], norm_gain[0], norm_bias[0]], 0).astype(f32)
    heads = cols // HD
    dma = pltpu.SemaphoreType.DMA
    near = lambda a, dtype=bf16: pltpu.VMEM(a, dtype)

    letters, lens = char_ids.T, char_lens[None]
    letters_other, lens_other = swap(letters), swap(lens)
    tokens_other = swap(tokens)
    cot_other = swap(cotangent)
    letters = jnp.concatenate([letters, letters_other], 1)
    lens = jnp.concatenate([lens, lens_other], 1)
    tall = slots * both
    ids = letters.reshape(1, tall)
    one_hot = (ids.reshape(-1, 1) == jnp.arange(vocab, dtype=jnp.int32)[None, :]).astype(bf16)
    emb = seq.after(dot(one_hot, char_table).astype(bf16))

    seq.after(cot_other)

    q, k, v, p, mixed, base, send = seq.call(
        attend_fwd,
        [tokens, tokens_other, Far(wqkv), b_qkv[0], Far(wout), vec],
        [((both, cols), bf16)] * 3
        + [((heads, both, both), bf16), ((both, cols), bf16), ((both, width), f32), ((both, width), bf16)],
        [near(wqkv.shape), near(wout.shape), dma((2,))],
        name="attend_fwd",
        token=6,
        limit=14,
    )
    got = swap(send)
    chars, co, hpt = seq.call(
        gru_fwd,
        [Far(emb.reshape(slots, both, embed)), lens, Far(gru_in[0]), Far(gru_hid[0]), gru_bias[0]],
        [((both, gh), bf16), Far(((3 * tall, 5 * gh), bf16)), Far(((gh, tall), bf16))],
        [near((slots, both, embed)), near(gru_in.shape[2:]), near(gru_hid.shape[2:]), near((RING, both, 5 * gh))]
        + [near((RING, gh, both)), near((both, gh), f32), dma((3,)), dma((2, RING))],
        limit=16,
        name="gru_fwd",
    )
    chars_other = swap(chars)
    hat1, scale1, act, slope, base, send = seq.call(
        feed_fwd,
        [base, got, Far(wup), up_bias, Far(wdown), vec],
        [((both, width), f32), ((both, 1), f32), ((both, units), bf16), ((both, units), bf16)]
        + [((both, width), f32), ((both, width), bf16)],
        [near(wup.shape), near(wdown.shape), dma((2,))],
        name="feed_fwd",
        token=5,
        limit=14,
    )
    orders = [first(*order) for order in ORDERS]
    conv_order, up_order, down_order, attend_order, hid_order, in_order = orders
    halves = Halves(2 * width, conv_order[0])
    span = 3 * width // 2
    result, d_chars, d_r2, sums_b, gone, kept = seq.call(
        lambda *refs: unite(halves, *refs),
        [base, swap(send), chars, chars_other, Far(conv), cotangent, cot_other, vec, *halves.operands()],
        [Block(((rows, width), bf16)), ((both, gh), f32), ((both, width), f32), ((6, width), f32)]
        + [Block(((width, span), bf16))] * 2,
        halves.scratch(both) + [near((3, both, width)), near(conv.shape), dma((3,))],
        limit=26,
        name="unite",
        token=3,
    )
    def summed(name, gone, kept, order):
        sums[name] = SumByColumn(gone, kept, order[:2]) if name in BY_COLUMN else Sum(gone, kept, order)

    sums = {}
    summed("conv", gone, kept, conv_order)
    done = {}
    chunk = width // count

    def feed():
        halves = (Halves(width, up_order[0]), Halves(width, down_order[0]))
        sizes = [Block(((width // 2, units), bf16))] * 4
        if TOGETHER:
            sizes = [Block(((width // 2, 2 * units), bf16))] * 2
        out = seq.call(
            lambda *refs: feed_back(halves, *refs),
            [d_r2, act, slope, hat1, Far(wup), Far(wdown), vec, *halves[0].operands(), *halves[1].operands()],
            [((both, width), f32), ((both, width), bf16), ((1, units), f32)] + sizes,
            halves[0].scratch(both) + [near(wup.shape), near(wdown.shape), dma((2,))],
            limit=16,
        name="feed_back",
            token=2,
        )
        base, send, done["up_shift"] = out[:3]
        done["feed"] = base, swap(send)
        if TOGETHER:
            summed("ud", *out[3:], up_order)
        else:
            summed("up", *out[3:5], up_order)
            summed("down", *out[5:], down_order)

    def attend():
        halves = Halves(width, attend_order[0])
        base, send, done["sums"], done["q_shift"], gone, kept = seq.call(
            lambda *refs: attend_back(halves, *refs),
            [*done["feed"], hat1, scale1, q, k, v, p, mixed, tokens, tokens_other, Far(wqkv), Far(wout), vec]
            + halves.operands(),
            [((rows, width), f32), ((rows, width), bf16), ((3, width), f32), ((2, cols), f32)]
            + [Block(((width // 2, 4 * cols), bf16))] * 2,
            halves.scratch(both) + [near(wqkv.shape), near(wout.shape), dma((2,))],
            name="attend_back",
            token=2,
            limit=16,
        )
        done["attend"] = base, swap(send)
        summed("attend", gone, kept, attend_order)

    def tokens_end():
        base, got = done["attend"]
        done["tokens"] = seq.after(added(seq.tie(base), got))

    def chars_back():
        done["g"], done["bias"], gone, kept = seq.call(
            lambda *refs: gru_back(hid_order[0], *refs),
            [d_chars, Far(gru_hid[0]), Far(co), Far(hpt)],
            [((tall, 4 * gh), bf16), ((1, 6 * gh), f32)] + [Block(((gh // 2, 3 * gh), bf16))] * 2,
            [near((both, gh), f32), near(gru_hid.shape[2:]), near((3 * gh, gh))]
            + [near((8, 4 * gh), f32), near((gh, tall)), near((AHEAD, both, 5 * gh)), near((gh, 3 * gh))]
            + [dma((2,)), dma((AHEAD,))],
            limit=18,
        name="gru_back",
            token=1,
        )
        sums["hid"] = SumForAll(gone, kept, hid_order[:2])

    def chars_rest():
        pack = embed + vocab // 4
        gone, kept = seq.call(
            lambda *refs: gru_rest(in_order[0], *refs),
            [done["g"], char_table, Far(gru_in[0]), ids, done["bias"], done["sums"], sums_b]
            + [done["q_shift"], done["up_shift"]],
            [Block(((pack // 2, 3 * gh), bf16))] * 2,
            [near(gru_in.shape[2:]), near((pack, 3 * gh)), dma((1,))],
            limit=18,
        name="gru_rest",
        )
        sums["in"] = SumForAll(gone, kept, in_order[:2])

    def finish(name):
        item = sums[name]
        wide = done.setdefault("wide", {})
        if name != "attend":
            total = item.total.astype(f32) if isinstance(item, SumByColumn) else added(seq.tie(item.kept), item.got)
            total = seq.after(total)
            wide[name] = [total[:, i : i + units] for i in range(0, total.shape[1], units)]
            return
        left = [Block(item.total)] if isinstance(item, SumByColumn) else [Block(item.kept), Block(item.got)]
        shapes = [(3, chunk, cols), (chunk, cols)]
        wide[name] = seq.call(finish_rows, left, [Block((shape, f32)) for shape in shapes], name=name + "_end")

    def conv_out():
        own = sums["conv"].total
        (done["kernel"],) = seq.call(
            finish_kernel, [Block(own), Block(done["conv"])], [Block(((3, 2 * chunk, width), f32))], name="conv_out"
        )

    def hid_out():
        (done["hid"],) = seq.call(
            lambda *refs: unpack_hid(hid_order[0], *refs),
            [Block(a) for a in sums["hid"].quarters],
            [Block(((2, gh, 3 * gh), f32))],
            name="hid_out",
        )

    steps = {
        "feed": feed,
        "attend_back": attend,
        "tokens": tokens_end,
        "gru": chars_back,
        "rest": chars_rest,
        "conv_out": conv_out,
        "hid_out": hid_out,
    }
    ended = set()

    def ready(name):
        return {"conv_out": "conv", "hid_out": "hid"}.get(name, name) in ended if name.endswith("_out") else name not in ended

    def advance(name):
        if name in steps:
            ended.add(name)
            return steps[name]()
        item = sums[name]
        if item.halving():
            return halve(seq, [item], f"{name}_{item.stage}")
        if isinstance(item, SumForAll):
            if item.next(seq, name):
                ended.add(name)
        elif (name == "conv" or isinstance(item, SumByColumn)) and not hasattr(item, "total"):
            item.close(seq, name + "_sum")
            if name == "conv":
                done["conv"] = swap(item.total)
                ended.add(name)
        else:
            finish(name)
            ended.add(name)

    for name in PLAN:
        if ready(name):
            advance(name)
    while True:
        left = [n for n in sums if n not in ended]
        if not left:
            break
        for n in left:
            advance(n)
    for name in ("conv_out", "hid_out"):
        if name not in ended:
            advance(name)
    in_out, table_out, res_out, gain_out, offset_out, bias_out, q_out, up_out = seq.call(
        lambda *refs: unpack(in_order[0], *refs),
        [Block(a) for a in sums["in"].quarters],
        [Block(((2, embed, 3 * gh), f32)), Block(((vocab, embed), f32))]
        + [Block(((3, 1, width), f32))] * 3
        + [Block(((2, 2, 3 * gh), f32)), Block(((2, cols), f32)), Block(((1, units), f32))],
        limit=16,
        name="unpack",
    )
    hid_grad = done["hid"]
    qkv_grad, out_grad = done["wide"]["attend"]
    up_grad, down_grad = done["wide"]["ud"] if "ud" in sums else done["wide"]["up"] + done["wide"]["down"]
    return (
        result,
        done["tokens"],
        qkv_grad.swapaxes(0, 1)[None],
        q_out[None],
        out_grad.T[None],
        up_grad[None],
        up_out,
        down_grad.T[None],
        res_out.swapaxes(0, 1),
        gain_out.swapaxes(0, 1),
        offset_out.swapaxes(0, 1),
        table_out,
        in_out[None],
        hid_grad[None],
        bias_out[None],
        done["kernel"][None],
    )


def solution(mesh):
    return jax.shard_map(
        per_device,
        mesh=mesh,
        in_specs=(
            P(("dp", "mp"), None),
            P(("dp", "mp"), None),
            P(("dp", "mp"), None),
            P(("dp", "mp")),
            P(None, None, None, "mp"),
            P(None, None, "mp"),
            P(None, "mp", None),
            P(None, None, "mp"),
            P(None, "mp"),
            P(None, "mp", None),
            P(),
            P(),
            P(),
            P(),
            P(),
            P(),
            P(),
            P(),
        ),
        out_specs=(
            P(("dp", "mp"), None),
            P(("dp", "mp"), None),
            P(None, "dp", None, "mp"),
            P(None, None, "mp"),
            P(None, "mp", "dp"),
            P(None, "dp", "mp"),
            P(None, "mp"),
            P(None, "mp", "dp"),
            P(),
            P(),
            P(),
            P(),
            P(),
            P(),
            P(),
            P(None, None, "dp", None),
        ),
        check_vma=False,
    )
```
